32 devices in a mesh: dp: 8 (over z, x), tensor: 4 (over y, core).
Axes of the slice: x: 2, y: 2, z: 4, core: 2. Of those that a mesh axis runs over, the one named last changes fastest.
Arguments:
- tokens: bfloat16 [16384, 768], P(('dp', 'tensor')), may hold values from -6 to 6
- cotangent: bfloat16 [16384, 768], P(('dp', 'tensor')), may hold values from -6 to 6
- w_qkv: float32 [3, 768, 768], P(None, 'dp', 'tensor'), may hold values from -0.3125 to 0.3125
- w_attn_out: float32 [768, 768], P('tensor', 'dp'), may hold values from -0.625 to 0.625
- w_in: float32 [2, 768, 1152], P(None, 'dp', 'tensor'), may hold values from -0.21875 to 0.21875
- w_mlp_out: float32 [1152, 768], P('tensor', 'dp'), may hold values from -0.1875 to 0.1875
- gains: float32 [2, 768], P(None, 'dp'), may hold values from 0.5 to 1.5
- first_qkv: float32 [3, 768, 768], P(None, 'dp', 'tensor'), may hold values from -80 to 80
- first_attn_out: float32 [768, 768], P('tensor', 'dp'), may hold values from -24 to 24
- first_in: float32 [2, 768, 1152], P(None, 'dp', 'tensor'), may hold values from -48 to 48
- first_mlp_out: float32 [1152, 768], P('tensor', 'dp'), may hold values from -56 to 56
- first_gains: float32 [2, 768], P(None, 'dp'), may hold values from -128 to 128
- second_qkv: float32 [3, 768, 768], P(None, 'dp', 'tensor'), may hold values from 334.2336 to 1336.9344
- second_attn_out: float32 [768, 768], P('tensor', 'dp'), may hold values from 30.14656 to 120.25856
- second_in: float32 [2, 768, 1152], P(None, 'dp', 'tensor'), may hold values from 120.25856 to 481.6896
- second_mlp_out: float32 [1152, 768], P('tensor', 'dp'), may hold values from 141.23009 to 565.248
- second_gains: float32 [2, 768], P(None, 'dp'), may hold values from 752.0256 to 3008.1023
Outputs:
- output: bfloat16 [16384, 768], P(('dp', 'tensor'))
- grad_tokens: float32 [16384, 768], P(('dp', 'tensor'))
- grad_qkv: float32 [3, 768, 768], P(None, 'dp', 'tensor')
- grad_attn_out: float32 [768, 768], P('tensor', 'dp')
- grad_in: float32 [2, 768, 1152], P(None, 'dp', 'tensor')
- grad_mlp_out: float32 [1152, 768], P('tensor', 'dp')
- grad_gains: float32 [2, 768], P(None, 'dp')
- new_w_qkv: float32 [3, 768, 768], P(None, 'dp', 'tensor')
- new_w_attn_out: float32 [768, 768], P('tensor', 'dp')
- new_w_in: float32 [2, 768, 1152], P(None, 'dp', 'tensor')
- new_w_mlp_out: float32 [1152, 768], P('tensor', 'dp')
- new_gains: float32 [2, 768], P(None, 'dp')
- new_first_qkv: float32 [3, 768, 768], P(None, 'dp', 'tensor')
- new_first_attn_out: float32 [768, 768], P('tensor', 'dp')
- new_first_in: float32 [2, 768, 1152], P(None, 'dp', 'tensor')
- new_first_mlp_out: float32 [1152, 768], P('tensor', 'dp')
- new_first_gains: float32 [2, 768], P(None, 'dp')
- new_second_qkv: float32 [3, 768, 768], P(None, 'dp', 'tensor')
- new_second_attn_out: float32 [768, 768], P('tensor', 'dp')
- new_second_in: float32 [2, 768, 1152], P(None, 'dp', 'tensor')
- new_second_mlp_out: float32 [1152, 768], P('tensor', 'dp')
- new_second_gains: float32 [2, 768], P(None, 'dp')
The draws below stay inside these ranges and needn't reach their ends.
All inputs are finite; a program needn't handle non-finite values.
Results may differ from the reference program's by a relative error of at most 0.014.
The reference program's roundings to bfloat16 on the way count: a program that leaves them out, or rounds other values in their place, can miss the bound.
Values may be sent and summed in bfloat16 or wider, within the bound.
No kernel may reach another device: no remote copies, remote signals or barrier semaphores. Data moves between devices by JAX's collectives and lax.ppermute only.
A program may use at most 128 MiB of HBM per device.

```python
import math
import jax
import jax.numpy as jnp
from jax import lax

D = 768
H = 12
HD = 64
FF = 1152
L = 1024
SEQ_DEV = 2
STEP = 10
TOKENS = 16384
N_DP = 8


def raised(array, rng, source, target, shards_of, factor):
    def block_of(axis_at):
        return (jnp.arange(array.shape[axis_at]) // (array.shape[axis_at] // shards_of)).reshape((-1,) + (1,) * (array.ndim - 1 - axis_at))

    one_side = jax.random.permutation(rng, shards_of)[block_of(target)]
    other_side = (block_of(target) + shards_of // 2) % shards_of
    return jnp.where((block_of(source) == one_side) | (block_of(source) == other_side), factor * array, array)


def levels(key, dims, shards, smallest, top_value):
    factor_of, own = 1.0, jax.random.fold_in(key, 6)
    for dim, blocks in shards:
        steps = jnp.exp(jax.random.uniform(jax.random.fold_in(own, dim), (blocks,), jnp.float32, smallest / len(shards), top_value / len(shards)))
        factor_of = factor_of * jnp.repeat(steps, dims[dim] // blocks).reshape([-1 if axis == dim else 1 for axis in range(len(dims))])
    return factor_of


def noise(stream_key, extent, scale, reach, pieces=(), kind=jnp.bfloat16):
    values = jax.random.normal(stream_key, extent, jnp.float32) * scale
    if len(pieces) > 0:
        values = levels(stream_key, extent, pieces, -0.22, 0.18) * values
    return jnp.clip(values, min=-reach, max=reach).astype(kind)


def gaussian_with(key, shape, scale, reach, pieces, heavy, held_as=jnp.bfloat16):
    array = scale * jax.random.normal(key, shape, jnp.float32)
    if pieces:
        array = array * levels(key, shape, pieces, -0.22, 0.18)
    return jnp.clip(raised(array, jax.random.fold_in(key, 3), *heavy), -reach, reach).astype(held_as)


def setup_inputs(seed: int = 0) -> dict:
    key_list = jax.random.split(jax.random.key(seed), 18)
    tokens = noise(key_list[0], (TOKENS, D), 1.0, 6.0, ((0, 32),))
    cotangent = gaussian_with(key_list[1], (TOKENS, D), 1.0, 6.0, ((0, 32),), (0, 1, 32, 2.75))
    w_qkv = noise(key_list[2], (3, D, H * HD), (D // 2) ** -0.5, 0.3125, ((1, 8), (2, 4)), jnp.float32)
    w_attn_out = noise(key_list[3], (H * HD, D), (D // 8) ** -0.5, 0.625, ((0, 4), (1, 8)), jnp.float32)
    w_in = noise(key_list[4], (2, D, FF), D ** -0.5, 0.21875, ((1, 8), (2, 4)), jnp.float32)
    w_mlp_out = noise(key_list[5], (FF, D), FF ** -0.5, 0.1875, ((0, 4), (1, 8)), jnp.float32)
    gains = jnp.clip(1.0 + 0.1 * jax.random.normal(key_list[6], (2, D), jnp.float32), 0.5, 1.5)
    first_qkv = noise(key_list[7], (3, D, H * HD), (0.111 * TOKENS ** 0.5), 80.0, ((1, 8), (2, 4)), jnp.float32)
    first_attn_out = noise(key_list[8], (H * HD, D), (0.0333 * TOKENS ** 0.5), 24.0, ((0, 4), (1, 8)), jnp.float32)
    first_in = noise(key_list[9], (2, D, FF), (0.0666 * TOKENS ** 0.5), 48.0, ((1, 8), (2, 4)), jnp.float32)
    first_mlp_out = noise(key_list[10], (FF, D), (0.0722 * TOKENS ** 0.5), 56.0, ((0, 4), (1, 8)), jnp.float32)
    first_gains = noise(key_list[11], (2, D), (0.1665 * TOKENS ** 0.5), 128.0, ((1, 8),), jnp.float32)
    second_qkv = jnp.clip(jnp.exp(math.log(1336.9344) - 1.3862944 * jax.random.uniform(key_list[12], (3, D, H * HD), jnp.float32) ** levels(key_list[12], (3, D, H * HD), ((1, 8), (2, 4)), -0.2, 0.2)), 334.2336, 1336.9344)
    second_attn_out = jnp.clip(jnp.exp(math.log(120.25856) - 1.3835733 * jax.random.uniform(key_list[13], (H * HD, D), jnp.float32) ** levels(key_list[13], (H * HD, D), ((0, 4), (1, 8)), -0.2, 0.2)), 30.14656, 120.25856)
    second_in = jnp.clip(jnp.exp(math.log(481.6896) - 1.3876558 * jax.random.uniform(key_list[14], (2, D, FF), jnp.float32) ** levels(key_list[14], (2, D, FF), ((1, 8), (2, 4)), -0.2, 0.2)), 120.25856, 481.6896)
    second_mlp_out = jnp.clip(jnp.exp(math.log(565.248) - 1.3868742 * jax.random.uniform(key_list[15], (FF, D), jnp.float32) ** levels(key_list[15], (FF, D), ((0, 4), (1, 8)), -0.2, 0.2)), 141.23009, 565.248)
    second_gains = jnp.clip(jnp.exp(math.log(3008.1023) - 1.3862944 * jax.random.uniform(key_list[16], (2, D), jnp.float32) ** levels(key_list[16], (2, D), ((1, 8),), -0.2, 0.2)), 752.0256, 3008.1023)
    return dict(tokens=tokens, cotangent=cotangent, w_qkv=w_qkv, w_attn_out=w_attn_out, w_in=w_in, w_mlp_out=w_mlp_out, gains=gains, first_qkv=first_qkv, first_attn_out=first_attn_out, first_in=first_in, first_mlp_out=first_mlp_out, first_gains=first_gains, second_qkv=second_qkv, second_attn_out=second_attn_out, second_in=second_in, second_mlp_out=second_mlp_out, second_gains=second_gains)


@jax.custom_vjp
def low(v):
    return lax.optimization_barrier(v.astype(jnp.bfloat16)).astype(jnp.float32)

@jax.custom_vjp
def low_back(v):
    return v

def low_keep(v):
    return (low(v), None)

def low_pass(kept, grad):
    return (grad,)

def back_keep(v):
    return (v, None)

def back_low(kept, grad):
    return (low(grad),)
low.defvjp(low_keep, low_pass)
low_back.defvjp(back_keep, back_low)
eps_norm = 1e-05
rope_base = 160000.0
beta_one = 0.9
beta_two = 0.98
adam_eps = 1e-06
weight_rate = 0.02
gain_rate = 0.2
weight_decay = 0.01
highest = lax.Precision.HIGHEST

def layer_norm(values, scales):
    centred = values - lax.optimization_barrier(jnp.mean(values, axis=-1, keepdims=True))
    spread = lax.optimization_barrier(jnp.mean(centred * centred, axis=-1, keepdims=True))
    return centred * lax.rsqrt(spread + eps_norm) * scales

def rotary(values, seq_len):
    row_count, head_count, head_width = values.shape
    half_width = head_width // 2
    frequency = rope_base ** (-(jnp.arange(half_width, dtype=jnp.float32) * 2.0 / head_width))
    position = (jnp.arange(row_count) % seq_len).astype(jnp.float32)
    angles = position[:, None] * frequency[None, :]
    angles = jnp.concatenate([angles, angles], axis=-1)[:, None, :]
    turned = jnp.concatenate([-values[..., half_width:], values[..., :half_width]], axis=-1)
    return values * jnp.cos(angles) + turned * jnp.sin(angles)

def attend(triple):
    queries, keys, values = triple
    scores = low_back(jnp.einsum('qhd,khd->hqk', queries, keys, precision=highest) * HD ** (-0.5))
    probs = low(jax.nn.softmax(scores, axis=-1))
    return jnp.einsum('hqk,khd->qhd', probs, values, precision=highest)

def forward(tokens, w_qkv, w_attn_out, w_in, w_mlp_out, gains):
    row_count = tokens.shape[0]
    normed_one = low(layer_norm(tokens, gains[0]))
    proj = low_back(jnp.einsum('td,cdn->ctn', normed_one, low(w_qkv), precision=highest))
    queries = low(rotary(proj[0].reshape(row_count, H, HD), L)).reshape(row_count // L, L, H, HD)
    keys = low(rotary(proj[1].reshape(row_count, H, HD), L)).reshape(row_count // L, L, H, HD)
    values = low(proj[2]).reshape(row_count // L, L, H, HD)
    mixed = lax.map(jax.checkpoint(attend), (queries, keys, values))
    mixed = low(low_back(mixed.reshape(row_count, H * HD)))
    resid = tokens + low_back(jnp.dot(mixed, low(w_attn_out), precision=highest))
    normed_two = low(layer_norm(resid, gains[1]))
    both = low_back(jnp.einsum('td,cdf->ctf', normed_two, low(w_in), precision=highest))
    hidden = low(jax.nn.gelu(both[0], approximate=False) * both[1])
    return resid + low_back(jnp.dot(hidden, low(w_mlp_out), precision=highest))

def adamw(weight, grad, first, second, rate, decay):
    first_new = beta_one * first + (1.0 - beta_one) * grad
    second_new = beta_two * second + (1.0 - beta_two) * grad * grad
    step_size = first_new / (1.0 - beta_one ** STEP) / (jnp.sqrt(second_new / (1.0 - beta_two ** STEP)) + adam_eps)
    return (weight - rate * (step_size + decay * weight), first_new, second_new)

def reference(tokens, cotangent, w_qkv, w_attn_out, w_in, w_mlp_out, gains, first_qkv, first_attn_out, first_in, first_mlp_out, first_gains, second_qkv, second_attn_out, second_in, second_mlp_out, second_gains):
    group_rows = SEQ_DEV * L
    inputs = tokens.astype(jnp.float32).reshape(N_DP, group_rows, D)
    pulls = cotangent.astype(jnp.float32).reshape(N_DP, group_rows, D)
    params = (w_qkv, w_attn_out, w_in, w_mlp_out, gains)

    def one_group(carry, item):
        source, incoming = item
        result, pull_fn = jax.vjp(forward, source, *params)
        grads = pull_fn(incoming)
        return (tuple((total + part for total, part in zip(carry, grads[1:]))), (result.astype(jnp.bfloat16), grads[0]))
    zeros = tuple((jnp.zeros_like(param) for param in params))
    sums, (outputs, grad_inputs) = lax.scan(one_group, zeros, (inputs, pulls))
    firsts = (first_qkv, first_attn_out, first_in, first_mlp_out, first_gains)
    seconds = (second_qkv, second_attn_out, second_in, second_mlp_out, second_gains)
    updated = []
    for index in range(5):
        rate = gain_rate if index == 4 else weight_rate
        decay = 0.0 if index == 4 else weight_decay
        updated.append(adamw(params[index], sums[index], firsts[index], seconds[index], rate, decay))
    return (outputs.reshape(N_DP * group_rows, D), grad_inputs.reshape(N_DP * group_rows, D), sums[0], sums[1], sums[2], sums[3], sums[4], updated[0][0], updated[1][0], updated[2][0], updated[3][0], updated[4][0], updated[0][1], updated[1][1], updated[2][1], updated[3][1], updated[4][1], updated[0][2], updated[1][2], updated[2][2], updated[3][2], updated[4][2])
```

```python
import functools

import jax
import jax.numpy as jnp
import numpy as np
from jax import lax
from jax.experimental import pallas as pl
from jax.experimental.pallas import tpu as pltpu
from jax.sharding import PartitionSpec as P

HD = 64
L = 1024
STEP = 10


eps_norm = 1e-05
rope_base = 160000.0
beta_one = 0.9
beta_two = 0.98
adam_eps = 1e-06
weight_rate = 0.02
gain_rate = 0.2
weight_decay = 0.01

low = jnp.bfloat16
full = jnp.float32
ROWS = 256
PAIR = 2 * HD
VMEM_BYTES = 52 << 20


def dot(left, right, left_dim, right_dim):
    return lax.dot_general(
        left, right, (((left_dim,), (right_dim,)), ((), ())), preferred_element_type=full
    )


def params():
    return pltpu.CompilerParams(vmem_limit_bytes=VMEM_BYTES)


def whole(shape):
    return pl.BlockSpec(shape, lambda *_: (0,) * len(shape))


def rows_of(width, index=lambda i: i):
    return pl.BlockSpec((ROWS, width), lambda i: (index(i), 0))


def own_half(i):
    return jnp.minimum(i, L // ROWS // 2 - 1)


def other_half(i):
    return jnp.maximum(i - L // ROWS // 2, 0)


def swapped(i):
    return (i + L // ROWS // 2) % (L // ROWS)


def is_own(i):
    return i < L // ROWS // 2


def core_swap(array):
    return lax.ppermute(array, "tensor", [(t, t ^ 1) for t in range(4)])


def y_swap(array):
    return lax.ppermute(array, "tensor", [(t, t ^ 2) for t in range(4)])


def x_swap(array, count):
    return lax.ppermute(array, "dp", [(d, d ^ 1) for d in range(count)])


def z_shift(array, count, step):
    around = count // 2
    return lax.ppermute(
        array, "dp", [(d, (d // 2 + step) % around * 2 + d % 2) for d in range(count)]
    )


def staged(count):
    return count == 8


def assemble_kernel(widths, place_ref, za, xa, ya, zb, yb, xb, *outs):
    place = place_ref[0]
    half = za.shape[1]
    for jx in range(2):
        for jz in range(4):
            source = (place // 2 + 4 - jz) % 4 * 2 + (place % 2 + jx) % 2
            own_a = (za, xa)[jx][jz]
            other_a = ya[jx, jz]
            own_b = zb[jz] if jx == 0 else xb[0, jz]
            other_b = yb[jz] if jx == 0 else xb[1, jz]
            for part, (own, other) in enumerate(((own_a, other_a), (own_b, other_b))):
                start = pl.multiple_of(source * 2 * half + part * half, half)
                offset = 0
                for width, out in zip(widths, outs):
                    out[pl.ds(start, half), :] = jnp.concatenate(
                        [own[:, offset : offset + width], other[:, offset : offset + width]], axis=1
                    )
                    offset += width


def gather_weights(parts, count):
    widths = [part.shape[1] for part in parts]
    shard = jnp.concatenate(parts, axis=1)
    height, total = shard.shape
    if not staged(count):
        own = lax.all_gather(shard, "dp", axis=0, tiled=True)
        other = y_swap(own)
        gathered, offset = [], 0
        for width in widths:
            gathered.append(
                jnp.concatenate(
                    [own[:, offset : offset + width], other[:, offset : offset + width]], axis=1
                )
            )
            offset += width
        return gathered
    half = height // 2
    along_z = [shard] + [z_shift(shard, count, step) for step in (1, 2, 3)]
    za = jnp.stack([piece[:half] for piece in along_z])
    zb = jnp.stack([piece[half:] for piece in along_z])
    xa = x_swap(za, count)
    yb = y_swap(zb)
    ya = y_swap(jnp.stack([za, xa]))
    xb = x_swap(jnp.stack([zb, yb]), count)
    place = lax.axis_index("dp").astype(jnp.int32)[None]
    return pl.pallas_call(
        functools.partial(assemble_kernel, widths),
        in_specs=[pl.BlockSpec(memory_space=pltpu.SMEM)]
        + [pl.BlockSpec(memory_space=pltpu.VMEM)] * 6,
        out_specs=[pl.BlockSpec(memory_space=pltpu.VMEM)] * len(widths),
        out_shape=[jax.ShapeDtypeStruct((height * count, 2 * width), low) for width in widths],
        compiler_params=params(),
        name="assemble",
    )(place, za, xa, ya, zb, yb, xb)


def weight_grad_kernel(pairs, sources, fast, place_ref, *refs):
    ins, outs, scratch = refs[: sources], refs[sources : sources + 4], refs[sources + 4 :]
    place = place_ref[0]
    for (left, right), held in zip(pairs, scratch):
        held[...] = dot(ins[left][...], ins[right][...], 0, 0)
    if not fast:
        offset = 0
        for held in scratch:
            width = held.shape[1] // 2
            outs[0][:, offset : offset + width] = held[:, :width].astype(low)
            outs[1][:, offset : offset + width] = held[:, width:].astype(low)
            offset += width
        return
    ay, by, ax, bx = outs
    half = ay.shape[2]
    for jx in range(2):
        for jz in range(4):
            target = (place // 2 + jz) % 4 * 2 + (place % 2 + jx) % 2
            for part in range(2):
                start = pl.multiple_of(target * 2 * half + part * half, half)
                own, other = [], []
                for held in scratch:
                    width = held.shape[1] // 2
                    rows = held[pl.ds(start, half), :].astype(low)
                    own.append(rows[:, :width])
                    other.append(rows[:, width:])
                own = jnp.concatenate(own, axis=1)
                other = jnp.concatenate(other, axis=1)
                if part == 0:
                    ay[jx, jz] = own
                    by[jx, jz] = other
                else:
                    (ax, bx)[jx][0, jz] = own
                    (ax, bx)[jx][1, jz] = other


def reduced_weight_grad(arrays, pairs, count):
    depth = arrays[pairs[0][0]].shape[1]
    widths = [arrays[right].shape[1] for _, right in pairs]
    total = sum(widths) // 2
    fast = staged(count)
    if fast:
        half = depth // count // 2
        outs = [jax.ShapeDtypeStruct((2, 4, half, total), low)] * 4
    else:
        outs = [jax.ShapeDtypeStruct((depth, total), low)] * 2 + [
            jax.ShapeDtypeStruct((8, 128), low)
        ] * 2
    place = lax.axis_index("dp").astype(jnp.int32)[None]
    flops = 2 * depth * sum(widths) * L
    first, second, third, fourth = pl.pallas_call(
        functools.partial(weight_grad_kernel, pairs, len(arrays), fast),
        in_specs=[pl.BlockSpec(memory_space=pltpu.SMEM)]
        + [pl.BlockSpec(memory_space=pltpu.VMEM)] * len(arrays),
        out_specs=[pl.BlockSpec(memory_space=pltpu.VMEM)] * 4,
        out_shape=outs,
        scratch_shapes=[pltpu.VMEM((depth, width), full) for width in widths],
        compiler_params=params(),
        cost_estimate=pl.CostEstimate(
            flops=flops, bytes_accessed=4 * depth * sum(widths), transcendentals=0
        ),
        name="weight_grad",
    )(place, *arrays)
    if not fast:
        summed = first.astype(full) + y_swap(second).astype(full)
        return lax.psum_scatter(summed, "dp", scatter_dimension=0, tiled=True)

    def add(here, there):
        return (here.astype(full) + there.astype(full)).astype(low)

    from_y = y_swap(second)
    from_x = x_swap(fourth, count)
    part_a = add(first, from_y)
    part_b = add(third, from_x)
    next_a = x_swap(part_a[1], count)
    next_b = y_swap(part_b[1])
    merged = jnp.concatenate([add(part_a[0], next_a), add(part_b[0], next_b)], axis=1)
    result = merged[0].astype(full)
    for step in (1, 2, 3):
        result = result + z_shift(merged[step], count, step).astype(full)
    return result


def sum_everywhere(array, count):
    array = array + core_swap(array)
    array = array + y_swap(array)
    if not staged(count):
        return lax.psum(array, "dp")
    array = array + x_swap(array, count)
    return array + sum(z_shift(array, count, step) for step in (1, 2, 3))


def gather_gains(gains, count):
    if not staged(count):
        return lax.all_gather(gains, "dp", axis=1, tiled=True)
    along_z = jnp.stack([gains] + [z_shift(gains, count, step) for step in (1, 2, 3)])
    pieces = jnp.concatenate([along_z, x_swap(along_z, count)])
    place = lax.axis_index("dp")
    order = np.arange(count)
    sources = (place // 2 + 4 - order % 4) % 4 * 2 + (place % 2 + order // 4) % 2
    chosen = sources[:, None] == order[None, :]
    spread = jnp.where(chosen[:, :, None, None], pieces[:, None], 0.0).sum(axis=0)
    return spread.transpose(1, 0, 2).reshape(gains.shape[0], -1)


def normalized(values):
    centred = values - jnp.mean(values, axis=-1, keepdims=True)
    spread = jnp.mean(centred * centred, axis=-1, keepdims=True)
    scale = lax.rsqrt(spread + eps_norm)
    return centred * scale, scale


def norm_back(values, scales, grads):
    unit, scale = normalized(values)
    inner = grads * scales
    mean_inner = jnp.mean(inner, axis=-1, keepdims=True)
    mean_unit = jnp.mean(inner * unit, axis=-1, keepdims=True)
    return scale * (inner - mean_inner - unit * mean_unit), jnp.sum(
        grads * unit, axis=0, keepdims=True
    )


def rope_tables(offset):
    half_width = HD // 2
    frequency = rope_base ** (-(jnp.arange(half_width, dtype=full) * 2.0 / HD))
    position = ((jnp.arange(L) + offset) % L).astype(full)
    angles = position[:, None] * frequency[None, :]
    cosine, sine = jnp.cos(angles), jnp.sin(angles)
    return (
        jnp.concatenate([cosine] * 4, axis=1),
        jnp.concatenate([-sine, sine, -sine, sine], axis=1),
    )


def turn(values, cosine, sine):
    lane = lax.broadcasted_iota(jnp.int32, values.shape, 1)
    ahead = pltpu.roll(values, PAIR - HD // 2, 1)
    behind = pltpu.roll(values, HD // 2, 1)
    turned = jnp.where(lane % HD < HD // 2, ahead, behind)
    return values * cosine + turned * sine


def qkv_kernel(x_own, x_other, gain, wq, wk, wv, cosine, sine, normed, q_out, k_out, v_out):
    values = jnp.where(is_own(pl.program_id(0)), x_own[...], x_other[...]).astype(full)
    unit, _ = normalized(values)
    rows = (unit * gain[...]).astype(low)
    normed[...] = rows
    query = dot(rows, wq[...], 1, 0)
    key = dot(rows, wk[...], 1, 0)
    for start in range(0, query.shape[1], PAIR):
        lanes = slice(start, start + PAIR)
        turned = turn(query[:, lanes], cosine[...], sine[...]).astype(low)
        q_out[:, lanes] = turned * jnp.asarray(HD ** (-0.5), low)
        k_out[:, lanes] = turn(key[:, lanes], cosine[...], sine[...]).astype(low)
    v_out[...] = dot(rows, wv[...], 1, 0).astype(low)


def project(x_own, x_other, gain, wq, wk, wv, cosine, sine):
    depth, width = wq.shape
    return pl.pallas_call(
        qkv_kernel,
        grid=(L // ROWS,),
        in_specs=[
            rows_of(depth, own_half),
            rows_of(depth, other_half),
            whole((1, depth)),
            whole((depth, width)),
            whole((depth, width)),
            whole((depth, width)),
            rows_of(PAIR),
            rows_of(PAIR),
        ],
        out_specs=[rows_of(depth), rows_of(width), rows_of(width), rows_of(width)],
        out_shape=[jax.ShapeDtypeStruct((L, depth), low)]
        + [jax.ShapeDtypeStruct((L, width), low)] * 3,
        compiler_params=params(),
        cost_estimate=pl.CostEstimate(
            flops=6 * L * depth * width, bytes_accessed=8 * L * depth, transcendentals=0
        ),
        name="project",
    )(x_own, x_other, gain, wq, wk, wv, cosine, sine)


def head_masks(height):
    lane = lax.broadcasted_iota(jnp.int32, (height, PAIR), 1)
    return [(lane // HD == head).astype(full).astype(low) for head in range(2)]


def attend_kernel(q_ref, k_ref, v_ref, mixed, lse_ref):
    keys, values = k_ref[...], v_ref[...]
    masks = head_masks(ROWS)
    lane = lax.broadcasted_iota(jnp.int32, (ROWS, PAIR), 1)
    for start in range(0, L, ROWS):
        rows = slice(start, start + ROWS)
        query = q_ref[rows, :]
        results = []
        for head in range(2):
            scores = dot(query * masks[head], keys, 1, 1)
            row_max = jnp.max(scores, axis=1, keepdims=True)
            raised = jnp.exp(scores - row_max)
            total = jnp.sum(raised, axis=1, keepdims=True)
            results.append(dot(raised.astype(low), values, 1, 0) / total)
            lse = jnp.broadcast_to(row_max + jnp.log(total), (ROWS, PAIR))
            lse_ref[0, head : head + 1, rows] = lse.T[0:1]
        mixed[rows, :] = jnp.where(lane < HD, results[0], results[1]).astype(low)


def attend(query, key, value):
    width = query.shape[1]
    pairs = width // PAIR
    block = pl.BlockSpec((L, PAIR), lambda i: (0, i))
    totals = pl.BlockSpec((1, 2, L), lambda i: (i, 0, 0))
    return pl.pallas_call(
        attend_kernel,
        grid=(pairs,),
        in_specs=[block] * 3,
        out_specs=[block, totals],
        out_shape=[
            jax.ShapeDtypeStruct((L, width), low),
            jax.ShapeDtypeStruct((pairs, 2, L), full),
        ],
        compiler_params=params(),
        cost_estimate=pl.CostEstimate(
            flops=16 * L * L * width, bytes_accessed=8 * L * width, transcendentals=2 * pairs * L * L
        ),
        name="attend",
    )(query, key, value)


def attend_back_kernel(
    q_ref, k_ref, v_ref, o_ref, grad_ref, lse_ref, cosine, sine, dq_out, dk_out, dv_out, dk, dv
):
    masks = head_masks(L)
    chunk_masks = head_masks(ROWS)
    keys, values = k_ref[...], v_ref[...]
    head_keys = [keys * mask for mask in masks]
    head_values = [values * mask for mask in masks]
    product = (grad_ref[...].astype(full) * o_ref[...].astype(full)).T
    inner = [jnp.sum(product[head * HD : (head + 1) * HD], axis=0, keepdims=True) for head in range(2)]
    for start in range(0, L, ROWS):
        rows = slice(start, start + ROWS)
        query, grad = q_ref[rows, :], grad_ref[rows, :]
        dq = None
        for head in range(2):
            scores = dot(head_keys[head], query, 1, 1)
            probs = jnp.exp(scores - lse_ref[0, head : head + 1, rows])
            grad_probs = dot(head_values[head], grad, 1, 1)
            grad_scores = (probs * (grad_probs - inner[head][:, rows])).astype(low)
            add_v = dot(probs.astype(low), grad * chunk_masks[head], 1, 0)
            add_k = dot(grad_scores, query * chunk_masks[head], 1, 0)
            add_q = dot(grad_scores, head_keys[head], 0, 0)
            dq = add_q if dq is None else dq + add_q
            if start == 0 and head == 0:
                dv[...] = add_v
                dk[...] = add_k
            else:
                dv[...] += add_v
                dk[...] += add_k
        dq_out[rows, :] = turn(dq * HD ** (-0.5), cosine[rows, :], -sine[rows, :]).astype(low)
    dk_out[...] = turn(dk[...], cosine[...], -sine[...]).astype(low)
    dv_out[...] = dv[...].astype(low)


def attend_back(query, key, value, mixed, grad, lse, cosine, sine):
    width = query.shape[1]
    pairs = width // PAIR
    block = pl.BlockSpec((L, PAIR), lambda i: (0, i))
    totals = pl.BlockSpec((1, 2, L), lambda i: (i, 0, 0))
    return pl.pallas_call(
        attend_back_kernel,
        grid=(pairs,),
        in_specs=[block] * 5 + [totals] + [whole((L, PAIR))] * 2,
        out_specs=[block] * 3,
        out_shape=[jax.ShapeDtypeStruct((L, width), low)] * 3,
        scratch_shapes=[pltpu.VMEM((L, PAIR), full)] * 2,
        compiler_params=params(),
        cost_estimate=pl.CostEstimate(
            flops=40 * L * L * width, bytes_accessed=16 * L * width, transcendentals=2 * pairs * L * L
        ),
        name="attend_back",
    )(query, key, value, mixed, grad, lse, cosine, sine)


def feed_forward_kernel(
    mixed_own,
    mixed_other,
    x_own,
    x_other,
    dy_own,
    dy_other,
    gain,
    wo_own,
    wo_other,
    w_gate,
    w_up,
    w_down,
    resid_out,
    normed,
    hidden_out,
    dgate_out,
    dup_out,
    out_own,
    out_other,
    dnormed,
    dnormed_low,
):
    step = pl.program_id(0)
    own = is_own(step)
    tokens = jnp.where(own, x_own[...], x_other[...]).astype(full)
    pull = jnp.where(own, dy_own[...], dy_other[...])
    resid = (
        tokens + dot(mixed_own[...], wo_own[...], 1, 1) + dot(mixed_other[...], wo_other[...], 1, 1)
    )
    resid_out[...] = resid
    unit, _ = normalized(resid)
    rows = (unit * gain[...]).astype(low)
    normed[...] = rows
    gate = dot(rows, w_gate[...], 1, 0)
    up = dot(rows, w_up[...], 1, 0)
    cumulative = 0.5 + 0.5 * lax.erf(gate * np.float32(0.5**0.5))
    density = jnp.exp(gate * gate * -0.5) * np.float32((2.0 * np.pi) ** -0.5)
    activated = gate * cumulative
    hidden = (activated * up).astype(low)
    hidden_out[...] = hidden
    part = dot(hidden, w_down[...], 1, 1)

    @pl.when(own)
    def _():
        out_own[...] = resid + part

    @pl.when(jnp.logical_not(own))
    def _():
        out_other[...] = part.astype(low)

    dhidden = dot(pull, w_down[...], 1, 0)
    dgate = (dhidden * up * (cumulative + gate * density)).astype(low)
    dup = (dhidden * activated).astype(low)
    dgate_out[...] = dgate
    dup_out[...] = dup
    grad = dot(dgate, w_gate[...], 1, 1) + dot(dup, w_up[...], 1, 1)
    dnormed[...] = grad
    dnormed_low[...] = grad.astype(low)


def feed_forward(
    mixed, mixed_other, x_own, x_other, dy_own, dy_other, gain, wo, wo_other, w_gate, w_up, w_down
):
    depth, width = wo.shape
    units = w_gate.shape[1]
    half = L // 2
    return pl.pallas_call(
        feed_forward_kernel,
        grid=(L // ROWS,),
        in_specs=[
            rows_of(width),
            rows_of(width, swapped),
            rows_of(depth, own_half),
            rows_of(depth, other_half),
            rows_of(depth, own_half),
            rows_of(depth, other_half),
            whole((1, depth)),
            whole((depth, width)),
            whole((depth, width)),
            whole((depth, units)),
            whole((depth, units)),
            whole((depth, units)),
        ],
        out_specs=[
            rows_of(depth),
            rows_of(depth),
            rows_of(units),
            rows_of(units),
            rows_of(units),
            rows_of(depth, own_half),
            rows_of(depth, other_half),
            rows_of(depth),
            rows_of(depth),
        ],
        out_shape=[
            jax.ShapeDtypeStruct((L, depth), full),
            jax.ShapeDtypeStruct((L, depth), low),
            jax.ShapeDtypeStruct((L, units), low),
            jax.ShapeDtypeStruct((L, units), low),
            jax.ShapeDtypeStruct((L, units), low),
            jax.ShapeDtypeStruct((half, depth), full),
            jax.ShapeDtypeStruct((half, depth), low),
            jax.ShapeDtypeStruct((L, depth), full),
            jax.ShapeDtypeStruct((L, depth), low),
        ],
        compiler_params=params(),
        cost_estimate=pl.CostEstimate(
            flops=2 * L * depth * (2 * width + 6 * units),
            bytes_accessed=24 * L * depth,
            transcendentals=2 * L * units,
        ),
        name="feed_forward",
    )(mixed, mixed_other, x_own, x_other, dy_own, dy_other, gain, wo, wo_other, w_gate, w_up, w_down)


def resid_back_kernel(
    resid, grad_own, grad_other, dy_own, dy_other, gain, wo, dresid, dresid_low, dmixed, gain_grad
):
    step = pl.program_id(0)
    own = is_own(step)
    pull = jnp.where(own, dy_own[...], dy_other[...]).astype(full)
    grads = grad_own[...] + grad_other[...].astype(full)
    back, gain_part = norm_back(resid[...], gain[...], grads)
    total = pull + back
    rounded = total.astype(low)
    dresid_low[...] = rounded
    dmixed[...] = dot(rounded, wo[...], 1, 0).astype(low)

    @pl.when(step == 0)
    def _():
        gain_grad[...] = jnp.zeros_like(gain_grad)

    @pl.when(own)
    def _():
        dresid[...] = total
        gain_grad[...] += gain_part


def resid_back(resid, grad_own, grad_other, dy_own, dy_other, gain, wo):
    depth, width = wo.shape
    return pl.pallas_call(
        resid_back_kernel,
        grid=(L // ROWS,),
        in_specs=[
            rows_of(depth),
            rows_of(depth),
            rows_of(depth, swapped),
            rows_of(depth, own_half),
            rows_of(depth, other_half),
            whole((1, depth)),
            whole((depth, width)),
        ],
        out_specs=[rows_of(depth, own_half), rows_of(depth), rows_of(width), whole((1, depth))],
        out_shape=[
            jax.ShapeDtypeStruct((L // 2, depth), full),
            jax.ShapeDtypeStruct((L, depth), low),
            jax.ShapeDtypeStruct((L, width), low),
            jax.ShapeDtypeStruct((1, depth), full),
        ],
        compiler_params=params(),
        cost_estimate=pl.CostEstimate(
            flops=2 * L * depth * width, bytes_accessed=16 * L * depth, transcendentals=0
        ),
        name="resid_back",
    )(resid, grad_own, grad_other, dy_own, dy_other, gain, wo)


def project_back_kernel(dq, dk, dv, wq, wk, wv, grad_own, grad_other):
    grad = (
        dot(dq[...], wq[...], 1, 1) + dot(dk[...], wk[...], 1, 1) + dot(dv[...], wv[...], 1, 1)
    )
    own = is_own(pl.program_id(0))

    @pl.when(own)
    def _():
        grad_own[...] = grad

    @pl.when(jnp.logical_not(own))
    def _():
        grad_other[...] = grad.astype(low)


def project_back(dq, dk, dv, wq, wk, wv):
    depth, width = wq.shape
    return pl.pallas_call(
        project_back_kernel,
        grid=(L // ROWS,),
        in_specs=[rows_of(width)] * 3 + [whole((depth, width))] * 3,
        out_specs=[rows_of(depth, own_half), rows_of(depth, other_half)],
        out_shape=[
            jax.ShapeDtypeStruct((L // 2, depth), full),
            jax.ShapeDtypeStruct((L // 2, depth), low),
        ],
        compiler_params=params(),
        cost_estimate=pl.CostEstimate(
            flops=6 * L * depth * width, bytes_accessed=8 * L * depth, transcendentals=0
        ),
        name="project_back",
    )(dq, dk, dv, wq, wk, wv)


def input_back_kernel(tokens, grad_own, grad_other, dresid, gain, result, gain_grad):
    grads = grad_own[...] + grad_other[...].astype(full)
    back, gain_part = norm_back(tokens[...].astype(full), gain[...], grads)
    result[...] = dresid[...] + back

    @pl.when(pl.program_id(0) == 0)
    def _():
        gain_grad[...] = jnp.zeros_like(gain_grad)

    gain_grad[...] += gain_part


def input_back(tokens, grad_own, grad_other, dresid, gain):
    height, depth = tokens.shape
    return pl.pallas_call(
        input_back_kernel,
        grid=(height // ROWS,),
        in_specs=[rows_of(depth)] * 4 + [whole((1, depth))],
        out_specs=[rows_of(depth), whole((1, depth))],
        out_shape=[
            jax.ShapeDtypeStruct((height, depth), full),
            jax.ShapeDtypeStruct((1, depth), full),
        ],
        compiler_params=params(),
        cost_estimate=pl.CostEstimate(
            flops=20 * height * depth, bytes_accessed=16 * height * depth, transcendentals=0
        ),
        name="input_back",
    )(tokens, grad_own, grad_other, dresid, gain)


def adamw(weight, grad, first, second, rate, decay):
    first_new = beta_one * first + (1.0 - beta_one) * grad
    second_new = beta_two * second + (1.0 - beta_two) * grad * grad
    step_size = (
        first_new
        / (1.0 - beta_one**STEP)
        / (jnp.sqrt(second_new / (1.0 - beta_two**STEP)) + adam_eps)
    )
    return (weight - rate * (step_size + decay * weight), first_new, second_new)


def shards(
    tokens,
    cotangent,
    w_qkv,
    w_attn_out,
    w_in,
    w_mlp_out,
    gains,
    first_qkv,
    first_attn_out,
    first_in,
    first_mlp_out,
    first_gains,
    second_qkv,
    second_attn_out,
    second_in,
    second_mlp_out,
    second_gains,
):
    count = lax.axis_size("dp")
    core = lax.axis_index("tensor") % 2
    place = lax.axis_index("dp")
    x_other = core_swap(tokens)
    gains_all = gather_gains(gains, count)
    gain_one, gain_two = gains_all[0:1], gains_all[1:2]
    wq, wk, wv = gather_weights([w_qkv[c].astype(low) for c in range(3)], count)
    wo, w_gate, w_up, w_down = gather_weights(
        [w_attn_out.astype(low).T, w_in[0].astype(low), w_in[1].astype(low), w_mlp_out.astype(low).T],
        count,
    )
    wo_other = core_swap(wo)
    dy_other = core_swap(cotangent)
    cosine, sine = rope_tables(core * (L // 2))

    normed_one, query, key, value = project(
        tokens, x_other, gain_one, wq, wk, wv, cosine, sine
    )
    mixed, lse = attend(query, key, value)
    mixed_other = core_swap(mixed)
    resid, normed_two, hidden, dgate, dup, out_own, out_other, dnormed, dnormed_low = feed_forward(
        mixed,
        mixed_other,
        tokens,
        x_other,
        cotangent,
        dy_other,
        gain_two,
        wo,
        wo_other,
        w_gate,
        w_up,
        w_down,
    )
    dnormed_other = core_swap(dnormed_low)
    output = (out_own + core_swap(out_other).astype(full)).astype(low)
    dy_rows = jnp.concatenate([cotangent, dy_other])
    grad_mlp = reduced_weight_grad(
        [normed_two, dgate, dup, dy_rows, hidden], [(0, 1), (0, 2), (3, 4)], count
    )
    dresid, dresid_low, dmixed, grad_gain_two = resid_back(
        resid, dnormed, dnormed_other, cotangent, dy_other, gain_two, wo
    )
    dq, dk, dv = attend_back(query, key, value, mixed, dmixed, lse, cosine, sine)
    grad_attn = reduced_weight_grad([dresid_low, mixed], [(0, 1)], count)
    grad_proj = reduced_weight_grad([normed_one, dq, dk, dv], [(0, 1), (0, 2), (0, 3)], count)
    grad_one, grad_one_low = project_back(dq, dk, dv, wq, wk, wv)
    grad_inputs, grad_gain_one = input_back(
        tokens, grad_one, core_swap(grad_one_low), dresid, gain_one
    )
    grad_gains = sum_everywhere(jnp.concatenate([grad_gain_one, grad_gain_two]), count)

    head_width = w_qkv.shape[2]
    unit_width = w_in.shape[2]
    shard_qkv = jnp.stack([grad_proj[:, c * head_width : (c + 1) * head_width] for c in range(3)])
    shard_attn = grad_attn.T
    shard_in = jnp.stack([grad_mlp[:, c * unit_width : (c + 1) * unit_width] for c in range(2)])
    shard_down = grad_mlp[:, 2 * unit_width :].T
    shard_gain = lax.dynamic_slice_in_dim(grad_gains, place * gains.shape[1], gains.shape[1], axis=1)

    new_qkv = adamw(w_qkv, shard_qkv, first_qkv, second_qkv, weight_rate, weight_decay)
    new_attn = adamw(
        w_attn_out, shard_attn, first_attn_out, second_attn_out, weight_rate, weight_decay
    )
    new_in = adamw(w_in, shard_in, first_in, second_in, weight_rate, weight_decay)
    new_down = adamw(
        w_mlp_out, shard_down, first_mlp_out, second_mlp_out, weight_rate, weight_decay
    )
    new_gain = adamw(gains, shard_gain, first_gains, second_gains, gain_rate, 0.0)
    return (
        output,
        grad_inputs,
        shard_qkv,
        shard_attn,
        shard_in,
        shard_down,
        shard_gain,
        new_qkv[0],
        new_attn[0],
        new_in[0],
        new_down[0],
        new_gain[0],
        new_qkv[1],
        new_attn[1],
        new_in[1],
        new_down[1],
        new_gain[1],
        new_qkv[2],
        new_attn[2],
        new_in[2],
        new_down[2],
        new_gain[2],
    )


def solution(mesh):
    return jax.shard_map(
        shards,
        mesh=mesh,
        in_specs=(
            P(("dp", "tensor"), None),
            P(("dp", "tensor"), None),
            P(None, "dp", "tensor"),
            P("tensor", "dp"),
            P(None, "dp", "tensor"),
            P("tensor", "dp"),
            P(None, "dp"),
            P(None, "dp", "tensor"),
            P("tensor", "dp"),
            P(None, "dp", "tensor"),
            P("tensor", "dp"),
            P(None, "dp"),
            P(None, "dp", "tensor"),
            P("tensor", "dp"),
            P(None, "dp", "tensor"),
            P("tensor", "dp"),
            P(None, "dp"),
        ),
        out_specs=(
            P(("dp", "tensor"), None),
            P(("dp", "tensor"), None),
            P(None, "dp", "tensor"),
            P("tensor", "dp"),
            P(None, "dp", "tensor"),
            P("tensor", "dp"),
            P(None, "dp"),
            P(None, "dp", "tensor"),
            P("tensor", "dp"),
            P(None, "dp", "tensor"),
            P("tensor", "dp"),
            P(None, "dp"),
            P(None, "dp", "tensor"),
            P("tensor", "dp"),
            P(None, "dp", "tensor"),
            P("tensor", "dp"),
            P(None, "dp"),
            P(None, "dp", "tensor"),
            P("tensor", "dp"),
            P(None, "dp", "tensor"),
            P("tensor", "dp"),
            P(None, "dp"),
        ),
        check_vma=False,
    )
```

```python
import functools

import jax
import jax.numpy as jnp
import numpy as np
from jax import lax
from jax.experimental import pallas as pl
from jax.experimental.pallas import tpu as pltpu
from jax.sharding import PartitionSpec as P

HD = 64
L = 1024
STEP = 10


eps_norm = 1e-05
rope_base = 160000.0
beta_one = 0.9
beta_two = 0.98
adam_eps = 1e-06
weight_rate = 0.02
gain_rate = 0.2
weight_decay = 0.01

low = jnp.bfloat16
full = jnp.float32
ROWS = 256
PAIR = 2 * HD
VMEM_BYTES = 52 << 20
SPARE = 64


def dot(left, right, left_dim, right_dim):
    return lax.dot_general(
        left, right, (((left_dim,), (right_dim,)), ((), ())), preferred_element_type=full
    )


def params():
    return pltpu.CompilerParams(vmem_limit_bytes=VMEM_BYTES)


def whole(shape):
    return pl.BlockSpec(shape, lambda *_: (0,) * len(shape))


def rows_of(width, index=lambda i: i):
    return pl.BlockSpec((ROWS, width), lambda i: (index(i), 0))


def own_half(i):
    return jnp.minimum(i, L // ROWS // 2 - 1)


def other_half(i):
    return jnp.maximum(i - L // ROWS // 2, 0)


def swapped(i):
    return (i + L // ROWS // 2) % (L // ROWS)


def is_own(i):
    return i < L // ROWS // 2


def core_swap(array):
    return lax.ppermute(array, "tensor", [(t, t ^ 1) for t in range(4)])


def y_swap(array):
    return lax.ppermute(array, "tensor", [(t, t ^ 2) for t in range(4)])


def x_swap(array, count):
    return lax.ppermute(array, "dp", [(d, d ^ 1) for d in range(count)])


def z_shift(array, count, step):
    around = count // 2
    return lax.ppermute(
        array, "dp", [(d, (d // 2 + step) % around * 2 + d % 2) for d in range(count)]
    )


def staged(count):
    return count == 8


def after(array, *others):
    return lax.optimization_barrier((array, *others))[0]


ANY = pl.BlockSpec(memory_space=pl.ANY)
LOCAL = pl.BlockSpec(memory_space=pltpu.VMEM)
SCALAR = pl.BlockSpec(memory_space=pltpu.SMEM)


def call(kernel, name, ins, shapes, later=(), place=None, scratch=(), cost=0):
    head = [] if place is None else [place]
    lead, skip = len(head), len(later)

    def body(*refs):
        kernel(*refs[: lead + len(ins)], *refs[lead + len(ins) + skip :])

    return pl.pallas_call(
        body,
        in_specs=[SCALAR] * lead + [LOCAL] * len(ins) + [ANY] * skip,
        out_specs=[LOCAL] * len(shapes),
        out_shape=shapes,
        scratch_shapes=list(scratch),
        compiler_params=params(),
        cost_estimate=pl.CostEstimate(
            flops=cost, bytes_accessed=sum(2 * array.size for array in ins), transcendentals=0
        ),
        name=name,
    )(*head, *ins, *later)


def like(shape, kind=low):
    return jax.ShapeDtypeStruct(shape, kind)


def pack_kernel(w_qkv, gains, shard, padded):
    rows = w_qkv.shape[1]
    padded[...] = jnp.zeros_like(padded)
    padded[0 : gains.shape[0], 0:rows] = gains[...]
    columns = padded[...].T[0:rows, 0:2]
    high = columns.astype(low)
    rest = columns - high.astype(full)
    middle = rest.astype(low)
    last = (rest - middle.astype(full)).astype(low)
    filler = jnp.zeros((rows, SPARE - 6), full)
    pieces = [w_qkv[part] for part in range(3)]
    shard[...] = jnp.concatenate(
        pieces + [high.astype(full), middle.astype(full), last.astype(full), filler], axis=1
    ).astype(low)


def pack(w_qkv, gains):
    rows, width = w_qkv.shape[1:]
    return call(
        pack_kernel,
        "pack",
        [w_qkv, gains],
        [like((rows, 3 * width + SPARE))],
        scratch=[pltpu.VMEM((128, 128), full)],
    )[0]


def unpack_gains(columns):
    wide = jnp.concatenate([columns.astype(full), jnp.zeros(columns.shape, full)], axis=1).T
    return wide[0:2] + wide[2:4] + wide[4:6]


def assemble_kernel(widths, with_gains, place_ref, za, xa, ya, zb, yb, xb, *outs):
    place = place_ref[0]
    half = za.shape[1]
    total = sum(widths)
    for jx in range(2):
        for jz in range(4):
            source = (place // 2 + 4 - jz) % 4 * 2 + (place % 2 + jx) % 2
            own_a = (za, xa)[jx][jz]
            other_a = ya[jx, jz]
            own_b = zb[jz] if jx == 0 else xb[0, jz]
            other_b = yb[jz] if jx == 0 else xb[1, jz]
            for part, (own, other) in enumerate(((own_a, other_a), (own_b, other_b))):
                start = pl.multiple_of(source * 2 * half + part * half, half)
                offset = 0
                for width, out in zip(widths, outs):
                    out[pl.ds(start, half), :] = jnp.concatenate(
                        [own[:, offset : offset + width], other[:, offset : offset + width]], axis=1
                    )
                    offset += width
                if with_gains:
                    outs[-1][pl.ds(start, half), :] = own[:, total : total + SPARE]
    if with_gains:
        outs[-2][...] = unpack_gains(outs[-1][...])


def assemble(pieces, widths, depth, with_gains=False):
    place = lax.axis_index("dp").astype(jnp.int32)[None]
    shapes = [like((depth, 2 * width)) for width in widths]
    scratch = []
    if with_gains:
        shapes.append(like((2, depth), full))
        scratch.append(pltpu.VMEM((depth, SPARE), low))
    return call(
        functools.partial(assemble_kernel, widths, with_gains),
        "assemble",
        pieces,
        shapes,
        place=place,
        scratch=scratch,
        cost=1 << 31,
    )


def gathered_plainly(shard, widths, with_gains=False):
    own = lax.all_gather(shard, "dp", axis=0, tiled=True)
    other = y_swap(own)
    results, offset = [], 0
    for width in widths:
        lanes = slice(offset, offset + width)
        results.append(jnp.concatenate([own[:, lanes], other[:, lanes]], axis=1))
        offset += width
    if with_gains:
        results.append(unpack_gains(own[:, offset : offset + SPARE]))
    return results


def weight_grad_kernel(pairs, halves, fast, with_gains, ins, place_ref, refs):
    outs, scratch = refs[: 2 * halves], refs[2 * halves :]
    place = place_ref[0]
    sums = None
    for index, (left, right) in enumerate(pairs):
        parts = [ins[at][...] for at in right]
        right_rows = parts[0] if len(parts) == 1 else jnp.concatenate(parts, axis=1)
        grad = dot(ins[left][...], right_rows, 0, 0)
        scratch[index][...] = grad
        if with_gains:
            weight = ins[with_gains[index]][...].astype(full)
            part = jnp.sum(weight * grad, axis=1, keepdims=True)
            sums = part if sums is None else sums + part
    if with_gains:
        scratch[len(pairs)][...] = jnp.broadcast_to(sums, (sums.shape[0], 128))
    held = scratch[: len(pairs)]

    def split(rows):
        own, other = [], []
        for array in held:
            values = array[rows, :]
            width = values.shape[1] // 2
            own.append(values[:, :width])
            other.append(values[:, width:])
        if with_gains:
            column = scratch[len(pairs)][rows, :][:, :SPARE]
            own.append(column)
            other.append(column)
        return [jnp.concatenate(side, axis=1).astype(low) for side in (own, other)]

    if not fast:
        outs[0][...], outs[1][...] = split(slice(None))
        return
    size = outs[0].shape[2]
    for jx in range(2):
        for jz in range(4):
            target = (place // 2 + jz) % 4 * 2 + (place % 2 + jx) % 2
            for part in range(halves):
                start = pl.multiple_of((target * halves + part) * size, size)
                own, other = split(pl.ds(start, size))
                if fast == "y" or (fast == "both" and part == 0):
                    outs[0][jx, jz] = own
                    outs[1][jx, jz] = other
                else:
                    outs[2 * part + jx][0, jz] = own
                    outs[2 * part + jx][1, jz] = other


def weight_grad(arrays, pairs, count, order, weights=(), later=()):
    depth = arrays[pairs[0][0]].shape[1]
    widths = [sum(arrays[at].shape[1] for at in right) for _, right in pairs]
    total = sum(widths) // 2 + (SPARE if weights else 0)
    fast = order if staged(count) else None
    halves = 2 if fast == "both" else 1
    if fast:
        shapes = [like((2, 4, depth // count // halves, total))] * (2 * halves)
    else:
        shapes = [like((depth, total))] * 2
    place = lax.axis_index("dp").astype(jnp.int32)[None]
    ins = list(arrays) + list(weights)
    with_gains = tuple(range(len(arrays), len(ins)))
    held = [pltpu.VMEM((depth, width), full) for width in widths]
    if weights:
        held.append(pltpu.VMEM((depth, 128), full))

    def kernel(place_ref, *refs):
        weight_grad_kernel(
            pairs, halves, fast, with_gains, refs[: len(ins)], place_ref, refs[len(ins) :]
        )

    return call(
        kernel,
        "weight_grad",
        ins,
        shapes,
        later=later,
        place=place,
        scratch=held,
        cost=6 * depth * sum(widths) * L,
    )


def reduced_plainly(own, other):
    summed = own.astype(full) + y_swap(other).astype(full)
    return [lax.psum_scatter(summed, "dp", scatter_dimension=0, tiled=True)]


def add_kernel(*refs):
    groups = len(refs) // 4
    for at in range(groups):
        here, there = refs[2 * at : 2 * at + 2]
        stay, go = refs[2 * groups + 2 * at : 2 * groups + 2 * at + 2]
        stay[...] = (here[0].astype(full) + there[0].astype(full)).astype(low)
        go[...] = (here[1].astype(full) + there[1].astype(full)).astype(low)


def add_first(pairs, later=()):
    shapes = [like(here.shape[1:]) for here, _ in pairs for _ in range(2)]
    flat = [array for pair in pairs for array in pair]
    return call(add_kernel, "add_first", flat, shapes, later=later, cost=1 << 30)


def merge_kernel(axis, here_a, there_a, here_b, there_b, *outs):
    for step, out in enumerate(outs):
        part_a = here_a[step].astype(full) + there_a[step].astype(full)
        part_b = here_b[step].astype(full) + there_b[step].astype(full)
        out[...] = jnp.concatenate([part_a, part_b], axis=axis).astype(low)


def add_second(here_a, there_a, here_b, there_b, axis, later=()):
    _, rows, width = here_a.shape
    if axis == 0:
        shape = (2 * rows, width)
    else:
        shape = (rows, width + here_b.shape[2])
    return call(
        functools.partial(merge_kernel, axis),
        "add_second",
        [here_a, there_a, here_b, there_b],
        [like(shape)] * 4,
        later=later,
        cost=1 << 30,
    )


def across_z(parts, count):
    return [parts[0]] + [z_shift(parts[step], count, step) for step in (1, 2, 3)]


def normalized(values):
    centred = values - jnp.mean(values, axis=-1, keepdims=True)
    spread = jnp.mean(centred * centred, axis=-1, keepdims=True)
    scale = lax.rsqrt(spread + eps_norm)
    return centred * scale, scale


def norm_back(values, scales, grads):
    unit, scale = normalized(values)
    inner = grads * scales
    mean_inner = jnp.mean(inner, axis=-1, keepdims=True)
    mean_unit = jnp.mean(inner * unit, axis=-1, keepdims=True)
    return scale * (inner - mean_inner - unit * mean_unit)


def rope_tables(offset):
    half_width = HD // 2
    frequency = rope_base ** (-(jnp.arange(half_width, dtype=full) * 2.0 / HD))
    position = ((jnp.arange(L) + offset) % L).astype(full)
    angles = position[:, None] * frequency[None, :]
    cosine, sine = jnp.cos(angles), jnp.sin(angles)
    return (
        jnp.concatenate([cosine] * 4, axis=1),
        jnp.concatenate([-sine, sine, -sine, sine], axis=1),
    )


def turn(values, cosine, sine):
    lane = lax.broadcasted_iota(jnp.int32, values.shape, 1)
    ahead = pltpu.roll(values, PAIR - HD // 2, 1)
    behind = pltpu.roll(values, HD // 2, 1)
    turned = jnp.where(lane % HD < HD // 2, ahead, behind)
    return values * cosine + turned * sine


def qkv_kernel(x_own, x_other, gain, wq, wk, wv, cosine, sine, normed, q_out, k_out, v_out):
    values = jnp.where(is_own(pl.program_id(0)), x_own[...], x_other[...]).astype(full)
    unit, _ = normalized(values)
    rows = (unit * gain[...]).astype(low)
    normed[...] = rows
    query = dot(rows, wq[...], 1, 0)
    key = dot(rows, wk[...], 1, 0)
    for start in range(0, query.shape[1], PAIR):
        lanes = slice(start, start + PAIR)
        turned = turn(query[:, lanes], cosine[...], sine[...]).astype(low)
        q_out[:, lanes] = turned * jnp.asarray(HD ** (-0.5), low)
        k_out[:, lanes] = turn(key[:, lanes], cosine[...], sine[...]).astype(low)
    v_out[...] = dot(rows, wv[...], 1, 0).astype(low)


def project(x_own, x_other, gain, wq, wk, wv, cosine, sine):
    depth, width = wq.shape
    return pl.pallas_call(
        qkv_kernel,
        grid=(L // ROWS,),
        in_specs=[
            rows_of(depth, own_half),
            rows_of(depth, other_half),
            whole((1, depth)),
            whole((depth, width)),
            whole((depth, width)),
            whole((depth, width)),
            rows_of(PAIR),
            rows_of(PAIR),
        ],
        out_specs=[rows_of(depth), rows_of(width), rows_of(width), rows_of(width)],
        out_shape=[jax.ShapeDtypeStruct((L, depth), low)]
        + [jax.ShapeDtypeStruct((L, width), low)] * 3,
        compiler_params=params(),
        cost_estimate=pl.CostEstimate(
            flops=6 * L * depth * width, bytes_accessed=8 * L * depth, transcendentals=0
        ),
        name="project",
    )(x_own, x_other, gain, wq, wk, wv, cosine, sine)


def head_masks(height):
    lane = lax.broadcasted_iota(jnp.int32, (height, PAIR), 1)
    return [(lane // HD == head).astype(full).astype(low) for head in range(2)]


def attend_kernel(q_ref, k_ref, v_ref, mixed, lse_ref):
    keys, values = k_ref[...], v_ref[...]
    masks = head_masks(ROWS)
    lane = lax.broadcasted_iota(jnp.int32, (ROWS, PAIR), 1)
    for start in range(0, L, ROWS):
        rows = slice(start, start + ROWS)
        query = q_ref[rows, :]
        results = []
        for head in range(2):
            scores = dot(query * masks[head], keys, 1, 1)
            row_max = jnp.max(scores, axis=1, keepdims=True)
            raised = jnp.exp(scores - row_max)
            total = jnp.sum(raised, axis=1, keepdims=True)
            results.append(dot(raised.astype(low), values, 1, 0) / total)
            lse = jnp.broadcast_to(row_max + jnp.log(total), (ROWS, PAIR))
            lse_ref[0, head : head + 1, rows] = lse.T[0:1]
        mixed[rows, :] = jnp.where(lane < HD, results[0], results[1]).astype(low)


def attend(query, key, value):
    width = query.shape[1]
    pairs = width // PAIR
    block = pl.BlockSpec((L, PAIR), lambda i: (0, i))
    totals = pl.BlockSpec((1, 2, L), lambda i: (i, 0, 0))
    return pl.pallas_call(
        attend_kernel,
        grid=(pairs,),
        in_specs=[block] * 3,
        out_specs=[block, totals],
        out_shape=[
            jax.ShapeDtypeStruct((L, width), low),
            jax.ShapeDtypeStruct((pairs, 2, L), full),
        ],
        compiler_params=params(),
        cost_estimate=pl.CostEstimate(
            flops=16 * L * L * width, bytes_accessed=8 * L * width, transcendentals=2 * pairs * L * L
        ),
        name="attend",
    )(query, key, value)


def attend_back_kernel(
    q_ref, k_ref, v_ref, o_ref, grad_ref, lse_ref, cosine, sine, dq_out, dk_out, dv_out, dk, dv
):
    masks = head_masks(L)
    chunk_masks = head_masks(ROWS)
    keys, values = k_ref[...], v_ref[...]
    head_keys = [keys * mask for mask in masks]
    head_values = [values * mask for mask in masks]
    product = (grad_ref[...].astype(full) * o_ref[...].astype(full)).T
    inner = [jnp.sum(product[head * HD : (head + 1) * HD], axis=0, keepdims=True) for head in range(2)]
    for start in range(0, L, ROWS):
        rows = slice(start, start + ROWS)
        query, grad = q_ref[rows, :], grad_ref[rows, :]
        dq = None
        for head in range(2):
            scores = dot(head_keys[head], query, 1, 1)
            probs = jnp.exp(scores - lse_ref[0, head : head + 1, rows])
            grad_probs = dot(head_values[head], grad, 1, 1)
            grad_scores = (probs * (grad_probs - inner[head][:, rows])).astype(low)
            add_v = dot(probs.astype(low), grad * chunk_masks[head], 1, 0)
            add_k = dot(grad_scores, query * chunk_masks[head], 1, 0)
            add_q = dot(grad_scores, head_keys[head], 0, 0)
            dq = add_q if dq is None else dq + add_q
            if start == 0 and head == 0:
                dv[...] = add_v
                dk[...] = add_k
            else:
                dv[...] += add_v
                dk[...] += add_k
        dq_out[rows, :] = turn(dq * HD ** (-0.5), cosine[rows, :], -sine[rows, :]).astype(low)
    dk_out[...] = turn(dk[...], cosine[...], -sine[...]).astype(low)
    dv_out[...] = dv[...].astype(low)


def attend_back(pair, query, key, value, mixed, grad, lse, cosine, sine, later=()):
    block = pl.BlockSpec((L, PAIR), lambda i: (0, pair))
    result = pl.BlockSpec((L, PAIR), lambda i: (0, 0))
    totals = pl.BlockSpec((1, 2, L), lambda i: (pair, 0, 0))
    skip = len(later)

    def body(*refs):
        attend_back_kernel(*refs[:8], *refs[8 + skip :])

    return pl.pallas_call(
        body,
        grid=(1,),
        in_specs=[block] * 5 + [totals] + [whole((L, PAIR))] * 2 + [ANY] * skip,
        out_specs=[result] * 3,
        out_shape=[like((L, PAIR))] * 3,
        scratch_shapes=[pltpu.VMEM((L, PAIR), full)] * 2,
        compiler_params=params(),
        cost_estimate=pl.CostEstimate(
            flops=60 * L * L * PAIR, bytes_accessed=16 * L * PAIR, transcendentals=2 * L * L
        ),
        name="attend_back",
    )(query, key, value, mixed, grad, lse, cosine, sine, *later)


def feed_forward_kernel(
    mixed_own,
    mixed_other,
    x_own,
    x_other,
    dy_own,
    dy_other,
    gain,
    wo_own,
    wo_other,
    w_gate,
    w_up,
    w_down,
    resid_out,
    normed,
    hidden_out,
    dgate_out,
    dup_out,
    out_own,
    out_other,
    dnormed,
    dnormed_low,
):
    step = pl.program_id(0)
    own = is_own(step)
    tokens = jnp.where(own, x_own[...], x_other[...]).astype(full)
    pull = jnp.where(own, dy_own[...], dy_other[...])
    resid = (
        tokens + dot(mixed_own[...], wo_own[...], 1, 1) + dot(mixed_other[...], wo_other[...], 1, 1)
    )
    resid_out[...] = resid
    unit, _ = normalized(resid)
    rows = (unit * gain[...]).astype(low)
    normed[...] = rows
    gate = dot(rows, w_gate[...], 1, 0)
    up = dot(rows, w_up[...], 1, 0)
    cumulative = 0.5 + 0.5 * lax.erf(gate * np.float32(0.5**0.5))
    density = jnp.exp(gate * gate * -0.5) * np.float32((2.0 * np.pi) ** -0.5)
    activated = gate * cumulative
    hidden = (activated * up).astype(low)
    hidden_out[...] = hidden
    part = dot(hidden, w_down[...], 1, 1)

    @pl.when(own)
    def _():
        out_own[...] = resid + part

    @pl.when(jnp.logical_not(own))
    def _():
        out_other[...] = part.astype(low)

    dhidden = dot(pull, w_down[...], 1, 0)
    dgate = (dhidden * up * (cumulative + gate * density)).astype(low)
    dup = (dhidden * activated).astype(low)
    dgate_out[...] = dgate
    dup_out[...] = dup
    grad = dot(dgate, w_gate[...], 1, 1) + dot(dup, w_up[...], 1, 1)
    dnormed[...] = grad
    dnormed_low[...] = grad.astype(low)


def feed_forward(
    mixed, mixed_other, x_own, x_other, dy_own, dy_other, gain, wo, wo_other, w_gate, w_up, w_down
):
    depth, width = wo.shape
    units = w_gate.shape[1]
    half = L // 2
    return pl.pallas_call(
        feed_forward_kernel,
        grid=(L // ROWS,),
        in_specs=[
            rows_of(width),
            rows_of(width, swapped),
            rows_of(depth, own_half),
            rows_of(depth, other_half),
            rows_of(depth, own_half),
            rows_of(depth, other_half),
            whole((1, depth)),
            whole((depth, width)),
            whole((depth, width)),
            whole((depth, units)),
            whole((depth, units)),
            whole((depth, units)),
        ],
        out_specs=[
            rows_of(depth),
            rows_of(depth),
            rows_of(units),
            rows_of(units),
            rows_of(units),
            rows_of(depth, own_half),
            rows_of(depth, other_half),
            rows_of(depth),
            rows_of(depth),
        ],
        out_shape=[
            jax.ShapeDtypeStruct((L, depth), full),
            jax.ShapeDtypeStruct((L, depth), low),
            jax.ShapeDtypeStruct((L, units), low),
            jax.ShapeDtypeStruct((L, units), low),
            jax.ShapeDtypeStruct((L, units), low),
            jax.ShapeDtypeStruct((half, depth), full),
            jax.ShapeDtypeStruct((half, depth), low),
            jax.ShapeDtypeStruct((L, depth), full),
            jax.ShapeDtypeStruct((L, depth), low),
        ],
        compiler_params=params(),
        cost_estimate=pl.CostEstimate(
            flops=2 * L * depth * (2 * width + 6 * units),
            bytes_accessed=24 * L * depth,
            transcendentals=2 * L * units,
        ),
        name="feed_forward",
    )(mixed, mixed_other, x_own, x_other, dy_own, dy_other, gain, wo, wo_other, w_gate, w_up, w_down)


def resid_back_kernel(
    resid, grad_own, grad_other, dy_own, dy_other, gain, wo, dresid, dresid_low, dmixed
):
    own = is_own(pl.program_id(0))
    pull = jnp.where(own, dy_own[...], dy_other[...]).astype(full)
    grads = grad_own[...] + grad_other[...].astype(full)
    total = pull + norm_back(resid[...], gain[...], grads)
    rounded = total.astype(low)
    dresid_low[...] = rounded
    dmixed[...] = dot(rounded, wo[...], 1, 0).astype(low)

    @pl.when(own)
    def _():
        dresid[...] = total


def resid_back(resid, grad_own, grad_other, dy_own, dy_other, gain, wo):
    depth, width = wo.shape
    return pl.pallas_call(
        resid_back_kernel,
        grid=(L // ROWS,),
        in_specs=[
            rows_of(depth),
            rows_of(depth),
            rows_of(depth, swapped),
            rows_of(depth, own_half),
            rows_of(depth, other_half),
            whole((1, depth)),
            whole((depth, width)),
        ],
        out_specs=[rows_of(depth, own_half), rows_of(depth), rows_of(width)],
        out_shape=[
            jax.ShapeDtypeStruct((L // 2, depth), full),
            jax.ShapeDtypeStruct((L, depth), low),
            jax.ShapeDtypeStruct((L, width), low),
        ],
        compiler_params=params(),
        cost_estimate=pl.CostEstimate(
            flops=2 * L * depth * width, bytes_accessed=16 * L * depth, transcendentals=0
        ),
        name="resid_back",
    )(resid, grad_own, grad_other, dy_own, dy_other, gain, wo)


def project_back_kernel(*refs):
    grads, weights, (grad_own, grad_other) = refs[:9], refs[9:12], refs[12:14]
    grad = None
    for part in range(3):
        rows = jnp.concatenate([ref[...] for ref in grads[3 * part : 3 * part + 3]], axis=1)
        term = dot(rows, weights[part][...], 1, 1)
        grad = term if grad is None else grad + term
    own = is_own(pl.program_id(0))

    @pl.when(own)
    def _():
        grad_own[...] = grad

    @pl.when(jnp.logical_not(own))
    def _():
        grad_other[...] = grad.astype(low)


def project_back(grads, wq, wk, wv, later=()):
    depth, width = wq.shape
    skip = len(later)

    def body(*refs):
        project_back_kernel(*refs[:12], *refs[12 + skip :])

    return pl.pallas_call(
        body,
        grid=(L // ROWS,),
        in_specs=[rows_of(PAIR)] * 9 + [whole((depth, width))] * 3 + [ANY] * skip,
        out_specs=[rows_of(depth, own_half), rows_of(depth, other_half)],
        out_shape=[like((L // 2, depth), full), like((L // 2, depth))],
        compiler_params=params(),
        cost_estimate=pl.CostEstimate(
            flops=18 * L * depth * width, bytes_accessed=8 * L * depth, transcendentals=0
        ),
        name="project_back",
    )(*grads, wq, wk, wv, *later)


def input_back_kernel(tokens, grad_own, grad_other, dresid, gain, result):
    grads = grad_own[...] + grad_other[...].astype(full)
    result[...] = dresid[...] + norm_back(tokens[...].astype(full), gain[...], grads)


def input_back(tokens, grad_own, grad_other, dresid, gain):
    height, depth = tokens.shape
    return pl.pallas_call(
        input_back_kernel,
        grid=(height // ROWS,),
        in_specs=[rows_of(depth)] * 4 + [whole((1, depth))],
        out_specs=rows_of(depth),
        out_shape=like((height, depth), full),
        compiler_params=params(),
        cost_estimate=pl.CostEstimate(
            flops=20 * height * depth, bytes_accessed=16 * height * depth, transcendentals=0
        ),
        name="input_back",
    )(tokens, grad_own, grad_other, dresid, gain)


def adamw(weight, grad, first, second, rate, decay):
    first_new = beta_one * first + (1.0 - beta_one) * grad
    second_new = beta_two * second + (1.0 - beta_two) * grad * grad
    step_size = (
        first_new
        / (1.0 - beta_one**STEP)
        / (jnp.sqrt(second_new / (1.0 - beta_two**STEP)) + adam_eps)
    )
    return (weight - rate * (step_size + decay * weight), first_new, second_new)


def step_kernel(parts, flipped, spans, *refs):
    pieces, rest = refs[:parts], refs[parts:]
    count = len(spans)
    states, outs = rest[: 3 * count], rest[3 * count : 7 * count]
    scratch = rest[7 * count :]
    total = pieces[0][...].astype(full)
    for piece in pieces[1:]:
        total = total + piece[...].astype(full)
    rows = total.shape[0]
    for at, span in enumerate(spans):
        weight, first, second = states[3 * at : 3 * at + 3]
        grad_out, weight_out, first_out, second_out = outs[4 * at : 4 * at + 4]
        for part, (start, width) in enumerate(span):
            grad = total[:, start : start + width]
            if flipped[at]:
                padded = scratch[at]
                padded[...] = jnp.zeros_like(padded)
                padded[0:rows, 0:width] = grad
                grad = padded[...].T[0:width, 0:rows]
                where = Ellipsis
            else:
                where = part
            new = adamw(
                weight[where], grad, first[where], second[where], weight_rate, weight_decay
            )
            grad_out[where] = grad
            weight_out[where], first_out[where], second_out[where] = new


def step(pieces, spans, states, flipped, later=()):
    shapes, scratch = [], []
    for (weight, _, _), span, flip in zip(states, spans, flipped):
        shapes += [like(weight.shape, full)] * 4
        lanes = -(-span[0][1] // 128) * 128
        scratch.append(pltpu.VMEM((128, lanes) if flip else (8, 128), full))
    flat = [array for state in states for array in state]
    results = call(
        functools.partial(step_kernel, len(pieces), flipped, spans),
        "step",
        list(pieces) + flat,
        shapes,
        later=later,
        scratch=scratch,
        cost=1 << 30,
    )
    return [results[4 * at : 4 * at + 4] for at in range(len(states))]


def column(pieces, at):
    return sum(piece[:, at : at + 1].astype(full) for piece in pieces)


def shards(
    tokens,
    cotangent,
    w_qkv,
    w_attn_out,
    w_in,
    w_mlp_out,
    gains,
    first_qkv,
    first_attn_out,
    first_in,
    first_mlp_out,
    first_gains,
    second_qkv,
    second_attn_out,
    second_in,
    second_mlp_out,
    second_gains,
):
    count = lax.axis_size("dp")
    fast = staged(count)
    core = lax.axis_index("tensor") % 2
    head_width = w_qkv.shape[2]
    unit_width = w_in.shape[2]
    depth = tokens.shape[1]
    qkv_widths = [head_width] * 3
    rest_widths = [head_width, unit_width, unit_width, unit_width]

    shard_one = pack(w_qkv, gains)
    shard_two = jnp.concatenate(
        [
            w_attn_out.astype(low).T,
            w_in[0].astype(low),
            w_in[1].astype(low),
            w_mlp_out.astype(low).T,
        ],
        axis=1,
    )
    cosine, sine = rope_tables(core * (L // 2))

    def halves(shard, along):
        half = shard.shape[0] // 2
        pieces = [shard] + along
        return jnp.stack([p[:half] for p in pieces]), jnp.stack([p[half:] for p in pieces])

    if fast:
        along_one = [z_shift(shard_one, count, jump) for jump in (1, 2, 3)]
        za, zb = halves(shard_one, along_one)
        x_other = core_swap(after(tokens, *along_one))
        shard_two = after(shard_two, *along_one)
        along_two = [z_shift(shard_two, count, jump) for jump in (1, 2, 3)]
        xa, yb = x_swap(za, count), y_swap(zb)
        ya, xb = y_swap(jnp.stack([za, xa])), x_swap(jnp.stack([zb, yb]), count)
        wq, wk, wv, gains_all = assemble([za, xa, ya, zb, yb, xb], qkv_widths, depth, True)
    else:
        x_other = core_swap(tokens)
        wq, wk, wv, gains_all = gathered_plainly(shard_one, qkv_widths, True)
    gain_one, gain_two = gains_all[0:1], gains_all[1:2]
    normed_one, query, key, value = project(
        tokens, x_other, gain_one, wq, wk, wv, cosine, sine
    )
    if fast:
        za, zb = halves(shard_two, [after(piece, ya, xb) for piece in along_two])
        xa, yb = after(x_swap(za, count), query), after(y_swap(zb), query)
        ya, xb = y_swap(jnp.stack([za, xa])), x_swap(jnp.stack([zb, yb]), count)
    dy_other = core_swap(after(cotangent, query))
    mixed, lse = attend(query, key, value)
    mixed_other = core_swap(mixed)
    if fast:
        ya, xb = after(ya, mixed), after(xb, mixed)
        wo, w_gate, w_up, w_down = assemble([za, xa, ya, zb, yb, xb], rest_widths, depth)
    else:
        wo, w_gate, w_up, w_down = gathered_plainly(shard_two, rest_widths)
    wo_other = core_swap(wo)
    dy_rows = jnp.concatenate([cotangent, dy_other])
    resid, normed_two, hidden, dgate, dup, out_own, out_other, dnormed, dnormed_low = feed_forward(
        mixed,
        mixed_other,
        tokens,
        x_other,
        cotangent,
        dy_other,
        gain_two,
        wo,
        wo_other,
        w_gate,
        w_up,
        w_down,
    )
    dnormed_other = core_swap(dnormed_low)
    grad_a = weight_grad(
        [normed_two, dgate, dup], [(0, (1,)), (0, (2,))], count, "y", [w_gate, w_up]
    )
    if fast:
        from_a = y_swap(grad_a[1])
    dnormed_other = after(dnormed_other, *grad_a)
    dresid, dresid_low, dmixed = resid_back(
        resid, dnormed, dnormed_other, cotangent, dy_other, gain_two, wo
    )
    grad_b = weight_grad(
        [dy_rows, hidden, dresid_low, mixed], [(0, (1,)), (2, (3,))], count, "x", later=[dmixed]
    )
    if fast:
        from_b = x_swap(grad_b[1], count)
    bundle = (query, key, value, mixed, dmixed, lse, cosine, sine)
    pair_0 = attend_back(0, *bundle, later=grad_b[:1])
    if fast:
        stay_a, go_a = add_first([(grad_a[0], from_a)], later=pair_0[:1])
        next_a = x_swap(go_a, count)
        pair_1 = attend_back(1, *bundle, later=[go_a])
        stay_b, go_b = add_first([(grad_b[0], from_b)], later=pair_1[:1])
        next_b = y_swap(go_b)
        pair_2 = attend_back(2, *bundle, later=[go_b])
    else:
        pair_1, pair_2 = attend_back(1, *bundle), attend_back(2, *bundle)
    trios = [group[part] for part in range(3) for group in (pair_0, pair_1, pair_2)]
    grad_c = weight_grad(
        [normed_one, *trios],
        [(0, (1, 2, 3)), (0, (4, 5, 6)), (0, (7, 8, 9))],
        count,
        "both",
        [wq, wk, wv],
    )
    if fast:
        from_y, from_x = y_swap(grad_c[1]), x_swap(grad_c[3], count)
        merged = add_second(stay_a, next_a, stay_b, next_b, 1, later=grad_c[:1])
        pieces_one = across_z(merged, count)
    else:
        first_sum = reduced_plainly(*grad_a)[0]
        pieces_one = [jnp.concatenate([first_sum, reduced_plainly(*grad_b)[0]], axis=1)]
    grad_one, grad_one_low = project_back(trios, wq, wk, wv, later=grad_c[:1])
    if fast:
        from_y, from_x = after(from_y, grad_one), after(from_x, grad_one)
        stay_a, go_a, stay_b, go_b = add_first([(grad_c[0], from_y), (grad_c[2], from_x)])
        next_a, next_b = x_swap(go_a, count), y_swap(go_b)
    grad_other = core_swap(grad_one_low)
    output = (out_own + core_swap(out_other).astype(full)).astype(low)
    grad_inputs = input_back(tokens, grad_one, grad_other, dresid, gain_one)
    if fast:
        next_a, next_b = after(next_a, grad_inputs, output), after(next_b, grad_inputs, output)
        merged = add_second(stay_a, next_a, stay_b, next_b, 0)
        pieces_two = across_z(merged, count)
    else:
        pieces_two = reduced_plainly(*grad_c)
    base = 2 * unit_width + SPARE
    new_in, new_attn, new_down = step(
        pieces_one,
        [
            [(0, unit_width), (unit_width, unit_width)],
            [(base + unit_width, head_width)],
            [(base, unit_width)],
        ],
        [
            (w_in, first_in, second_in),
            (w_attn_out, first_attn_out, second_attn_out),
            (w_mlp_out, first_mlp_out, second_mlp_out),
        ],
        (False, True, True),
        later=merged[:1] if fast else (),
    )
    if fast:
        pieces_two = [after(piece, new_in[0]) for piece in pieces_two]
    sums = jnp.concatenate([column(pieces_two, 3 * head_width), column(pieces_one, 2 * unit_width)], 1)
    shard_gain = (sums + core_swap(sums)).T / gains
    (new_qkv,) = step(
        pieces_two,
        [[(part * head_width, head_width) for part in range(3)]],
        [(w_qkv, first_qkv, second_qkv)],
        (False,),
    )
    new_gain = adamw(gains, shard_gain, first_gains, second_gains, gain_rate, 0.0)
    return (
        output,
        grad_inputs,
        new_qkv[0],
        new_attn[0],
        new_in[0],
        new_down[0],
        shard_gain,
        new_qkv[1],
        new_attn[1],
        new_in[1],
        new_down[1],
        new_gain[0],
        new_qkv[2],
        new_attn[2],
        new_in[2],
        new_down[2],
        new_gain[1],
        new_qkv[3],
        new_attn[3],
        new_in[3],
        new_down[3],
        new_gain[2],
    )


def solution(mesh):
    return jax.shard_map(
        shards,
        mesh=mesh,
        in_specs=(
            P(("dp", "tensor"), None),
            P(("dp", "tensor"), None),
            P(None, "dp", "tensor"),
            P("tensor", "dp"),
            P(None, "dp", "tensor"),
            P("tensor", "dp"),
            P(None, "dp"),
            P(None, "dp", "tensor"),
            P("tensor", "dp"),
            P(None, "dp", "tensor"),
            P("tensor", "dp"),
            P(None, "dp"),
            P(None, "dp", "tensor"),
            P("tensor", "dp"),
            P(None, "dp", "tensor"),
            P("tensor", "dp"),
            P(None, "dp"),
        ),
        out_specs=(
            P(("dp", "tensor"), None),
            P(("dp", "tensor"), None),
            P(None, "dp", "tensor"),
            P("tensor", "dp"),
            P(None, "dp", "tensor"),
            P("tensor", "dp"),
            P(None, "dp"),
            P(None, "dp", "tensor"),
            P("tensor", "dp"),
            P(None, "dp", "tensor"),
            P("tensor", "dp"),
            P(None, "dp"),
            P(None, "dp", "tensor"),
            P("tensor", "dp"),
            P(None, "dp", "tensor"),
            P("tensor", "dp"),
            P(None, "dp"),
            P(None, "dp", "tensor"),
            P("tensor", "dp"),
            P(None, "dp", "tensor"),
            P("tensor", "dp"),
            P(None, "dp"),
        ),
        check_vma=False,
    )
```

```python
import functools

import jax
import jax.numpy as jnp
import numpy as np
from jax import lax
from jax.experimental import pallas as pl
from jax.experimental.pallas import tpu as pltpu
from jax.sharding import PartitionSpec as P

HD = 64
L = 1024
STEP = 10


eps_norm = 1e-05
rope_base = 160000.0
beta_one = 0.9
beta_two = 0.98
adam_eps = 1e-06
weight_rate = 0.02
gain_rate = 0.2
weight_decay = 0.01

low = jnp.bfloat16
full = jnp.float32
ROWS = 256
PAIR = 2 * HD
VMEM_BYTES = 52 << 20
SPARE = 64
STRIP = 16
SHORT = pl.CostEstimate(flops=0, bytes_accessed=0, transcendentals=0)


def dot(left, right, left_dim, right_dim):
    return lax.dot_general(
        left, right, (((left_dim,), (right_dim,)), ((), ())), preferred_element_type=full
    )


def params():
    return pltpu.CompilerParams(vmem_limit_bytes=VMEM_BYTES)


def whole(shape):
    return pl.BlockSpec(shape, lambda *_: (0,) * len(shape))


def rows_of(width, index=lambda i: i):
    return pl.BlockSpec((ROWS, width), lambda i: (index(i), 0))


def own_half(i):
    return jnp.minimum(i, L // ROWS // 2 - 1)


def other_half(i):
    return jnp.maximum(i - L // ROWS // 2, 0)


def swapped(i):
    return (i + L // ROWS // 2) % (L // ROWS)


def is_own(i):
    return i < L // ROWS // 2


def core_swap(array):
    return lax.ppermute(array, "tensor", [(t, t ^ 1) for t in range(4)])


def y_swap(array):
    return lax.ppermute(array, "tensor", [(t, t ^ 2) for t in range(4)])


def x_swap(array, count):
    return lax.ppermute(array, "dp", [(d, d ^ 1) for d in range(count)])


def z_shift(array, count, step):
    around = count // 2
    return lax.ppermute(
        array, "dp", [(d, (d // 2 + step) % around * 2 + d % 2) for d in range(count)]
    )


def staged(count):
    return count == 8


def after(array, *others):
    return lax.optimization_barrier((array, *others))[0]


ANY = pl.BlockSpec(memory_space=pl.ANY)
LOCAL = pl.BlockSpec(memory_space=pltpu.VMEM)
SCALAR = pl.BlockSpec(memory_space=pltpu.SMEM)


def call(kernel, name, ins, shapes, later=(), place=None, scratch=()):
    head = [] if place is None else [place]
    lead, skip = len(head), len(later)

    def body(*refs):
        kernel(*refs[: lead + len(ins)], *refs[lead + len(ins) + skip :])

    return pl.pallas_call(
        body,
        in_specs=[SCALAR] * lead + [LOCAL] * len(ins) + [ANY] * skip,
        out_specs=[LOCAL] * len(shapes),
        out_shape=shapes,
        scratch_shapes=list(scratch),
        compiler_params=params(),
        cost_estimate=SHORT,
        name=name,
    )(*head, *ins, *later)


def like(shape, kind=low):
    return jax.ShapeDtypeStruct(shape, kind)


def pack_kernel(w_qkv, gains, shard, padded):
    rows = w_qkv.shape[1]
    padded[...] = jnp.zeros_like(padded)
    padded[0 : gains.shape[0], 0:rows] = gains[...]
    columns = padded[...].T[0:rows, 0:2]
    high = columns.astype(low)
    rest = columns - high.astype(full)
    middle = rest.astype(low)
    last = (rest - middle.astype(full)).astype(low)
    filler = jnp.zeros((rows, SPARE - 6), full)
    pieces = [w_qkv[part] for part in range(3)]
    shard[...] = jnp.concatenate(
        pieces + [high.astype(full), middle.astype(full), last.astype(full), filler], axis=1
    ).astype(low)


def pack(w_qkv, gains):
    rows, width = w_qkv.shape[1:]
    return call(
        pack_kernel,
        "pack",
        [w_qkv, gains],
        [like((rows, 3 * width + SPARE))],
        scratch=[pltpu.VMEM((128, 128), full)],
    )[0]


def pack_rest_kernel(w_attn_out, w_in, w_mlp_out, shard, wide):
    rows = w_in.shape[1]
    flipped = []
    for weight in (w_attn_out, w_mlp_out):
        wide[...] = jnp.zeros_like(wide)
        wide[0 : weight.shape[0], 0:rows] = weight[...]
        flipped.append(wide[...].T[0:rows, 0 : weight.shape[0]])
    pieces = [flipped[0], w_in[0], w_in[1], flipped[1]]
    shard[...] = jnp.concatenate(pieces, axis=1).astype(low)


def pack_rest(w_attn_out, w_in, w_mlp_out, later):
    rows, units = w_in.shape[1:]
    heads = w_attn_out.shape[0]
    return call(
        pack_rest_kernel,
        "pack_rest",
        [w_attn_out, w_in, w_mlp_out],
        [like((rows, heads + 3 * units))],
        later=later,
        scratch=[pltpu.VMEM((-(-units // 128) * 128, 128), full)],
    )[0]


def unpack_gains(columns):
    wide = jnp.concatenate([columns.astype(full), jnp.zeros(columns.shape, full)], axis=1).T
    return wide[0:2] + wide[2:4] + wide[4:6]


def columns_of(layout, own, other):
    pieces = []
    for item in layout:
        if item is None:
            pieces.append(jnp.zeros((own.shape[0], SPARE), own.dtype))
        else:
            lanes = slice(item[0], item[0] + item[1])
            pieces += [own[:, lanes], other[:, lanes]]
    return jnp.concatenate(pieces, axis=1)


def layout_width(layout):
    return sum(SPARE if item is None else 2 * item[1] for item in layout)


def assemble_kernel(layouts, gains_at, place_ref, za, xa, ya, zb, yb, xb, *outs):
    place = place_ref[0]
    half = za.shape[1]
    for jx in range(2):
        for jz in range(4):
            source = (place // 2 + 4 - jz) % 4 * 2 + (place % 2 + jx) % 2
            own_a = (za, xa)[jx][jz]
            other_a = ya[jx, jz]
            own_b = zb[jz] if jx == 0 else xb[0, jz]
            other_b = yb[jz] if jx == 0 else xb[1, jz]
            for part, (own, other) in enumerate(((own_a, other_a), (own_b, other_b))):
                start = pl.multiple_of(source * 2 * half + part * half, half)
                for layout, out in zip(layouts, outs):
                    out[pl.ds(start, half), :] = columns_of(layout, own, other)
                if gains_at is not None:
                    outs[-1][pl.ds(start, half), :] = own[:, gains_at : gains_at + SPARE]
    if gains_at is not None:
        outs[-2][...] = unpack_gains(outs[-1][...])


def assemble(pieces, layouts, depth, gains_at=None, later=()):
    place = lax.axis_index("dp").astype(jnp.int32)[None]
    shapes = [like((depth, layout_width(layout))) for layout in layouts]
    scratch = []
    if gains_at is not None:
        shapes.append(like((2, depth), full))
        scratch.append(pltpu.VMEM((depth, SPARE), low))
    return call(
        functools.partial(assemble_kernel, layouts, gains_at),
        "assemble",
        pieces,
        shapes,
        later=later,
        place=place,
        scratch=scratch,
    )


def gathered_plainly(shard, layouts, gains_at=None):
    own = lax.all_gather(shard, "dp", axis=0, tiled=True)
    other = y_swap(own)
    results = [columns_of(layout, own, other) for layout in layouts]
    if gains_at is not None:
        results.append(unpack_gains(own[:, gains_at : gains_at + SPARE]))
    return results


def stacked(ins, at, axis):
    parts = [ins[index][...] for index in at]
    return parts[0] if len(parts) == 1 else jnp.concatenate(parts, axis=axis)


def weight_grad_kernel(products, halves, fast, weights, ins, place_ref, refs):
    outs, scratch = refs[: 2 * halves], refs[2 * halves :]
    place = place_ref[0]
    for held, (left, right, _) in zip(scratch, products):
        grad = dot(stacked(ins, left, 0), stacked(ins, right, 1), 0, 0)
        held[...] = grad
        if weights:
            sums = jnp.sum(ins[weights[0]][...].astype(full) * grad, axis=1, keepdims=True)
            scratch[-1][...] = jnp.broadcast_to(sums, (sums.shape[0], 128))

    def split(rows):
        sides = [[], []]
        for held, (_, _, spans) in zip(scratch, products):
            values = held[rows, :]
            for start, width in spans:
                sides[0].append(values[:, start : start + width])
                sides[1].append(values[:, start + width : start + 2 * width])
        if weights:
            for side in sides:
                side.append(scratch[-1][rows, :][:, :SPARE])
        return [jnp.concatenate(side, axis=1).astype(low) for side in sides]

    if not fast:
        outs[0][...], outs[1][...] = split(slice(None))
        return
    size = outs[0].shape[2]
    for jx in range(2):
        for jz in range(4):
            target = (place // 2 + jz) % 4 * 2 + (place % 2 + jx) % 2
            for part in range(halves):
                start = pl.multiple_of((target * halves + part) * size, size)
                own, other = split(pl.ds(start, size))
                if fast == "y" or (fast == "both" and part == 0):
                    outs[0][jx, jz] = own
                    outs[1][jx, jz] = other
                else:
                    outs[2 * part + jx][0, jz] = own
                    outs[2 * part + jx][1, jz] = other


def weight_grad(arrays, products, count, order, weight=None, later=()):
    depth = arrays[products[0][0][0]].shape[1]
    widths = [sum(arrays[at].shape[1] for at in right) for _, right, _ in products]
    total = sum(width for _, _, spans in products for _, width in spans)
    total += SPARE if weight is not None else 0
    fast = order if staged(count) else None
    halves = 2 if fast == "both" else 1
    if fast:
        shapes = [like((2, 4, depth // count // halves, total))] * (2 * halves)
    else:
        shapes = [like((depth, total))] * 2
    place = lax.axis_index("dp").astype(jnp.int32)[None]
    ins = list(arrays) + ([] if weight is None else [weight])
    weights = [] if weight is None else [len(arrays)]
    held = [pltpu.VMEM((depth, width), full) for width in widths]
    if weights:
        held.append(pltpu.VMEM((depth, 128), full))

    def kernel(place_ref, *refs):
        weight_grad_kernel(
            products, halves, fast, weights, refs[: len(ins)], place_ref, refs[len(ins) :]
        )

    return call(
        kernel,
        "weight_grad",
        ins,
        shapes,
        later=later,
        place=place,
        scratch=held,
    )


def reduced_plainly(own, other):
    summed = own.astype(full) + y_swap(other).astype(full)
    return [lax.psum_scatter(summed, "dp", scatter_dimension=0, tiled=True)]


def add_kernel(*refs):
    groups = len(refs) // 4
    for at in range(groups):
        here, there = refs[2 * at : 2 * at + 2]
        stay, go = refs[2 * groups + 2 * at : 2 * groups + 2 * at + 2]
        stay[...] = (here[0].astype(full) + there[0].astype(full)).astype(low)
        go[...] = (here[1].astype(full) + there[1].astype(full)).astype(low)


def add_first(pairs, later=()):
    shapes = [like(here.shape[1:]) for here, _ in pairs for _ in range(2)]
    flat = [array for pair in pairs for array in pair]
    return call(add_kernel, "add_first", flat, shapes, later=later)


def merge_kernel(pairs, *refs):
    ins, outs = refs[: 2 * pairs], refs[2 * pairs :]
    for jump, out in enumerate(outs):
        parts = [
            (ins[2 * at][jump].astype(full) + ins[2 * at + 1][jump].astype(full)).astype(low)
            for at in range(pairs)
        ]
        out[...] = parts[0] if pairs == 1 else jnp.concatenate(parts, axis=0)


def add_second(pairs, later=()):
    _, rows, width = pairs[0][0].shape
    return call(
        functools.partial(merge_kernel, len(pairs)),
        "add_second",
        [array for pair in pairs for array in pair],
        [like((len(pairs) * rows, width))] * 4,
        later=later,
    )


def across_z(parts, count):
    return [parts[0]] + [z_shift(parts[step], count, step) for step in (1, 2, 3)]


def normalized(values):
    centred = values - jnp.mean(values, axis=-1, keepdims=True)
    spread = jnp.mean(centred * centred, axis=-1, keepdims=True)
    scale = lax.rsqrt(spread + eps_norm)
    return centred * scale, scale


def norm_back(unit, scale, gains, grads):
    inner = grads * gains
    mean_inner = jnp.mean(inner, axis=-1, keepdims=True)
    mean_unit = jnp.mean(inner * unit, axis=-1, keepdims=True)
    return scale * (inner - mean_inner - unit * mean_unit)


def rope_tables(offset):
    half_width = HD // 2
    frequency = rope_base ** (-(jnp.arange(half_width, dtype=full) * 2.0 / HD))
    position = ((jnp.arange(L) + offset) % L).astype(full)
    angles = position[:, None] * frequency[None, :]
    cosine, sine = jnp.cos(angles), jnp.sin(angles)
    return (
        jnp.concatenate([cosine] * 4, axis=1),
        jnp.concatenate([-sine, sine, -sine, sine], axis=1),
    )


def turn(values, cosine, sine):
    lane = lax.broadcasted_iota(jnp.int32, values.shape, 1)
    ahead = pltpu.roll(values, PAIR - HD // 2, 1)
    behind = pltpu.roll(values, HD // 2, 1)
    turned = jnp.where(lane % HD < HD // 2, ahead, behind)
    return values * cosine + turned * sine


def strips(height=ROWS, size=STRIP):
    return [slice(start, start + size) for start in range(0, height, size)]


def qkv_kernel(x_own, x_other, gain, weight, cosine, sine, normed, q_out, k_out, v_out, raw):
    own = is_own(pl.program_id(0))
    for rows in strips():
        values = jnp.where(own, x_own[rows, :], x_other[rows, :]).astype(full)
        unit, _ = normalized(values)
        normed[rows, :] = (unit * gain[...]).astype(low)
    raw[...] = dot(normed[...], weight[...], 1, 0)
    width = q_out.shape[1]
    for rows in strips(ROWS, 64):
        near, far = cosine[rows, :], sine[rows, :]
        for start in range(0, width, PAIR):
            lanes = slice(start, start + PAIR)
            query = turn(raw[rows, lanes], near, far).astype(low)
            q_out[rows, lanes] = query * jnp.asarray(HD ** (-0.5), low)
            key = raw[rows, width + start : width + start + PAIR]
            k_out[rows, lanes] = turn(key, near, far).astype(low)
    v_out[...] = raw[:, 2 * width :].astype(low)


def project(x_own, x_other, gain, weight, cosine, sine):
    depth, total = weight.shape
    width = total // 3
    return pl.pallas_call(
        qkv_kernel,
        grid=(L // ROWS,),
        in_specs=[
            rows_of(depth, own_half),
            rows_of(depth, other_half),
            whole((1, depth)),
            whole((depth, total)),
            rows_of(PAIR),
            rows_of(PAIR),
        ],
        out_specs=[rows_of(depth), rows_of(width), rows_of(width), rows_of(width)],
        out_shape=[like((L, depth))] + [like((L, width))] * 3,
        scratch_shapes=[pltpu.VMEM((ROWS, total), full)],
        compiler_params=params(),
        cost_estimate=SHORT,
        name="project",
    )(x_own, x_other, gain, weight, cosine, sine)


def head_masks(height):
    lane = lax.broadcasted_iota(jnp.int32, (height, PAIR), 1)
    return [(lane // HD == head).astype(full).astype(low) for head in range(2)]


def attend_kernel(q_ref, k_ref, v_ref, mixed, lse_ref):
    keys, values = k_ref[...], v_ref[...]
    masks = head_masks(ROWS)
    lane = lax.broadcasted_iota(jnp.int32, (ROWS, PAIR), 1)
    for start in range(0, L, ROWS):
        rows = slice(start, start + ROWS)
        query = q_ref[rows, :]
        results = []
        for head in range(2):
            scores = dot(query * masks[head], keys, 1, 1)
            row_max = jnp.max(scores, axis=1, keepdims=True)
            raised = jnp.exp(scores - row_max)
            total = jnp.sum(raised, axis=1, keepdims=True)
            results.append(dot(raised.astype(low), values, 1, 0) / total)
            lse = jnp.broadcast_to(row_max + jnp.log(total), (ROWS, PAIR))
            lse_ref[0, head : head + 1, rows] = lse.T[0:1]
        mixed[rows, :] = jnp.where(lane < HD, results[0], results[1]).astype(low)


def attend(query, key, value):
    width = query.shape[1]
    pairs = width // PAIR
    block = pl.BlockSpec((L, PAIR), lambda i: (0, i))
    totals = pl.BlockSpec((1, 2, L), lambda i: (i, 0, 0))
    return pl.pallas_call(
        attend_kernel,
        grid=(pairs,),
        in_specs=[block] * 3,
        out_specs=[block, totals],
        out_shape=[
            jax.ShapeDtypeStruct((L, width), low),
            jax.ShapeDtypeStruct((pairs, 2, L), full),
        ],
        compiler_params=params(),
        cost_estimate=SHORT,
        name="attend",
    )(query, key, value)


def attend_back_kernel(
    q_ref, k_ref, v_ref, o_ref, grad_ref, lse_ref, cosine, sine, dq_out, dk_out, dv_out, dk, dv
):
    masks = head_masks(L)
    chunk_masks = head_masks(ROWS)
    keys, values = k_ref[...], v_ref[...]
    head_keys = [keys * mask for mask in masks]
    head_values = [values * mask for mask in masks]
    flipped_keys = keys.astype(full).T
    half_rows = lax.broadcasted_iota(jnp.int32, flipped_keys.shape, 0) // HD
    flipped_keys = [jnp.where(half_rows == head, flipped_keys, 0.0).astype(low) for head in range(2)]
    product = (grad_ref[...].astype(full) * o_ref[...].astype(full)).T
    inner = [jnp.sum(product[head * HD : (head + 1) * HD], axis=0, keepdims=True) for head in range(2)]
    for start in range(0, L, ROWS):
        rows = slice(start, start + ROWS)
        query, grad = q_ref[rows, :], grad_ref[rows, :]
        dq = None
        for head in range(2):
            scores = dot(head_keys[head], query, 1, 1)
            probs = jnp.exp(scores - lse_ref[0, head : head + 1, rows])
            grad_probs = dot(head_values[head], grad, 1, 1)
            grad_scores = (probs * (grad_probs - inner[head][:, rows])).astype(low)
            add_v = dot(probs.astype(low), grad * chunk_masks[head], 1, 0)
            add_k = dot(grad_scores, query * chunk_masks[head], 1, 0)
            add_q = dot(flipped_keys[head], grad_scores, 1, 0)
            dq = add_q if dq is None else dq + add_q
            if start == 0 and head == 0:
                dv[...] = add_v
                dk[...] = add_k
            else:
                dv[...] += add_v
                dk[...] += add_k
        dq_out[rows, :] = turn(dq.T * HD ** (-0.5), cosine[rows, :], -sine[rows, :]).astype(low)
    dk_out[...] = turn(dk[...], cosine[...], -sine[...]).astype(low)
    dv_out[...] = dv[...].astype(low)


def attend_back(pair, query, key, value, mixed, grad, lse, cosine, sine, later=()):
    block = pl.BlockSpec((L, PAIR), lambda i: (0, pair))
    result = pl.BlockSpec((L, PAIR), lambda i: (0, 0))
    totals = pl.BlockSpec((1, 2, L), lambda i: (pair, 0, 0))
    skip = len(later)

    def body(*refs):
        attend_back_kernel(*refs[:8], *refs[8 + skip :])

    return pl.pallas_call(
        body,
        grid=(1,),
        in_specs=[block] * 5 + [totals] + [whole((L, PAIR))] * 2 + [ANY] * skip,
        out_specs=[result] * 3,
        out_shape=[like((L, PAIR))] * 3,
        scratch_shapes=[pltpu.VMEM((L, PAIR), full)] * 2,
        compiler_params=params(),
        cost_estimate=SHORT,
        name="attend_back",
    )(query, key, value, mixed, grad, lse, cosine, sine, *later)


def feed_forward_kernel(
    mixed_own,
    mixed_other,
    x_own,
    x_other,
    dy_own,
    dy_other,
    gain,
    wo_own,
    wo_other,
    w_both,
    w_down,
    normed,
    scale_out,
    hidden_out,
    dboth_out,
    out_own,
    out_other,
    dnormed,
    resid,
    both,
    dhidden,
):
    own = is_own(pl.program_id(0))
    units = w_down.shape[1]
    resid[...] = dot(mixed_own[...], wo_own[...], 1, 1) + dot(
        mixed_other[...], wo_other[...], 1, 1
    )
    dhidden[...] = dot(jnp.where(own, dy_own[...], dy_other[...]), w_down[...], 1, 0)
    for rows in strips():
        values = resid[rows, :] + jnp.where(own, x_own[rows, :], x_other[rows, :]).astype(full)
        resid[rows, :] = values
        unit, scale = normalized(values)
        normed[rows, :] = (unit * gain[...]).astype(low)
        scale_out[rows, :] = jnp.broadcast_to(scale, (STRIP, 128))
    both[...] = dot(normed[...], w_both[...], 1, 0)
    for rows in strips():
        gate, up, pull = both[rows, :units], both[rows, units:], dhidden[rows, :]
        cumulative = 0.5 + 0.5 * lax.erf(gate * np.float32(0.5**0.5))
        density = jnp.exp(gate * gate * -0.5) * np.float32((2.0 * np.pi) ** -0.5)
        activated = gate * cumulative
        hidden_out[rows, :] = (activated * up).astype(low)
        dboth_out[rows, :units] = (pull * up * (cumulative + gate * density)).astype(low)
        dboth_out[rows, units:] = (pull * activated).astype(low)
    dnormed[...] = dot(dboth_out[...], w_both[...], 1, 1).astype(low)
    part = dot(hidden_out[...], w_down[...], 1, 1)

    @pl.when(own)
    def _():
        out_own[...] = resid[...] + part

    @pl.when(jnp.logical_not(own))
    def _():
        out_other[...] = part.astype(low)


def feed_forward(
    mixed, mixed_other, x_own, x_other, dy_own, dy_other, gain, wo, wo_other, w_both, w_down
):
    depth, width = wo.shape
    units = w_down.shape[1]
    half = L // 2
    return pl.pallas_call(
        feed_forward_kernel,
        grid=(L // ROWS,),
        in_specs=[
            rows_of(width),
            rows_of(width, swapped),
            rows_of(depth, own_half),
            rows_of(depth, other_half),
            rows_of(depth, own_half),
            rows_of(depth, other_half),
            whole((1, depth)),
            whole((depth, width)),
            whole((depth, width)),
            whole((depth, 2 * units)),
            whole((depth, units)),
        ],
        out_specs=[
            rows_of(depth),
            rows_of(128),
            rows_of(units),
            rows_of(2 * units),
            rows_of(depth, own_half),
            rows_of(depth, other_half),
            rows_of(depth),
        ],
        out_shape=[
            like((L, depth)),
            like((L, 128), full),
            like((L, units)),
            like((L, 2 * units)),
            like((half, depth), full),
            like((half, depth)),
            like((L, depth)),
        ],
        scratch_shapes=[
            pltpu.VMEM((ROWS, depth), full),
            pltpu.VMEM((ROWS, 2 * units), full),
            pltpu.VMEM((ROWS, units), full),
        ],
        compiler_params=params(),
        cost_estimate=SHORT,
        name="feed_forward",
    )(mixed, mixed_other, x_own, x_other, dy_own, dy_other, gain, wo, wo_other, w_both, w_down)


def resid_back_kernel(
    normed, scale_ref, grad_own, grad_other, dy_own, dy_other, gain, wo, dresid, dresid_low, dmixed
):
    own = is_own(pl.program_id(0))
    inverse = 1.0 / gain[...]
    for rows in strips():
        pull = jnp.where(own, dy_own[rows, :], dy_other[rows, :]).astype(full)
        grads = grad_own[rows, :].astype(full) + grad_other[rows, :].astype(full)
        unit = normed[rows, :].astype(full) * inverse
        total = pull + norm_back(unit, scale_ref[rows, 0:1], gain[...], grads)
        dresid_low[rows, :] = total.astype(low)

        @pl.when(own)
        def _():
            dresid[rows, :] = total

    dmixed[...] = dot(dresid_low[...], wo[...], 1, 0).astype(low)


def resid_back(normed, scale, grad_own, grad_other, dy_own, dy_other, gain, wo, later=()):
    depth, width = wo.shape
    skip = len(later)

    def body(*refs):
        resid_back_kernel(*refs[:8], *refs[8 + skip :])

    return pl.pallas_call(
        body,
        grid=(L // ROWS,),
        in_specs=[
            rows_of(depth),
            rows_of(128),
            rows_of(depth),
            rows_of(depth, swapped),
            rows_of(depth, own_half),
            rows_of(depth, other_half),
            whole((1, depth)),
            whole((depth, width)),
        ]
        + [ANY] * skip,
        out_specs=[rows_of(depth, own_half), rows_of(depth), rows_of(width)],
        out_shape=[like((L // 2, depth), full), like((L, depth)), like((L, width))],
        compiler_params=params(),
        cost_estimate=SHORT,
        name="resid_back",
    )(normed, scale, grad_own, grad_other, dy_own, dy_other, gain, wo, *later)


def project_back_kernel(*refs):
    grads, weight, (grad_own, grad_other) = refs[:9], refs[9], refs[10:12]
    rows = jnp.concatenate([ref[...] for ref in grads], axis=1)
    grad = dot(rows, weight[...], 1, 1)
    own = is_own(pl.program_id(0))

    @pl.when(own)
    def _():
        grad_own[...] = grad

    @pl.when(jnp.logical_not(own))
    def _():
        grad_other[...] = grad.astype(low)


def project_back(grads, weight, later=()):
    depth, total = weight.shape
    skip = len(later)

    def body(*refs):
        project_back_kernel(*refs[:10], *refs[10 + skip :])

    return pl.pallas_call(
        body,
        grid=(L // ROWS,),
        in_specs=[rows_of(PAIR)] * 9 + [whole((depth, total))] + [ANY] * skip,
        out_specs=[rows_of(depth, own_half), rows_of(depth, other_half)],
        out_shape=[like((L // 2, depth), full), like((L // 2, depth))],
        compiler_params=params(),
        cost_estimate=SHORT,
        name="project_back",
    )(*grads, weight, *later)


def input_back_kernel(tokens, grad_own, grad_other, dresid, gain, result):
    for rows in strips():
        grads = grad_own[rows, :] + grad_other[rows, :].astype(full)
        unit, scale = normalized(tokens[rows, :].astype(full))
        result[rows, :] = dresid[rows, :] + norm_back(unit, scale, gain[...], grads)


def input_back(tokens, grad_own, grad_other, dresid, gain):
    height, depth = tokens.shape
    return pl.pallas_call(
        input_back_kernel,
        grid=(height // ROWS,),
        in_specs=[rows_of(depth)] * 4 + [whole((1, depth))],
        out_specs=rows_of(depth),
        out_shape=like((height, depth), full),
        compiler_params=params(),
        cost_estimate=SHORT,
        name="input_back",
    )(tokens, grad_own, grad_other, dresid, gain)


def adamw(weight, grad, first, second, rate, decay):
    first_new = beta_one * first + (1.0 - beta_one) * grad
    second_new = beta_two * second + (1.0 - beta_two) * grad * grad
    step_size = (
        first_new
        / (1.0 - beta_one**STEP)
        / (jnp.sqrt(second_new / (1.0 - beta_two**STEP)) + adam_eps)
    )
    return (weight - rate * (step_size + decay * weight), first_new, second_new)


def step_kernel(counts, flipped, spans, column_at, *refs):
    totals, used = [], 0
    for count in counts:
        total = refs[used][...].astype(full)
        for piece in refs[used + 1 : used + count]:
            total = total + piece[...].astype(full)
        totals.append(total)
        used += count
    rest, count = refs[used:], len(spans)
    states, outs = rest[: 3 * count], rest[3 * count : 7 * count]
    scratch = rest[7 * count + 1 :]
    rows = totals[0].shape[0]
    rest[7 * count][...] = totals[0][:, column_at : column_at + SPARE]
    for at, span in enumerate(spans):
        weight, first, second = states[3 * at : 3 * at + 3]
        grad_out, weight_out, first_out, second_out = outs[4 * at : 4 * at + 4]
        for part, (group, start, width) in enumerate(span):
            grad = totals[group][:, start : start + width]
            if flipped[at]:
                padded = scratch[at]
                padded[...] = jnp.zeros_like(padded)
                padded[0:rows, 0:width] = grad
                grad = padded[...].T[0:width, 0:rows]
                where = Ellipsis
            else:
                where = part
            new = adamw(
                weight[where], grad, first[where], second[where], weight_rate, weight_decay
            )
            grad_out[where] = grad
            weight_out[where], first_out[where], second_out[where] = new


def step(groups, spans, states, flipped, column_at, later=()):
    shapes, scratch = [], []
    for (weight, _, _), span, flip in zip(states, spans, flipped):
        shapes += [like(weight.shape, full)] * 4
        lanes = -(-span[0][2] // 128) * 128
        scratch.append(pltpu.VMEM((128, lanes) if flip else (8, 128), full))
    shapes.append(like((groups[0][0].shape[0], SPARE), full))
    flat = [array for state in states for array in state]
    results = call(
        functools.partial(step_kernel, [len(group) for group in groups], flipped, spans, column_at),
        "step",
        [piece for group in groups for piece in group] + flat,
        shapes,
        later=later,
        scratch=scratch,
    )
    return [results[4 * at : 4 * at + 4] for at in range(len(states))] + [results[-1]]


def column(pieces, at):
    return sum(piece[:, at : at + 1].astype(full) for piece in pieces)


def shards(
    tokens,
    cotangent,
    w_qkv,
    w_attn_out,
    w_in,
    w_mlp_out,
    gains,
    first_qkv,
    first_attn_out,
    first_in,
    first_mlp_out,
    first_gains,
    second_qkv,
    second_attn_out,
    second_in,
    second_mlp_out,
    second_gains,
):
    count = lax.axis_size("dp")
    fast = staged(count)
    core = lax.axis_index("tensor") % 2
    head_width = w_qkv.shape[2]
    unit_width = w_in.shape[2]
    depth = tokens.shape[1]
    qkv_layouts = [[(part * head_width, head_width) for part in range(3)]]
    gains_at = 3 * head_width
    gate_at, up_at, down_at = (head_width + part * unit_width for part in range(3))
    rest_layouts = [
        [(0, head_width)],
        [(gate_at, unit_width), None, (up_at, unit_width), None],
        [(down_at, unit_width), None],
    ]

    shard_one = pack(w_qkv, gains)
    shard_two = pack_rest(w_attn_out, w_in, w_mlp_out, [shard_one])
    cosine, sine = rope_tables(core * (L // 2))

    def halves(shard, along):
        half = shard.shape[0] // 2
        pieces = [shard] + along
        return jnp.stack([p[:half] for p in pieces]), jnp.stack([p[half:] for p in pieces])

    if fast:
        along_one = [z_shift(shard_one, count, jump) for jump in (1, 2, 3)]
        x_other = core_swap(tokens)
        za, zb = halves(after(shard_one, shard_two, x_other), along_one)
        shard_two = after(shard_two, *along_one)
        along_two = [z_shift(shard_two, count, jump) for jump in (1, 2, 3)]
        xa, yb = x_swap(za, count), y_swap(zb)
        both_a, both_b = jnp.stack([za, xa]), jnp.stack([zb, yb])
        ya, xb = y_swap(both_a), x_swap(both_b, count)
        first_pieces = [za, xa, ya, zb, yb, xb]
        za, zb = halves(shard_two, [after(piece, both_a, both_b) for piece in along_two])
        w_qkv_all, gains_all = assemble(
            first_pieces, qkv_layouts, depth, gains_at, later=[cosine, sine, za, zb]
        )
    else:
        x_other = core_swap(tokens)
        w_qkv_all, gains_all = gathered_plainly(shard_one, qkv_layouts, gains_at)
    gain_one, gain_two = gains_all[0:1], gains_all[1:2]
    if fast:
        xa, yb = x_swap(za, count), y_swap(zb)
    normed_one, query, key, value = project(tokens, x_other, gain_one, w_qkv_all, cosine, sine)
    if fast:
        xa, yb = after(xa, query), after(yb, query)
        ya, xb = y_swap(jnp.stack([za, xa])), x_swap(jnp.stack([zb, yb]), count)
    dy_other = core_swap(after(cotangent, query))
    mixed, lse = attend(query, key, value)
    mixed_other = core_swap(mixed)
    if fast:
        ya, xb = after(ya, mixed), after(xb, mixed)
        wo, w_both, w_down = assemble([za, xa, ya, zb, yb, xb], rest_layouts, depth)
    else:
        wo, w_both, w_down = gathered_plainly(shard_two, rest_layouts)
    wo_other = core_swap(wo)
    normed_two, scale_two, hidden, dboth, out_own, out_other, dnormed = feed_forward(
        mixed,
        mixed_other,
        tokens,
        x_other,
        cotangent,
        dy_other,
        gain_two,
        wo,
        wo_other,
        w_both,
        w_down,
    )
    units = w_down.shape[1]
    dnormed_other = core_swap(dnormed)
    grad_a = weight_grad(
        [normed_two, dboth],
        [((0,), (1,), [(0, unit_width), (units, unit_width)])],
        count,
        "y",
        w_both,
    )
    if fast:
        from_a = y_swap(grad_a[1])
    output = (out_own + core_swap(out_other).astype(full)).astype(low)
    dresid, dresid_low, dmixed = resid_back(
        normed_two,
        scale_two,
        dnormed,
        dnormed_other,
        cotangent,
        dy_other,
        gain_two,
        wo,
        later=grad_a[:1],
    )
    grad_b = weight_grad(
        [cotangent, dy_other, hidden, dresid_low, mixed],
        [((0, 1), (2,), [(0, unit_width)]), ((3,), (4,), [(0, head_width)])],
        count,
        "x",
        later=[dmixed, output],
    )
    if fast:
        from_b = x_swap(grad_b[1], count)
    bundle = (query, key, value, mixed, dmixed, lse, cosine, sine)
    pair_0 = attend_back(0, *bundle, later=grad_b[:1])
    if fast:
        stay_a, go_a = add_first([(grad_a[0], from_a)], later=pair_0[:1])
        next_a = x_swap(go_a, count)
        pair_1 = attend_back(1, *bundle, later=[go_a])
        stay_b, go_b = add_first([(grad_b[0], from_b)], later=pair_1[:1])
        next_b = y_swap(go_b)
        merged_a = add_second([(stay_a, next_a)], later=[go_b])
        pieces_a = across_z(merged_a, count)
        pair_2 = attend_back(2, *bundle, later=[merged_a[0]])
        merged_b = add_second([(stay_b, next_b)], later=pair_2[:1])
        pieces_b = across_z(merged_b, count)
    else:
        pair_1, pair_2 = attend_back(1, *bundle), attend_back(2, *bundle)
    trios = [group[part] for part in range(3) for group in (pair_0, pair_1, pair_2)]
    grad_c = weight_grad(
        [normed_one, *trios],
        [((0,), tuple(range(1, 10)), [(2 * part * head_width, head_width) for part in range(3)])],
        count,
        "both",
        w_qkv_all,
        later=[merged_b[0], *pieces_a] if fast else (),
    )
    if fast:
        from_y, from_x = y_swap(grad_c[1]), x_swap(grad_c[3], count)
    else:
        pieces_a, pieces_b = reduced_plainly(*grad_a), reduced_plainly(*grad_b)
    grad_one, grad_one_low = project_back(trios, w_qkv_all, later=grad_c[:1])
    if fast:
        from_y = after(from_y, grad_one, *pieces_b)
        from_x = after(from_x, grad_one, *pieces_b)
        stay_a, go_a, stay_b, go_b = add_first([(grad_c[0], from_y), (grad_c[2], from_x)])
        next_a, next_b = x_swap(go_a, count), y_swap(go_b)
    if fast:
        grad_one_low = after(grad_one_low, go_a, go_b)
    grad_other = core_swap(grad_one_low)
    grad_inputs = input_back(tokens, grad_one, grad_other, dresid, gain_one)
    new_in, new_attn, new_down, gain_sums = step(
        [pieces_a, pieces_b],
        [
            [(0, 0, unit_width), (0, unit_width, unit_width)],
            [(1, unit_width, head_width)],
            [(1, 0, unit_width)],
        ],
        [
            (w_in, first_in, second_in),
            (w_attn_out, first_attn_out, second_attn_out),
            (w_mlp_out, first_mlp_out, second_mlp_out),
        ],
        (False, True, True),
        2 * unit_width,
        later=(go_a, go_b) if fast else (),
    )
    if fast:
        done = (grad_inputs, gain_sums)
        next_a, next_b = after(next_a, *done), after(next_b, *done)
        pieces_c = across_z(add_second([(stay_a, next_a), (stay_b, next_b)]), count)
    else:
        pieces_c = reduced_plainly(*grad_c)
    sums = jnp.concatenate([column(pieces_c, 3 * head_width), gain_sums[:, :1]], axis=1)
    shard_gain = (sums + core_swap(sums)).T / gains
    new_qkv, _ = step(
        [pieces_c],
        [[(0, part * head_width, head_width) for part in range(3)]],
        [(w_qkv, first_qkv, second_qkv)],
        (False,),
        3 * head_width,
    )
    new_gain = adamw(gains, shard_gain, first_gains, second_gains, gain_rate, 0.0)
    return (
        output,
        grad_inputs,
        new_qkv[0],
        new_attn[0],
        new_in[0],
        new_down[0],
        shard_gain,
        new_qkv[1],
        new_attn[1],
        new_in[1],
        new_down[1],
        new_gain[0],
        new_qkv[2],
        new_attn[2],
        new_in[2],
        new_down[2],
        new_gain[1],
        new_qkv[3],
        new_attn[3],
        new_in[3],
        new_down[3],
        new_gain[2],
    )


def solution(mesh):
    return jax.shard_map(
        shards,
        mesh=mesh,
        in_specs=(
            P(("dp", "tensor"), None),
            P(("dp", "tensor"), None),
            P(None, "dp", "tensor"),
            P("tensor", "dp"),
            P(None, "dp", "tensor"),
            P("tensor", "dp"),
            P(None, "dp"),
            P(None, "dp", "tensor"),
            P("tensor", "dp"),
            P(None, "dp", "tensor"),
            P("tensor", "dp"),
            P(None, "dp"),
            P(None, "dp", "tensor"),
            P("tensor", "dp"),
            P(None, "dp", "tensor"),
            P("tensor", "dp"),
            P(None, "dp"),
        ),
        out_specs=(
            P(("dp", "tensor"), None),
            P(("dp", "tensor"), None),
            P(None, "dp", "tensor"),
            P("tensor", "dp"),
            P(None, "dp", "tensor"),
            P("tensor", "dp"),
            P(None, "dp"),
            P(None, "dp", "tensor"),
            P("tensor", "dp"),
            P(None, "dp", "tensor"),
            P("tensor", "dp"),
            P(None, "dp"),
            P(None, "dp", "tensor"),
            P("tensor", "dp"),
            P(None, "dp", "tensor"),
            P("tensor", "dp"),
            P(None, "dp"),
            P(None, "dp", "tensor"),
            P("tensor", "dp"),
            P(None, "dp", "tensor"),
            P("tensor", "dp"),
            P(None, "dp"),
        ),
        check_vma=False,
    )
```

```python
import functools

import jax
import jax.numpy as jnp
import numpy as np
from jax import lax
from jax.experimental import pallas as pl
from jax.experimental.pallas import tpu as pltpu
from jax.sharding import PartitionSpec as P

HD = 64
L = 1024
STEP = 10


eps_norm = 1e-05
rope_base = 160000.0
beta_one = 0.9
beta_two = 0.98
adam_eps = 1e-06
weight_rate = 0.02
gain_rate = 0.2
weight_decay = 0.01

low = jnp.bfloat16
full = jnp.float32
ROWS = 256
PAIR = 2 * HD
VMEM_BYTES = 52 << 20
SPARE = 64
SHORT = pl.CostEstimate(flops=0, bytes_accessed=0, transcendentals=0)


def dot(left, right, left_dim, right_dim):
    return lax.dot_general(
        left, right, (((left_dim,), (right_dim,)), ((), ())), preferred_element_type=full
    )


def params():
    return pltpu.CompilerParams(vmem_limit_bytes=VMEM_BYTES)


def whole(shape):
    return pl.BlockSpec(shape, lambda *_: (0,) * len(shape))


def rows_of(width, index=lambda i: i):
    return pl.BlockSpec((ROWS, width), lambda i: (index(i), 0))


def own_half(i):
    return jnp.minimum(i, L // ROWS // 2 - 1)


def other_half(i):
    return jnp.maximum(i - L // ROWS // 2, 0)


def swapped(i):
    return (i + L // ROWS // 2) % (L // ROWS)


def is_own(i):
    return i < L // ROWS // 2


def core_swap(array):
    return lax.ppermute(array, "tensor", [(t, t ^ 1) for t in range(4)])


def y_swap(array):
    return lax.ppermute(array, "tensor", [(t, t ^ 2) for t in range(4)])


def x_swap(array, count):
    return lax.ppermute(array, "dp", [(d, d ^ 1) for d in range(count)])


def z_shift(array, count, step):
    around = count // 2
    return lax.ppermute(
        array, "dp", [(d, (d // 2 + step) % around * 2 + d % 2) for d in range(count)]
    )


def staged(count):
    return count == 8


def after(array, *others):
    return lax.optimization_barrier((array, *others))[0]


ANY = pl.BlockSpec(memory_space=pl.ANY)
LOCAL = pl.BlockSpec(memory_space=pltpu.VMEM)
SCALAR = pl.BlockSpec(memory_space=pltpu.SMEM)


def call(kernel, name, ins, shapes, later=(), place=None, scratch=()):
    head = [] if place is None else [place]
    lead, skip = len(head), len(later)

    def body(*refs):
        kernel(*refs[: lead + len(ins)], *refs[lead + len(ins) + skip :])

    return pl.pallas_call(
        body,
        in_specs=[SCALAR] * lead + [LOCAL] * len(ins) + [ANY] * skip,
        out_specs=[LOCAL] * len(shapes),
        out_shape=shapes,
        scratch_shapes=list(scratch),
        compiler_params=params(),
        cost_estimate=SHORT,
        name=name,
    )(*head, *ins, *later)


def like(shape, kind=low):
    return jax.ShapeDtypeStruct(shape, kind)


def pack_kernel(w_qkv, gains, shard, padded):
    rows = w_qkv.shape[1]
    padded[...] = jnp.zeros_like(padded)
    padded[0 : gains.shape[0], 0:rows] = gains[...]
    columns = padded[...].T[0:rows, 0:2]
    high = columns.astype(low)
    rest = columns - high.astype(full)
    middle = rest.astype(low)
    last = (rest - middle.astype(full)).astype(low)
    filler = jnp.zeros((rows, SPARE - 6), full)
    pieces = [w_qkv[part] for part in range(3)]
    shard[...] = jnp.concatenate(
        pieces + [high.astype(full), middle.astype(full), last.astype(full), filler], axis=1
    ).astype(low)


def pack(w_qkv, gains):
    rows, width = w_qkv.shape[1:]
    return call(
        pack_kernel,
        "pack",
        [w_qkv, gains],
        [like((rows, 3 * width + SPARE))],
        scratch=[pltpu.VMEM((128, 128), full)],
    )[0]


def pack_rest_kernel(w_attn_out, w_in, w_mlp_out, shard, wide):
    rows = w_in.shape[1]
    flipped = []
    for weight in (w_attn_out, w_mlp_out):
        wide[...] = jnp.zeros_like(wide)
        wide[0 : weight.shape[0], 0:rows] = weight[...]
        flipped.append(wide[...].T[0:rows, 0 : weight.shape[0]])
    pieces = [flipped[0], w_in[0], w_in[1], flipped[1]]
    shard[...] = jnp.concatenate(pieces, axis=1).astype(low)


def pack_rest(w_attn_out, w_in, w_mlp_out, later):
    rows, units = w_in.shape[1:]
    heads = w_attn_out.shape[0]
    return call(
        pack_rest_kernel,
        "pack_rest",
        [w_attn_out, w_in, w_mlp_out],
        [like((rows, heads + 3 * units))],
        later=later,
        scratch=[pltpu.VMEM((-(-units // 128) * 128, 128), full)],
    )[0]


def unpack_gains(columns):
    wide = jnp.concatenate([columns.astype(full), jnp.zeros(columns.shape, full)], axis=1).T
    return wide[0:2] + wide[2:4] + wide[4:6]


def columns_of(layout, own, other):
    pieces = []
    for item in layout:
        if item is None:
            pieces.append(jnp.zeros((own.shape[0], SPARE), own.dtype))
        else:
            side, start, width = item
            pieces.append((own, other)[side][:, start : start + width])
    return jnp.concatenate(pieces, axis=1)


def layout_width(layout):
    return sum(SPARE if item is None else item[2] for item in layout)


def head_layout(start, width):
    first = width // 3 * 2
    return [(0, start, width), (1, start + first, width - first), (1, start, first)]


def unit_layout(start, width):
    return [(0, start, width), (1, start, width), None]


def assemble_kernel(layouts, gains_at, place_ref, za, xa, ya, zb, yb, xb, *outs):
    place = place_ref[0]
    half = za.shape[1]
    for jx in range(2):
        for jz in range(4):
            source = (place // 2 + 4 - jz) % 4 * 2 + (place % 2 + jx) % 2
            own_a = (za, xa)[jx][jz]
            other_a = ya[jx, jz]
            own_b = zb[jz] if jx == 0 else xb[0, jz]
            other_b = yb[jz] if jx == 0 else xb[1, jz]
            for part, (own, other) in enumerate(((own_a, other_a), (own_b, other_b))):
                start = pl.multiple_of(source * 2 * half + part * half, half)
                for layout, out in zip(layouts, outs):
                    out[pl.ds(start, half), :] = columns_of(layout, own, other)
                if gains_at is not None:
                    outs[-1][pl.ds(start, half), :] = own[:, gains_at : gains_at + SPARE]
    if gains_at is not None:
        outs[-2][...] = unpack_gains(outs[-1][...])


def assemble(pieces, layouts, depth, gains_at=None, later=()):
    place = lax.axis_index("dp").astype(jnp.int32)[None]
    shapes = [like((depth, layout_width(layout))) for layout in layouts]
    scratch = []
    if gains_at is not None:
        shapes.append(like((2, depth), full))
        scratch.append(pltpu.VMEM((depth, SPARE), low))
    return call(
        functools.partial(assemble_kernel, layouts, gains_at),
        "assemble",
        pieces,
        shapes,
        later=later,
        place=place,
        scratch=scratch,
    )


def gathered_plainly(shard, layouts, gains_at=None):
    own = lax.all_gather(shard, "dp", axis=0, tiled=True)
    other = y_swap(own)
    results = [columns_of(layout, own, other) for layout in layouts]
    if gains_at is not None:
        results.append(unpack_gains(own[:, gains_at : gains_at + SPARE]))
    return results


def stacked(ins, at, axis):
    parts = [ins[index][...] for index in at]
    return parts[0] if len(parts) == 1 else jnp.concatenate(parts, axis=axis)


def weight_grad_kernel(products, fast, weights, ins, place_ref, refs):
    outs, scratch = (refs[:4], refs[4:]) if fast else (refs[:2], refs[2:])
    place = place_ref[0]
    for index, (held, (left, right, _)) in enumerate(zip(scratch, products)):
        grad = dot(stacked(ins, left, 0), stacked(ins, right, 1), 0, 0)
        held[...] = grad
        if weights and index == 0:
            weight = [ins[-1][:, start : start + width] for start, width in weights]
            weight = weight[0] if len(weight) == 1 else jnp.concatenate(weight, axis=1)
            sums = jnp.sum(weight.astype(full) * grad, axis=1, keepdims=True)
            scratch[-1][...] = jnp.broadcast_to(sums, (sums.shape[0], 128))

    def split(rows):
        sides = [[], []]
        for held, (_, _, spans) in zip(scratch, products):
            values = held[rows, :]
            for *starts, width in spans:
                for side, start in zip(sides, starts):
                    side.append(values[:, start : start + width])
        if weights:
            for side in sides:
                side.append(scratch[-1][rows, :][:, :SPARE])
        return [jnp.concatenate(side, axis=1).astype(low) for side in sides]

    if not fast:
        outs[0][...], outs[1][...] = split(slice(None))
        return
    size = outs[0].shape[2]
    for jx in range(2):
        for jz in range(4):
            target = (place // 2 + jz) % 4 * 2 + (place % 2 + jx) % 2
            for part in range(2):
                start = pl.multiple_of((target * 2 + part) * size, size)
                own, other = split(pl.ds(start, size))
                if part == 0:
                    outs[0][jx, jz] = own
                    outs[1][jx, jz] = other
                else:
                    outs[2 + jx][0, jz] = own
                    outs[2 + jx][1, jz] = other


def weight_grad(arrays, products, count, weight=None, lanes=(), later=()):
    depth = arrays[products[0][0][0]].shape[1]
    widths = [sum(arrays[at].shape[1] for at in right) for _, right, _ in products]
    total = sum(span[2] for _, _, spans in products for span in spans)
    total += SPARE if weight is not None else 0
    fast = staged(count)
    if fast:
        shapes = [like((2, 4, depth // count // 2, total))] * 4
    else:
        shapes = [like((depth, total))] * 2
    place = lax.axis_index("dp").astype(jnp.int32)[None]
    ins = list(arrays) + ([] if weight is None else [weight])
    weights = [] if weight is None else list(lanes)
    held = [pltpu.VMEM((depth, width), full) for width in widths]
    if weights:
        held.append(pltpu.VMEM((depth, 128), full))

    def kernel(place_ref, *refs):
        weight_grad_kernel(
            products, fast, weights, refs[: len(ins)], place_ref, refs[len(ins) :]
        )

    return call(
        kernel,
        "weight_grad",
        ins,
        shapes,
        later=later,
        place=place,
        scratch=held,
    )


def reduced_plainly(own, other):
    summed = own.astype(full) + y_swap(other).astype(full)
    return [lax.psum_scatter(summed, "dp", scatter_dimension=0, tiled=True)]


def add_kernel(groups, *refs):
    ins, outs = refs[: 4 * groups], refs[4 * groups :]
    for half in range(2):
        for side in range(2):
            sums = []
            for group in range(groups):
                here, there = ins[4 * group + 2 * half : 4 * group + 2 * half + 2]
                sums.append((here[side].astype(full) + there[side].astype(full)).astype(low))
            out = outs[2 * half + side]
            out[...] = sums[0] if groups == 1 else jnp.concatenate(sums, axis=-1)


def add_first(groups, later=()):
    rows = groups[0][0].shape[2]
    width = sum(group[0].shape[3] for group in groups)
    return call(
        functools.partial(add_kernel, len(groups)),
        "add_first",
        [array for group in groups for array in group],
        [like((4, rows, width))] * 4,
        later=later,
    )


def merge_kernel(here_a, there_a, here_b, there_b, *outs):
    for jump, out in enumerate(outs):
        part_a = here_a[jump].astype(full) + there_a[jump].astype(full)
        part_b = here_b[jump].astype(full) + there_b[jump].astype(full)
        out[...] = jnp.concatenate([part_a.astype(low), part_b.astype(low)], axis=0)


def add_second(here_a, there_a, here_b, there_b, later=()):
    _, rows, width = here_a.shape
    return call(
        merge_kernel,
        "add_second",
        [here_a, there_a, here_b, there_b],
        [like((2 * rows, width))] * 4,
        later=later,
    )


def across_z(parts, count):
    return [parts[0]] + [z_shift(parts[step], count, step) for step in (1, 2, 3)]


def normalized(values):
    centred = values - jnp.mean(values, axis=-1, keepdims=True)
    spread = jnp.mean(centred * centred, axis=-1, keepdims=True)
    scale = lax.rsqrt(spread + eps_norm)
    return centred * scale, scale


def norm_back(unit, scale, gains, grads):
    inner = grads * gains
    mean_inner = jnp.mean(inner, axis=-1, keepdims=True)
    mean_unit = jnp.mean(inner * unit, axis=-1, keepdims=True)
    return scale * (inner - mean_inner - unit * mean_unit)


def rope_tables(offset):
    half_width = HD // 2
    frequency = rope_base ** (-(jnp.arange(half_width, dtype=full) * 2.0 / HD))
    position = ((jnp.arange(L) + offset) % L).astype(full)
    angles = position[:, None] * frequency[None, :]
    cosine, sine = jnp.cos(angles), jnp.sin(angles)
    return (
        jnp.concatenate([cosine] * 4, axis=1),
        jnp.concatenate([-sine, sine, -sine, sine], axis=1),
    )


def turn(values, cosine, sine):
    lane = lax.broadcasted_iota(jnp.int32, values.shape, 1)
    ahead = pltpu.roll(values, PAIR - HD // 2, 1)
    behind = pltpu.roll(values, HD // 2, 1)
    turned = jnp.where(lane % HD < HD // 2, ahead, behind)
    return values * cosine + turned * sine


def qkv_kernel(x_own, x_other, gain, weight, cosine, sine, normed, q_out, k_out, v_out, raw):
    own = is_own(pl.program_id(0))
    unit, _ = normalized(jnp.where(own, x_own[...], x_other[...]).astype(full))
    rows = (unit * gain[...]).astype(low)
    normed[...] = rows
    raw[...] = dot(rows, weight[...], 1, 0)
    width = q_out.shape[1]
    near, far = cosine[...], sine[...]
    for start in range(0, width, PAIR):
        lanes = slice(start, start + PAIR)
        query = turn(raw[:, lanes], near, far).astype(low)
        q_out[:, lanes] = query * jnp.asarray(HD ** (-0.5), low)
        key = raw[:, width + start : width + start + PAIR]
        k_out[:, lanes] = turn(key, near, far).astype(low)
    v_out[...] = raw[:, 2 * width :].astype(low)


def project(x_own, x_other, gain, weight, cosine, sine):
    depth, total = weight.shape
    width = total // 3
    return pl.pallas_call(
        qkv_kernel,
        grid=(L // ROWS,),
        in_specs=[
            rows_of(depth, own_half),
            rows_of(depth, other_half),
            whole((1, depth)),
            whole((depth, total)),
            rows_of(PAIR),
            rows_of(PAIR),
        ],
        out_specs=[rows_of(depth), rows_of(width), rows_of(width), rows_of(width)],
        out_shape=[like((L, depth))] + [like((L, width))] * 3,
        scratch_shapes=[pltpu.VMEM((ROWS, total), full)],
        compiler_params=params(),
        cost_estimate=SHORT,
        name="project",
    )(x_own, x_other, gain, weight, cosine, sine)


def head_masks(height):
    lane = lax.broadcasted_iota(jnp.int32, (height, PAIR), 1)
    return [(lane // HD == head).astype(full).astype(low) for head in range(2)]


def attend_kernel(q_ref, k_ref, v_ref, mixed, lse_ref):
    keys, values = k_ref[...], v_ref[...]
    masks = head_masks(ROWS)
    lane = lax.broadcasted_iota(jnp.int32, (ROWS, PAIR), 1)
    for start in range(0, L, ROWS):
        rows = slice(start, start + ROWS)
        query = q_ref[rows, :]
        results = []
        for head in range(2):
            scores = dot(query * masks[head], keys, 1, 1)
            row_max = jnp.max(scores, axis=1, keepdims=True)
            raised = jnp.exp(scores - row_max)
            total = jnp.sum(raised, axis=1, keepdims=True)
            results.append(dot(raised.astype(low), values, 1, 0) / total)
            lse = jnp.broadcast_to(row_max + jnp.log(total), (ROWS, PAIR))
            lse_ref[0, head : head + 1, rows] = lse.T[0:1]
        mixed[rows, :] = jnp.where(lane < HD, results[0], results[1]).astype(low)


def attend(query, key, value):
    width = query.shape[1]
    pairs = width // PAIR
    block = pl.BlockSpec((L, PAIR), lambda i: (0, i))
    totals = pl.BlockSpec((1, 2, L), lambda i: (i, 0, 0))
    return pl.pallas_call(
        attend_kernel,
        grid=(pairs,),
        in_specs=[block] * 3,
        out_specs=[block, totals],
        out_shape=[
            jax.ShapeDtypeStruct((L, width), low),
            jax.ShapeDtypeStruct((pairs, 2, L), full),
        ],
        compiler_params=params(),
        cost_estimate=SHORT,
        name="attend",
    )(query, key, value)


def attend_back_kernel(
    q_ref, k_ref, v_ref, o_ref, grad_ref, lse_ref, cosine, sine, dq_out, dk_out, dv_out, dk, dv
):
    masks = head_masks(L)
    chunk_masks = head_masks(ROWS)
    keys, values = k_ref[...], v_ref[...]
    head_keys = [keys * mask for mask in masks]
    head_values = [values * mask for mask in masks]
    flipped_keys = keys.astype(full).T
    half_rows = lax.broadcasted_iota(jnp.int32, flipped_keys.shape, 0) // HD
    flipped_keys = [jnp.where(half_rows == head, flipped_keys, 0.0).astype(low) for head in range(2)]
    product = (grad_ref[...].astype(full) * o_ref[...].astype(full)).T
    inner = [jnp.sum(product[head * HD : (head + 1) * HD], axis=0, keepdims=True) for head in range(2)]
    for start in range(0, L, ROWS):
        rows = slice(start, start + ROWS)
        query, grad = q_ref[rows, :], grad_ref[rows, :]
        dq = None
        for head in range(2):
            scores = dot(head_keys[head], query, 1, 1)
            probs = jnp.exp(scores - lse_ref[0, head : head + 1, rows])
            grad_probs = dot(head_values[head], grad, 1, 1)
            grad_scores = (probs * (grad_probs - inner[head][:, rows])).astype(low)
            add_v = dot(probs.astype(low), grad * chunk_masks[head], 1, 0)
            add_k = dot(grad_scores, query * chunk_masks[head], 1, 0)
            add_q = dot(flipped_keys[head], grad_scores, 1, 0)
            dq = add_q if dq is None else dq + add_q
            if start == 0 and head == 0:
                dv[...] = add_v
                dk[...] = add_k
            else:
                dv[...] += add_v
                dk[...] += add_k
        dq_out[rows, :] = turn(dq.T * HD ** (-0.5), cosine[rows, :], -sine[rows, :]).astype(low)
    dk_out[...] = turn(dk[...], cosine[...], -sine[...]).astype(low)
    dv_out[...] = dv[...].astype(low)


def attend_back(pair, query, key, value, mixed, grad, lse, cosine, sine, later=()):
    block = pl.BlockSpec((L, PAIR), lambda i: (0, pair))
    result = pl.BlockSpec((L, PAIR), lambda i: (0, 0))
    totals = pl.BlockSpec((1, 2, L), lambda i: (pair, 0, 0))
    skip = len(later)

    def body(*refs):
        attend_back_kernel(*refs[:8], *refs[8 + skip :])

    return pl.pallas_call(
        body,
        grid=(1,),
        in_specs=[block] * 5 + [totals] + [whole((L, PAIR))] * 2 + [ANY] * skip,
        out_specs=[result] * 3,
        out_shape=[like((L, PAIR))] * 3,
        scratch_shapes=[pltpu.VMEM((L, PAIR), full)] * 2,
        compiler_params=params(),
        cost_estimate=SHORT,
        name="attend_back",
    )(query, key, value, mixed, grad, lse, cosine, sine, *later)


def feed_forward_kernel(
    mixed_own,
    mixed_other,
    x_own,
    x_other,
    dy_own,
    dy_other,
    gain,
    wo_own,
    wo_other,
    w_both,
    w_down,
    normed,
    scale_out,
    hidden_out,
    dboth_out,
    out_own,
    out_other,
    dnormed,
):
    own = is_own(pl.program_id(0))
    units = w_down.shape[1]
    tokens = jnp.where(own, x_own[...], x_other[...]).astype(full)
    resid = (
        tokens + dot(mixed_own[...], wo_own[...], 1, 1) + dot(mixed_other[...], wo_other[...], 1, 1)
    )
    unit, scale = normalized(resid)
    rows = (unit * gain[...]).astype(low)
    normed[...] = rows
    scale_out[...] = jnp.broadcast_to(scale, scale_out.shape)
    both = dot(rows, w_both[...], 1, 0)
    gate, up = both[:, :units], both[:, units:]
    cumulative = 0.5 + 0.5 * lax.erf(gate * np.float32(0.5**0.5))
    density = jnp.exp(gate * gate * -0.5) * np.float32((2.0 * np.pi) ** -0.5)
    activated = gate * cumulative
    hidden = (activated * up).astype(low)
    hidden_out[...] = hidden
    part = dot(hidden, w_down[...], 1, 1)
    dhidden = dot(jnp.where(own, dy_own[...], dy_other[...]), w_down[...], 1, 0)
    dgate = (dhidden * up * (cumulative + gate * density)).astype(low)
    dup = (dhidden * activated).astype(low)
    dboth = jnp.concatenate([dgate, dup], axis=1)
    dboth_out[...] = dboth
    dnormed[...] = dot(dboth, w_both[...], 1, 1).astype(low)

    @pl.when(own)
    def _():
        out_own[...] = resid + part

    @pl.when(jnp.logical_not(own))
    def _():
        out_other[...] = part.astype(low)


def feed_forward(
    mixed, mixed_other, x_own, x_other, dy_own, dy_other, gain, wo, wo_other, w_both, w_down
):
    depth, width = wo.shape
    units = w_down.shape[1]
    half = L // 2
    return pl.pallas_call(
        feed_forward_kernel,
        grid=(L // ROWS,),
        in_specs=[
            rows_of(width),
            rows_of(width, swapped),
            rows_of(depth, own_half),
            rows_of(depth, other_half),
            rows_of(depth, own_half),
            rows_of(depth, other_half),
            whole((1, depth)),
            whole((depth, width)),
            whole((depth, width)),
            whole((depth, 2 * units)),
            whole((depth, units)),
        ],
        out_specs=[
            rows_of(depth),
            rows_of(128),
            rows_of(units),
            rows_of(2 * units),
            rows_of(depth, own_half),
            rows_of(depth, other_half),
            rows_of(depth),
        ],
        out_shape=[
            like((L, depth)),
            like((L, 128), full),
            like((L, units)),
            like((L, 2 * units)),
            like((half, depth), full),
            like((half, depth)),
            like((L, depth)),
        ],
        compiler_params=params(),
        cost_estimate=SHORT,
        name="feed_forward",
    )(mixed, mixed_other, x_own, x_other, dy_own, dy_other, gain, wo, wo_other, w_both, w_down)


def resid_back_kernel(
    normed, scale_ref, grad_own, grad_other, dy_own, dy_other, gain, wo, dresid, dresid_low, dmixed
):
    own = is_own(pl.program_id(0))
    inverse = 1.0 / gain[...]
    pull = jnp.where(own, dy_own[...], dy_other[...]).astype(full)
    grads = grad_own[...].astype(full) + grad_other[...].astype(full)
    unit = normed[...].astype(full) * inverse
    total = pull + norm_back(unit, scale_ref[:, 0:1], gain[...], grads)
    rounded = total.astype(low)
    dresid_low[...] = rounded
    dmixed[...] = dot(rounded, wo[...], 1, 0).astype(low)

    @pl.when(own)
    def _():
        dresid[...] = total


def resid_back(normed, scale, grad_own, grad_other, dy_own, dy_other, gain, wo, later=()):
    depth, width = wo.shape
    skip = len(later)

    def body(*refs):
        resid_back_kernel(*refs[:8], *refs[8 + skip :])

    return pl.pallas_call(
        body,
        grid=(L // ROWS,),
        in_specs=[
            rows_of(depth),
            rows_of(128),
            rows_of(depth),
            rows_of(depth, swapped),
            rows_of(depth, own_half),
            rows_of(depth, other_half),
            whole((1, depth)),
            whole((depth, width)),
        ]
        + [ANY] * skip,
        out_specs=[rows_of(depth, own_half), rows_of(depth), rows_of(width)],
        out_shape=[like((L // 2, depth), full), like((L, depth)), like((L, width))],
        compiler_params=params(),
        cost_estimate=SHORT,
        name="resid_back",
    )(normed, scale, grad_own, grad_other, dy_own, dy_other, gain, wo, *later)


def project_back_kernel(*refs):
    grads, weight, (grad_own, grad_other) = refs[:9], refs[9], refs[10:12]
    rows = jnp.concatenate([ref[...] for ref in grads], axis=1)
    grad = dot(rows, weight[...], 1, 1)
    own = is_own(pl.program_id(0))

    @pl.when(own)
    def _():
        grad_own[...] = grad

    @pl.when(jnp.logical_not(own))
    def _():
        grad_other[...] = grad.astype(low)


def project_back(grads, weight, later=()):
    depth, total = weight.shape
    skip = len(later)

    def body(*refs):
        project_back_kernel(*refs[:10], *refs[10 + skip :])

    return pl.pallas_call(
        body,
        grid=(L // ROWS,),
        in_specs=[rows_of(PAIR)] * 9 + [whole((depth, total))] + [ANY] * skip,
        out_specs=[rows_of(depth, own_half), rows_of(depth, other_half)],
        out_shape=[like((L // 2, depth), full), like((L // 2, depth))],
        compiler_params=params(),
        cost_estimate=SHORT,
        name="project_back",
    )(*grads, weight, *later)


def input_back_kernel(tokens, grad_own, grad_other, dresid, gain, result):
    grads = grad_own[...] + grad_other[...].astype(full)
    unit, scale = normalized(tokens[...].astype(full))
    result[...] = dresid[...] + norm_back(unit, scale, gain[...], grads)


def input_back(tokens, grad_own, grad_other, dresid, gain):
    height, depth = tokens.shape
    return pl.pallas_call(
        input_back_kernel,
        grid=(height // ROWS,),
        in_specs=[rows_of(depth)] * 4 + [whole((1, depth))],
        out_specs=rows_of(depth),
        out_shape=like((height, depth), full),
        compiler_params=params(),
        cost_estimate=SHORT,
        name="input_back",
    )(tokens, grad_own, grad_other, dresid, gain)


def adamw(weight, grad, first, second, rate, decay):
    first_new = beta_one * first + (1.0 - beta_one) * grad
    second_new = beta_two * second + (1.0 - beta_two) * grad * grad
    step_size = (
        first_new
        / (1.0 - beta_one**STEP)
        / (jnp.sqrt(second_new / (1.0 - beta_two**STEP)) + adam_eps)
    )
    return (weight - rate * (step_size + decay * weight), first_new, second_new)


def step_kernel(counts, flipped, spans, column_at, *refs):
    totals, used = [], 0
    for count in counts:
        total = refs[used][...].astype(full)
        for piece in refs[used + 1 : used + count]:
            total = total + piece[...].astype(full)
        totals.append(total)
        used += count
    rest, count = refs[used:], len(spans)
    states, outs = rest[: 3 * count], rest[3 * count : 7 * count]
    scratch = rest[7 * count + 1 :]
    rows = totals[0].shape[0]
    column = None
    for group, start in column_at:
        term = totals[group][:, start : start + SPARE]
        column = term if column is None else column + term
    rest[7 * count][...] = column
    for at, span in enumerate(spans):
        weight, first, second = states[3 * at : 3 * at + 3]
        grad_out, weight_out, first_out, second_out = outs[4 * at : 4 * at + 4]
        for part, slices in enumerate(span):
            pieces = [totals[group][:, start : start + size] for group, start, size in slices]
            grad = pieces[0] if len(pieces) == 1 else jnp.concatenate(pieces, axis=1)
            width = grad.shape[1]
            if flipped[at]:
                padded = scratch[at]
                padded[...] = jnp.zeros_like(padded)
                padded[0:rows, 0:width] = grad
                grad = padded[...].T[0:width, 0:rows]
                where = Ellipsis
            else:
                where = part
            new = adamw(
                weight[where], grad, first[where], second[where], weight_rate, weight_decay
            )
            grad_out[where] = grad
            weight_out[where], first_out[where], second_out[where] = new


def step(groups, spans, states, flipped, column_at, later=()):
    shapes, scratch = [], []
    for (weight, _, _), span, flip in zip(states, spans, flipped):
        shapes += [like(weight.shape, full)] * 4
        lanes = -(-sum(size for _, _, size in span[0]) // 128) * 128
        scratch.append(pltpu.VMEM((128, lanes) if flip else (8, 128), full))
    shapes.append(like((groups[0][0].shape[0], SPARE), full))
    flat = [array for state in states for array in state]
    results = call(
        functools.partial(step_kernel, [len(group) for group in groups], flipped, spans, column_at),
        "step",
        [piece for group in groups for piece in group] + flat,
        shapes,
        later=later,
        scratch=scratch,
    )
    return [results[4 * at : 4 * at + 4] for at in range(len(states))] + [results[-1]]


def shards(
    tokens,
    cotangent,
    w_qkv,
    w_attn_out,
    w_in,
    w_mlp_out,
    gains,
    first_qkv,
    first_attn_out,
    first_in,
    first_mlp_out,
    first_gains,
    second_qkv,
    second_attn_out,
    second_in,
    second_mlp_out,
    second_gains,
):
    count = lax.axis_size("dp")
    fast = staged(count)
    core = lax.axis_index("tensor") % 2
    head_width = w_qkv.shape[2]
    unit_width = w_in.shape[2]
    depth = tokens.shape[1]
    qkv_layouts = [sum((head_layout(part * head_width, head_width) for part in range(3)), [])]
    gains_at = 3 * head_width
    gate_at, up_at, down_at = (head_width + part * unit_width for part in range(3))
    rest_layouts = [
        head_layout(0, head_width),
        unit_layout(gate_at, unit_width) + unit_layout(up_at, unit_width),
        unit_layout(down_at, unit_width),
    ]

    shard_one = pack(w_qkv, gains)
    shard_two = pack_rest(w_attn_out, w_in, w_mlp_out, [shard_one])
    cosine, sine = rope_tables(core * (L // 2))

    def halves(shard, along):
        half = shard.shape[0] // 2
        pieces = [shard] + along
        return jnp.stack([p[:half] for p in pieces]), jnp.stack([p[half:] for p in pieces])

    if fast:
        along_one = [z_shift(shard_one, count, jump) for jump in (1, 2, 3)]
        x_other = core_swap(tokens)
        za, zb = halves(after(shard_one, shard_two, x_other, cosine, sine), along_one)
        shard_two = after(shard_two, *along_one)
        along_two = [z_shift(shard_two, count, jump) for jump in (1, 2, 3)]
        xa, yb = x_swap(za, count), y_swap(zb)
        both_a, both_b = jnp.stack([za, xa]), jnp.stack([zb, yb])
        ya, xb = y_swap(both_a), x_swap(both_b, count)
        first_pieces = [za, xa, ya, zb, yb, xb]
        za, zb = halves(shard_two, [after(piece, both_a, both_b) for piece in along_two])
        w_qkv_all, gains_all = assemble(
            first_pieces, qkv_layouts, depth, gains_at, later=[za, zb]
        )
    else:
        x_other = core_swap(tokens)
        w_qkv_all, gains_all = gathered_plainly(shard_one, qkv_layouts, gains_at)
    gain_one, gain_two = gains_all[0:1], gains_all[1:2]
    if fast:
        xa, yb = x_swap(za, count), y_swap(zb)
    normed_one, query, key, value = project(tokens, x_other, gain_one, w_qkv_all, cosine, sine)
    if fast:
        xa, yb = after(xa, query), after(yb, query)
        ya, xb = y_swap(jnp.stack([za, xa])), x_swap(jnp.stack([zb, yb]), count)
    dy_other = core_swap(after(cotangent, query))
    mixed, lse = attend(query, key, value)
    mixed_other = core_swap(mixed)
    if fast:
        ya, xb = after(ya, mixed), after(xb, mixed)
        wo, w_both, w_down = assemble([za, xa, ya, zb, yb, xb], rest_layouts, depth)
    else:
        wo, w_both, w_down = gathered_plainly(shard_two, rest_layouts)
    wo_other = core_swap(wo)
    normed_two, scale_two, hidden, dboth, out_own, out_other, dnormed = feed_forward(
        mixed,
        mixed_other,
        tokens,
        x_other,
        cotangent,
        dy_other,
        gain_two,
        wo,
        wo_other,
        w_both,
        w_down,
    )
    units = w_down.shape[1]
    dnormed_other = core_swap(dnormed)
    grad_1 = weight_grad(
        [normed_two, dboth, cotangent, dy_other, hidden],
        [
            ((0,), (1,), [(0, unit_width, unit_width), (units, units + unit_width, unit_width)]),
            ((2, 3), (4,), [(0, unit_width, unit_width)]),
        ],
        count,
        w_both,
        [(0, 2 * units)],
    )
    if fast:
        from_y, from_x = y_swap(grad_1[1]), x_swap(grad_1[3], count)
    output = (out_own + core_swap(out_other).astype(full)).astype(low)
    dresid, dresid_low, dmixed = resid_back(
        normed_two,
        scale_two,
        dnormed,
        dnormed_other,
        cotangent,
        dy_other,
        gain_two,
        wo,
        later=grad_1[:1],
    )
    bundle = (query, key, value, mixed, dmixed, lse, cosine, sine)
    pair_0 = attend_back(0, *bundle, later=[output])
    pair_2 = attend_back(2, *bundle, later=pair_0[:1])
    if fast:
        sums_1 = add_first([(grad_1[0], from_y, grad_1[2], from_x)], later=pair_2[:1])
        next_a, next_b = x_swap(sums_1[1], count), y_swap(sums_1[3])
    grad_2 = weight_grad(
        [normed_one, *(group[part] for part in range(3) for group in (pair_0, pair_2)), dresid_low, mixed],
        [
            ((0,), tuple(range(1, 7)), [(2 * part * PAIR, (2 * part + 1) * PAIR, PAIR) for part in range(3)]),
            ((7,), (8,), [(0, 2 * PAIR, PAIR), (PAIR, PAIR + HD, HD)]),
        ],
        count,
        w_qkv_all,
        [(part * 3 * PAIR + at * PAIR, PAIR) for part in range(3) for at in (0, 2)],
        later=[sums_1[1], sums_1[3]] if fast else pair_2[:1],
    )
    if fast:
        from_y2, from_x2 = y_swap(grad_2[1]), x_swap(grad_2[3], count)
    pair_1 = attend_back(1, *bundle, later=grad_2[:1])
    if fast:
        merged = add_second(sums_1[0], next_a, sums_1[2], next_b, later=pair_1[:1])
        pieces_1 = across_z(merged, count)
    grad_3 = weight_grad(
        [normed_one, *pair_1],
        [((0,), (1, 2, 3), [(part * PAIR, part * PAIR + HD, HD) for part in range(3)])],
        count,
        w_qkv_all,
        [(part * 3 * PAIR + PAIR, PAIR) for part in range(3)],
        later=merged[:1] if fast else (),
    )
    trios = [group[part] for part in range(3) for group in (pair_0, pair_1, pair_2)]
    grad_one, grad_one_low = project_back(trios, w_qkv_all, later=grad_3[:1])
    if fast:
        from_y3, from_x3 = y_swap(grad_3[1]), x_swap(grad_3[3], count)
        from_y2, from_x2 = after(from_y2, grad_one), after(from_x2, grad_one)
        from_y3, from_x3 = after(from_y3, grad_one), after(from_x3, grad_one)
        sums_2 = add_first(
            [(grad_2[0], from_y2, grad_2[2], from_x2), (grad_3[0], from_y3, grad_3[2], from_x3)]
        )
        next_a, next_b = x_swap(sums_2[1], count), y_swap(sums_2[3])
        grad_one_low = after(grad_one_low, sums_2[1], sums_2[3])
    else:
        pieces_1 = reduced_plainly(*grad_1)
    grad_other = core_swap(grad_one_low)
    grad_inputs = input_back(tokens, grad_one, grad_other, dresid, gain_one)
    new_in, new_down, column_two = step(
        [pieces_1],
        [
            [[(0, 0, unit_width)], [(0, unit_width, unit_width)]],
            [[(0, 2 * unit_width, unit_width)]],
        ],
        [(w_in, first_in, second_in), (w_mlp_out, first_mlp_out, second_mlp_out)],
        (False, True),
        [(0, 3 * unit_width)],
        later=[grad_inputs],
    )
    if fast:
        next_a, next_b = after(next_a, grad_inputs), after(next_b, grad_inputs)
        pieces_2 = across_z(add_second(sums_2[0], next_a, sums_2[2], next_b), count)
    else:
        joined = [jnp.concatenate(pair, axis=1) for pair in zip(grad_2[:2], grad_3[:2])]
        pieces_2 = reduced_plainly(*joined)
    split = grad_2[0].shape[-1]
    new_qkv, new_attn, column_one = step(
        [pieces_2],
        [
            [[(0, part * PAIR, PAIR), (0, split + part * HD, HD)] for part in range(3)],
            [[(0, 3 * PAIR, head_width)]],
        ],
        [(w_qkv, first_qkv, second_qkv), (w_attn_out, first_attn_out, second_attn_out)],
        (False, True),
        [(0, split - SPARE), (0, split + 3 * HD)],
    )
    sums = jnp.concatenate([column_one[:, :1], column_two[:, :1]], axis=1)
    shard_gain = (sums + core_swap(sums)).T / gains
    new_gain = adamw(gains, shard_gain, first_gains, second_gains, gain_rate, 0.0)
    return (
        output,
        grad_inputs,
        new_qkv[0],
        new_attn[0],
        new_in[0],
        new_down[0],
        shard_gain,
        new_qkv[1],
        new_attn[1],
        new_in[1],
        new_down[1],
        new_gain[0],
        new_qkv[2],
        new_attn[2],
        new_in[2],
        new_down[2],
        new_gain[1],
        new_qkv[3],
        new_attn[3],
        new_in[3],
        new_down[3],
        new_gain[2],
    )


def solution(mesh):
    return jax.shard_map(
        shards,
        mesh=mesh,
        in_specs=(
            P(("dp", "tensor"), None),
            P(("dp", "tensor"), None),
            P(None, "dp", "tensor"),
            P("tensor", "dp"),
            P(None, "dp", "tensor"),
            P("tensor", "dp"),
            P(None, "dp"),
            P(None, "dp", "tensor"),
            P("tensor", "dp"),
            P(None, "dp", "tensor"),
            P("tensor", "dp"),
            P(None, "dp"),
            P(None, "dp", "tensor"),
            P("tensor", "dp"),
            P(None, "dp", "tensor"),
            P("tensor", "dp"),
            P(None, "dp"),
        ),
        out_specs=(
            P(("dp", "tensor"), None),
            P(("dp", "tensor"), None),
            P(None, "dp", "tensor"),
            P("tensor", "dp"),
            P(None, "dp", "tensor"),
            P("tensor", "dp"),
            P(None, "dp"),
            P(None, "dp", "tensor"),
            P("tensor", "dp"),
            P(None, "dp", "tensor"),
            P("tensor", "dp"),
            P(None, "dp"),
            P(None, "dp", "tensor"),
            P("tensor", "dp"),
            P(None, "dp", "tensor"),
            P("tensor", "dp"),
            P(None, "dp"),
            P(None, "dp", "tensor"),
            P("tensor", "dp"),
            P(None, "dp", "tensor"),
            P("tensor", "dp"),
            P(None, "dp"),
        ),
        check_vma=False,
    )
```

```python
import functools

import jax
import jax.numpy as jnp
import numpy as np
from jax import lax
from jax.experimental import pallas as pl
from jax.experimental.pallas import tpu as pltpu
from jax.sharding import PartitionSpec as P

HD = 64
L = 1024
STEP = 10


eps_norm = 1e-05
rope_base = 160000.0
beta_one = 0.9
beta_two = 0.98
adam_eps = 1e-06
weight_rate = 0.02
gain_rate = 0.2
weight_decay = 0.01

low = jnp.bfloat16
full = jnp.float32
ROWS = 512
CHUNK = 256
PAIR = 2 * HD
VMEM_BYTES = 52 << 20
SPARE = 64
PACE = 800_000_000


def pace(microseconds):
    return pl.CostEstimate(flops=int(microseconds * PACE), bytes_accessed=0, transcendentals=0)


def dot(left, right, left_dim, right_dim):
    return lax.dot_general(
        left, right, (((left_dim,), (right_dim,)), ((), ())), preferred_element_type=full
    )


def params():
    return pltpu.CompilerParams(vmem_limit_bytes=VMEM_BYTES)


def whole(shape):
    return pl.BlockSpec(shape, lambda *_: (0,) * len(shape))


def rows_of(width, index=lambda i: i):
    return pl.BlockSpec((ROWS, width), lambda i: (index(i), 0))


def own_half(i):
    return jnp.minimum(i, L // ROWS // 2 - 1)


def other_half(i):
    return jnp.maximum(i - L // ROWS // 2, 0)


def swapped(i):
    return (i + L // ROWS // 2) % (L // ROWS)


def is_own(i):
    return i < L // ROWS // 2


def core_swap(array):
    return lax.ppermute(array, "tensor", [(t, t ^ 1) for t in range(4)])


def y_swap(array):
    return lax.ppermute(array, "tensor", [(t, t ^ 2) for t in range(4)])


def x_swap(array, count):
    return lax.ppermute(array, "dp", [(d, d ^ 1) for d in range(count)])


def z_shift(array, count, step):
    around = count // 2
    return lax.ppermute(
        array, "dp", [(d, (d // 2 + step) % around * 2 + d % 2) for d in range(count)]
    )


def staged(count):
    return count == 8


def after(array, *others):
    return lax.optimization_barrier((array, *others))[0]


ANY = pl.BlockSpec(memory_space=pl.ANY)
LOCAL = pl.BlockSpec(memory_space=pltpu.VMEM)
SCALAR = pl.BlockSpec(memory_space=pltpu.SMEM)


TIMES = {"weight_grad": 6, "assemble": 3, "step": 2, "pack": 1, "pack_rest": 1, "add_first": 2, "add_second": 1}


def call(kernel, name, ins, shapes, later=(), place=None, scratch=()):
    head = [] if place is None else [place]
    lead, skip = len(head), len(later)

    def body(*refs):
        kernel(*refs[: lead + len(ins)], *refs[lead + len(ins) + skip :])

    return pl.pallas_call(
        body,
        in_specs=[SCALAR] * lead + [LOCAL] * len(ins) + [ANY] * skip,
        out_specs=[LOCAL] * len(shapes),
        out_shape=shapes,
        scratch_shapes=list(scratch),
        compiler_params=params(),
        cost_estimate=pace(TIMES[name]),
        name=name,
    )(*head, *ins, *later)


def like(shape, kind=low):
    return jax.ShapeDtypeStruct(shape, kind)


def pack_kernel(w_qkv, gains, shard, padded):
    rows = w_qkv.shape[1]
    padded[...] = jnp.zeros_like(padded)
    padded[0 : gains.shape[0], 0:rows] = gains[...]
    columns = padded[...].T[0:rows, 0:2]
    high = columns.astype(low)
    rest = columns - high.astype(full)
    middle = rest.astype(low)
    last = (rest - middle.astype(full)).astype(low)
    filler = jnp.zeros((rows, SPARE - 6), full)
    pieces = [w_qkv[part] for part in range(3)]
    shard[...] = jnp.concatenate(
        pieces + [high.astype(full), middle.astype(full), last.astype(full), filler], axis=1
    ).astype(low)


def pack(w_qkv, gains):
    rows, width = w_qkv.shape[1:]
    return call(
        pack_kernel,
        "pack",
        [w_qkv, gains],
        [like((rows, 3 * width + SPARE))],
        scratch=[pltpu.VMEM((128, 128), full)],
    )[0]


def pack_rest_kernel(w_attn_out, w_in, w_mlp_out, shard, wide):
    rows = w_in.shape[1]
    flipped = []
    for weight in (w_attn_out, w_mlp_out):
        wide[...] = jnp.zeros_like(wide)
        wide[0 : weight.shape[0], 0:rows] = weight[...]
        flipped.append(wide[...].T[0:rows, 0 : weight.shape[0]])
    pieces = [flipped[0], w_in[0], w_in[1], flipped[1]]
    shard[...] = jnp.concatenate(pieces, axis=1).astype(low)


def pack_rest(w_attn_out, w_in, w_mlp_out, later):
    rows, units = w_in.shape[1:]
    heads = w_attn_out.shape[0]
    return call(
        pack_rest_kernel,
        "pack_rest",
        [w_attn_out, w_in, w_mlp_out],
        [like((rows, heads + 3 * units))],
        later=later,
        scratch=[pltpu.VMEM((-(-units // 128) * 128, 128), full)],
    )[0]


def unpack_gains(columns):
    wide = jnp.concatenate([columns.astype(full), jnp.zeros(columns.shape, full)], axis=1).T
    return wide[0:2] + wide[2:4] + wide[4:6]


def columns_of(layout, own, other):
    pieces = []
    for item in layout:
        if item is None:
            pieces.append(jnp.zeros((own.shape[0], SPARE), own.dtype))
        else:
            side, start, width = item
            pieces.append((own, other)[side][:, start : start + width])
    return jnp.concatenate(pieces, axis=1)


def layout_width(layout):
    return sum(SPARE if item is None else item[2] for item in layout)


def head_layout(start, width):
    first = width // 3 * 2
    return [(0, start, width), (1, start + first, width - first), (1, start, first)]


def unit_layout(start, width):
    return [(0, start, width), (1, start, width), None]


def assemble_kernel(layouts, flips, gains_at, place_ref, za, xa, ya, zb, yb, xb, *outs):
    place = place_ref[0]
    half = za.shape[1]
    for jx in range(2):
        for jz in range(4):
            source = (place // 2 + 4 - jz) % 4 * 2 + (place % 2 + jx) % 2
            own_a = (za, xa)[jx][jz]
            other_a = ya[jx, jz]
            own_b = zb[jz] if jx == 0 else xb[0, jz]
            other_b = yb[jz] if jx == 0 else xb[1, jz]
            for part, (own, other) in enumerate(((own_a, other_a), (own_b, other_b))):
                start = pl.multiple_of(source * 2 * half + part * half, half)
                for layout, out in zip(layouts, outs):
                    out[pl.ds(start, half), :] = columns_of(layout, own, other)
                if gains_at is not None:
                    outs[-1][pl.ds(start, half), :] = own[:, gains_at : gains_at + SPARE]
    for at, flip in enumerate(flips):
        outs[len(layouts) + at][...] = outs[flip][...].T
    if gains_at is not None:
        outs[-2][...] = unpack_gains(outs[-1][...])


def assemble(pieces, layouts, depth, flips=(), gains_at=None, later=()):
    place = lax.axis_index("dp").astype(jnp.int32)[None]
    shapes = [like((depth, layout_width(layout))) for layout in layouts]
    shapes += [like((layout_width(layouts[flip]), depth)) for flip in flips]
    scratch = []
    if gains_at is not None:
        shapes.append(like((2, depth), full))
        scratch.append(pltpu.VMEM((depth, SPARE), low))
    return call(
        functools.partial(assemble_kernel, layouts, flips, gains_at),
        "assemble",
        pieces,
        shapes,
        later=later,
        place=place,
        scratch=scratch,
    )


def gathered_plainly(shard, layouts, flips=(), gains_at=None):
    own = lax.all_gather(shard, "dp", axis=0, tiled=True)
    other = y_swap(own)
    results = [columns_of(layout, own, other) for layout in layouts]
    results += [results[flip].T for flip in flips]
    if gains_at is not None:
        results.append(unpack_gains(own[:, gains_at : gains_at + SPARE]))
    return results


def stacked(ins, at, axis):
    parts = [ins[index][...] for index in at]
    return parts[0] if len(parts) == 1 else jnp.concatenate(parts, axis=axis)


def weight_grad_kernel(products, fast, weights, ins, place_ref, refs):
    outs, scratch = (refs[:4], refs[4:]) if fast else (refs[:2], refs[2:])
    place = place_ref[0]
    for index, (held, (left, right, _)) in enumerate(zip(scratch, products)):
        grad = dot(stacked(ins, left, 0), stacked(ins, right, 1), 0, 0)
        held[...] = grad
        if weights and index == 0:
            weight = [ins[-1][:, start : start + width] for start, width in weights]
            weight = weight[0] if len(weight) == 1 else jnp.concatenate(weight, axis=1)
            sums = jnp.sum(weight.astype(full) * grad, axis=1, keepdims=True)
            scratch[-1][...] = jnp.broadcast_to(sums, (sums.shape[0], 128))

    def split(rows):
        sides = [[], []]
        for held, (_, _, spans) in zip(scratch, products):
            values = held[rows, :]
            for *starts, width in spans:
                for side, start in zip(sides, starts):
                    side.append(values[:, start : start + width])
        if weights:
            for side in sides:
                side.append(scratch[-1][rows, :][:, :SPARE])
        return [jnp.concatenate(side, axis=1).astype(low) for side in sides]

    if not fast:
        outs[0][...], outs[1][...] = split(slice(None))
        return
    size = outs[0].shape[2]
    for jx in range(2):
        for jz in range(4):
            target = (place // 2 + jz) % 4 * 2 + (place % 2 + jx) % 2
            for part in range(2):
                start = pl.multiple_of((target * 2 + part) * size, size)
                own, other = split(pl.ds(start, size))
                if part == 0:
                    outs[0][jx, jz] = own
                    outs[1][jx, jz] = other
                else:
                    outs[2 + jx][0, jz] = own
                    outs[2 + jx][1, jz] = other


def weight_grad(arrays, products, count, weight=None, lanes=(), later=()):
    depth = arrays[products[0][0][0]].shape[1]
    widths = [sum(arrays[at].shape[1] for at in right) for _, right, _ in products]
    total = sum(span[2] for _, _, spans in products for span in spans)
    total += SPARE if weight is not None else 0
    fast = staged(count)
    if fast:
        shapes = [like((2, 4, depth // count // 2, total))] * 4
    else:
        shapes = [like((depth, total))] * 2
    place = lax.axis_index("dp").astype(jnp.int32)[None]
    ins = list(arrays) + ([] if weight is None else [weight])
    weights = [] if weight is None else list(lanes)
    held = [pltpu.VMEM((depth, width), full) for width in widths]
    if weights:
        held.append(pltpu.VMEM((depth, 128), full))

    def kernel(place_ref, *refs):
        weight_grad_kernel(
            products, fast, weights, refs[: len(ins)], place_ref, refs[len(ins) :]
        )

    return call(
        kernel,
        "weight_grad",
        ins,
        shapes,
        later=later,
        place=place,
        scratch=held,
    )


def reduced_plainly(own, other):
    summed = own.astype(full) + y_swap(other).astype(full)
    return [lax.psum_scatter(summed, "dp", scatter_dimension=0, tiled=True)]


def add_kernel(groups, *refs):
    ins, outs = refs[: 4 * groups], refs[4 * groups :]
    for half in range(2):
        for side in range(2):
            sums = []
            for group in range(groups):
                here, there = ins[4 * group + 2 * half : 4 * group + 2 * half + 2]
                sums.append((here[side].astype(full) + there[side].astype(full)).astype(low))
            out = outs[2 * half + side]
            out[...] = sums[0] if groups == 1 else jnp.concatenate(sums, axis=-1)


def add_first(groups, later=()):
    rows = groups[0][0].shape[2]
    width = sum(group[0].shape[3] for group in groups)
    return call(
        functools.partial(add_kernel, len(groups)),
        "add_first",
        [array for group in groups for array in group],
        [like((4, rows, width))] * 4,
        later=later,
    )


def merge_kernel(here_a, there_a, here_b, there_b, *outs):
    for jump, out in enumerate(outs):
        part_a = here_a[jump].astype(full) + there_a[jump].astype(full)
        part_b = here_b[jump].astype(full) + there_b[jump].astype(full)
        out[...] = jnp.concatenate([part_a.astype(low), part_b.astype(low)], axis=0)


def add_second(here_a, there_a, here_b, there_b, later=()):
    _, rows, width = here_a.shape
    return call(
        merge_kernel,
        "add_second",
        [here_a, there_a, here_b, there_b],
        [like((2 * rows, width))] * 4,
        later=later,
    )


def across_z(parts, count):
    return [parts[0]] + [z_shift(parts[step], count, step) for step in (1, 2, 3)]


def normalized(values):
    centred = values - jnp.mean(values, axis=-1, keepdims=True)
    spread = jnp.mean(centred * centred, axis=-1, keepdims=True)
    scale = lax.rsqrt(spread + eps_norm)
    return centred * scale, scale


def norm_back(unit, scale, gains, grads):
    inner = grads * gains
    mean_inner = jnp.mean(inner, axis=-1, keepdims=True)
    mean_unit = jnp.mean(inner * unit, axis=-1, keepdims=True)
    return scale * (inner - mean_inner - unit * mean_unit)


def rope_tables(offset):
    half_width = HD // 2
    frequency = rope_base ** (-(jnp.arange(half_width, dtype=full) * 2.0 / HD))
    position = ((jnp.arange(L) + offset) % L).astype(full)
    angles = position[:, None] * frequency[None, :]
    cosine, sine = jnp.cos(angles), jnp.sin(angles)
    return (
        jnp.concatenate([cosine] * 4, axis=1),
        jnp.concatenate([-sine, sine, -sine, sine], axis=1),
    )


def turn(values, cosine, sine):
    lane = lax.broadcasted_iota(jnp.int32, values.shape, 1)
    ahead = pltpu.roll(values, PAIR - HD // 2, 1)
    behind = pltpu.roll(values, HD // 2, 1)
    turned = jnp.where(lane % HD < HD // 2, ahead, behind)
    return values * cosine + turned * sine


def qkv_kernel(x_own, x_other, gain, weight, cosine, sine, normed, q_out, k_out, v_out, raw):
    own = is_own(pl.program_id(0))
    unit, _ = normalized(jnp.where(own, x_own[...], x_other[...]).astype(full))
    rows = (unit * gain[...]).astype(low)
    normed[...] = rows
    raw[...] = dot(rows, weight[...], 1, 0)
    width = q_out.shape[1]
    near, far = cosine[...], sine[...]
    for start in range(0, width, PAIR):
        lanes = slice(start, start + PAIR)
        query = turn(raw[:, lanes], near, far).astype(low)
        q_out[:, lanes] = query * jnp.asarray(HD ** (-0.5), low)
        key = raw[:, width + start : width + start + PAIR]
        k_out[:, lanes] = turn(key, near, far).astype(low)
    v_out[...] = raw[:, 2 * width :].astype(low)


def project(x_own, x_other, gain, weight, cosine, sine):
    depth, total = weight.shape
    width = total // 3
    return pl.pallas_call(
        qkv_kernel,
        grid=(L // ROWS,),
        in_specs=[
            rows_of(depth, own_half),
            rows_of(depth, other_half),
            whole((1, depth)),
            whole((depth, total)),
            rows_of(PAIR),
            rows_of(PAIR),
        ],
        out_specs=[rows_of(depth), rows_of(width), rows_of(width), rows_of(width)],
        out_shape=[like((L, depth))] + [like((L, width))] * 3,
        scratch_shapes=[pltpu.VMEM((ROWS, total), full)],
        compiler_params=params(),
        cost_estimate=pace(6),
        name="project",
    )(x_own, x_other, gain, weight, cosine, sine)


def head_masks(height):
    lane = lax.broadcasted_iota(jnp.int32, (height, PAIR), 1)
    return [(lane // HD == head).astype(full).astype(low) for head in range(2)]


def flat_heads(rows):
    flat = rows.astype(full).T
    head_of = lax.broadcasted_iota(jnp.int32, flat.shape, 0) // HD
    return [jnp.where(head_of == head, flat, 0.0).astype(low) for head in range(2)]


def attend_kernel(q_ref, k_ref, v_ref, mixed, lse_ref):
    flat_keys, values = flat_heads(k_ref[...]), v_ref[...]
    lane = lax.broadcasted_iota(jnp.int32, (CHUNK, PAIR), 1)
    for start in range(0, L, CHUNK):
        rows = slice(start, start + CHUNK)
        query = q_ref[rows, :]
        results = []
        for head in range(2):
            scores = dot(query, flat_keys[head], 1, 0)
            row_max = jnp.max(scores, axis=1, keepdims=True)
            raised = jnp.exp(scores - row_max)
            total = jnp.sum(raised, axis=1, keepdims=True)
            results.append(dot(raised.astype(low), values, 1, 0) / total)
            lse = jnp.broadcast_to(row_max + jnp.log(total), (CHUNK, PAIR))
            lse_ref[0, head : head + 1, rows] = lse.T[0:1]
        mixed[rows, :] = jnp.where(lane < HD, results[0], results[1]).astype(low)


def attend(query, key, value):
    width = query.shape[1]
    pairs = width // PAIR
    block = pl.BlockSpec((L, PAIR), lambda i: (0, i))
    totals = pl.BlockSpec((1, 2, L), lambda i: (i, 0, 0))
    return pl.pallas_call(
        attend_kernel,
        grid=(pairs,),
        in_specs=[block] * 3,
        out_specs=[block, totals],
        out_shape=[
            jax.ShapeDtypeStruct((L, width), low),
            jax.ShapeDtypeStruct((pairs, 2, L), full),
        ],
        compiler_params=params(),
        cost_estimate=pace(13),
        name="attend",
    )(query, key, value)


def attend_back_kernel(
    q_ref, k_ref, v_ref, o_ref, grad_ref, lse_ref, cosine, sine, dq_out, dk_out, dv_out, dk, dv
):
    masks = head_masks(L)
    chunk_masks = head_masks(CHUNK)
    keys, values = k_ref[...], v_ref[...]
    head_keys = [keys * mask for mask in masks]
    head_values = [values * mask for mask in masks]
    flipped_keys = flat_heads(keys)
    flat_query = q_ref[...].astype(full).T.astype(low)
    flat_grad = grad_ref[...].astype(full).T.astype(low)
    product = (grad_ref[...].astype(full) * o_ref[...].astype(full)).T
    inner = [jnp.sum(product[head * HD : (head + 1) * HD], axis=0, keepdims=True) for head in range(2)]
    for start in range(0, L, CHUNK):
        rows = slice(start, start + CHUNK)
        query, grad = q_ref[rows, :], grad_ref[rows, :]
        dq = None
        for head in range(2):
            scores = dot(head_keys[head], flat_query[:, rows], 1, 0)
            probs = jnp.exp(scores - lse_ref[0, head : head + 1, rows])
            grad_probs = dot(head_values[head], flat_grad[:, rows], 1, 0)
            grad_scores = (probs * (grad_probs - inner[head][:, rows])).astype(low)
            add_v = dot(probs.astype(low), grad * chunk_masks[head], 1, 0)
            add_k = dot(grad_scores, query * chunk_masks[head], 1, 0)
            add_q = dot(flipped_keys[head], grad_scores, 1, 0)
            dq = add_q if dq is None else dq + add_q
            if start == 0 and head == 0:
                dv[...] = add_v
                dk[...] = add_k
            else:
                dv[...] += add_v
                dk[...] += add_k
        dq_out[rows, :] = turn(dq.T * HD ** (-0.5), cosine[rows, :], -sine[rows, :]).astype(low)
    dk_out[...] = turn(dk[...], cosine[...], -sine[...]).astype(low)
    dv_out[...] = dv[...].astype(low)


def attend_back(pair, query, key, value, mixed, grad, lse, cosine, sine, later=()):
    block = pl.BlockSpec((L, PAIR), lambda i: (0, pair))
    result = pl.BlockSpec((L, PAIR), lambda i: (0, 0))
    totals = pl.BlockSpec((1, 2, L), lambda i: (pair, 0, 0))
    skip = len(later)

    def body(*refs):
        attend_back_kernel(*refs[:8], *refs[8 + skip :])

    return pl.pallas_call(
        body,
        grid=(1,),
        in_specs=[block] * 5 + [totals] + [whole((L, PAIR))] * 2 + [ANY] * skip,
        out_specs=[result] * 3,
        out_shape=[like((L, PAIR))] * 3,
        scratch_shapes=[pltpu.VMEM((L, PAIR), full)] * 2,
        compiler_params=params(),
        cost_estimate=pace(7),
        name="attend_back",
    )(query, key, value, mixed, grad, lse, cosine, sine, *later)


def feed_forward_kernel(
    mixed_own,
    mixed_other,
    x_own,
    x_other,
    dy_own,
    dy_other,
    gain,
    wo_own,
    wo_other,
    w_both,
    w_both_flat,
    w_down,
    w_down_flat,
    normed,
    scale_out,
    hidden_out,
    dboth_out,
    out_own,
    out_other,
    dnormed,
):
    own = is_own(pl.program_id(0))
    units = w_down.shape[0]
    tokens = jnp.where(own, x_own[...], x_other[...]).astype(full)
    resid = (
        tokens + dot(mixed_own[...], wo_own[...], 1, 0) + dot(mixed_other[...], wo_other[...], 1, 0)
    )
    unit, scale = normalized(resid)
    rows = (unit * gain[...]).astype(low)
    normed[...] = rows
    scale_out[...] = jnp.broadcast_to(scale, scale_out.shape)
    both = dot(rows, w_both[...], 1, 0)
    gate, up = both[:, :units], both[:, units:]
    cumulative = 0.5 + 0.5 * lax.erf(gate * np.float32(0.5**0.5))
    density = jnp.exp(gate * gate * -0.5) * np.float32((2.0 * np.pi) ** -0.5)
    activated = gate * cumulative
    hidden = (activated * up).astype(low)
    hidden_out[...] = hidden
    part = dot(hidden, w_down[...], 1, 0)
    dhidden = dot(jnp.where(own, dy_own[...], dy_other[...]), w_down_flat[...], 1, 0)
    dgate = (dhidden * up * (cumulative + gate * density)).astype(low)
    dup = (dhidden * activated).astype(low)
    dboth = jnp.concatenate([dgate, dup], axis=1)
    dboth_out[...] = dboth
    dnormed[...] = dot(dboth, w_both_flat[...], 1, 0).astype(low)

    @pl.when(own)
    def _():
        out_own[...] = resid + part

    @pl.when(jnp.logical_not(own))
    def _():
        out_other[...] = part.astype(low)


def feed_forward(*arrays):
    width, depth = arrays[7].shape
    units = arrays[11].shape[0]
    half = L // 2
    return pl.pallas_call(
        feed_forward_kernel,
        grid=(L // ROWS,),
        in_specs=[
            rows_of(width),
            rows_of(width, swapped),
            rows_of(depth, own_half),
            rows_of(depth, other_half),
            rows_of(depth, own_half),
            rows_of(depth, other_half),
            whole((1, depth)),
            whole((width, depth)),
            whole((width, depth)),
            whole((depth, 2 * units)),
            whole((2 * units, depth)),
            whole((units, depth)),
            whole((depth, units)),
        ],
        out_specs=[
            rows_of(depth),
            rows_of(128),
            rows_of(units),
            rows_of(2 * units),
            rows_of(depth, own_half),
            rows_of(depth, other_half),
            rows_of(depth),
        ],
        out_shape=[
            like((L, depth)),
            like((L, 128), full),
            like((L, units)),
            like((L, 2 * units)),
            like((half, depth), full),
            like((half, depth)),
            like((L, depth)),
        ],
        compiler_params=params(),
        cost_estimate=pace(18),
        name="feed_forward",
    )(*arrays)


def resid_back_kernel(
    normed, scale_ref, grad_own, grad_other, dy_own, dy_other, gain, wo, dresid, dresid_low, dmixed
):
    own = is_own(pl.program_id(0))
    inverse = 1.0 / gain[...]
    pull = jnp.where(own, dy_own[...], dy_other[...]).astype(full)
    grads = grad_own[...].astype(full) + grad_other[...].astype(full)
    unit = normed[...].astype(full) * inverse
    total = pull + norm_back(unit, scale_ref[:, 0:1], gain[...], grads)
    rounded = total.astype(low)
    dresid_low[...] = rounded
    dmixed[...] = dot(rounded, wo[...], 1, 0).astype(low)

    @pl.when(own)
    def _():
        dresid[...] = total


def resid_back(normed, scale, grad_own, grad_other, dy_own, dy_other, gain, wo, later=()):
    depth, width = wo.shape
    skip = len(later)

    def body(*refs):
        resid_back_kernel(*refs[:8], *refs[8 + skip :])

    return pl.pallas_call(
        body,
        grid=(L // ROWS,),
        in_specs=[
            rows_of(depth),
            rows_of(128),
            rows_of(depth),
            rows_of(depth, swapped),
            rows_of(depth, own_half),
            rows_of(depth, other_half),
            whole((1, depth)),
            whole((depth, width)),
        ]
        + [ANY] * skip,
        out_specs=[rows_of(depth, own_half), rows_of(depth), rows_of(width)],
        out_shape=[like((L // 2, depth), full), like((L, depth)), like((L, width))],
        compiler_params=params(),
        cost_estimate=pace(7),
        name="resid_back",
    )(normed, scale, grad_own, grad_other, dy_own, dy_other, gain, wo, *later)


def project_back_kernel(*refs):
    grads, weight, (grad_own, grad_other, flat) = refs[:9], refs[9], refs[10:13]

    @pl.when(pl.program_id(0) == 0)
    def _():
        flat[...] = weight[...].T

    rows = jnp.concatenate([ref[...] for ref in grads], axis=1)
    grad = dot(rows, flat[...], 1, 0)
    own = is_own(pl.program_id(0))

    @pl.when(own)
    def _():
        grad_own[...] = grad

    @pl.when(jnp.logical_not(own))
    def _():
        grad_other[...] = grad.astype(low)


def project_back(grads, weight, later=()):
    depth, total = weight.shape
    skip = len(later)

    def body(*refs):
        project_back_kernel(*refs[:10], *refs[10 + skip :])

    return pl.pallas_call(
        body,
        grid=(L // ROWS,),
        in_specs=[rows_of(PAIR)] * 9 + [whole((depth, total))] + [ANY] * skip,
        out_specs=[rows_of(depth, own_half), rows_of(depth, other_half)],
        out_shape=[like((L // 2, depth), full), like((L // 2, depth))],
        scratch_shapes=[pltpu.VMEM((total, depth), low)],
        compiler_params=params(),
        cost_estimate=pace(6),
        name="project_back",
    )(*grads, weight, *later)


def input_back_kernel(tokens, grad_own, grad_other, dresid, gain, result):
    grads = grad_own[...] + grad_other[...].astype(full)
    unit, scale = normalized(tokens[...].astype(full))
    result[...] = dresid[...] + norm_back(unit, scale, gain[...], grads)


def input_back(tokens, grad_own, grad_other, dresid, gain):
    height, depth = tokens.shape
    return pl.pallas_call(
        input_back_kernel,
        grid=(height // ROWS,),
        in_specs=[rows_of(depth)] * 4 + [whole((1, depth))],
        out_specs=rows_of(depth),
        out_shape=like((height, depth), full),
        compiler_params=params(),
        cost_estimate=pace(3),
        name="input_back",
    )(tokens, grad_own, grad_other, dresid, gain)


def adamw(weight, grad, first, second, rate, decay):
    first_new = beta_one * first + (1.0 - beta_one) * grad
    second_new = beta_two * second + (1.0 - beta_two) * grad * grad
    step_size = (
        first_new
        / (1.0 - beta_one**STEP)
        / (jnp.sqrt(second_new / (1.0 - beta_two**STEP)) + adam_eps)
    )
    return (weight - rate * (step_size + decay * weight), first_new, second_new)


def step_kernel(counts, flipped, spans, column_at, *refs):
    totals, used = [], 0
    for count in counts:
        total = refs[used][...].astype(full)
        for piece in refs[used + 1 : used + count]:
            total = total + piece[...].astype(full)
        totals.append(total)
        used += count
    rest, count = refs[used:], len(spans)
    states, outs = rest[: 3 * count], rest[3 * count : 7 * count]
    scratch = rest[7 * count + 1 :]
    rows = totals[0].shape[0]
    column = None
    for group, start in column_at:
        term = totals[group][:, start : start + SPARE]
        column = term if column is None else column + term
    rest[7 * count][...] = column
    for at, span in enumerate(spans):
        weight, first, second = states[3 * at : 3 * at + 3]
        grad_out, weight_out, first_out, second_out = outs[4 * at : 4 * at + 4]
        for part, slices in enumerate(span):
            pieces = [totals[group][:, start : start + size] for group, start, size in slices]
            grad = pieces[0] if len(pieces) == 1 else jnp.concatenate(pieces, axis=1)
            width = grad.shape[1]
            if flipped[at]:
                padded = scratch[at]
                padded[...] = jnp.zeros_like(padded)
                padded[0:rows, 0:width] = grad
                grad = padded[...].T[0:width, 0:rows]
                where = Ellipsis
            else:
                where = part
            new = adamw(
                weight[where], grad, first[where], second[where], weight_rate, weight_decay
            )
            grad_out[where] = grad
            weight_out[where], first_out[where], second_out[where] = new


def step(groups, spans, states, flipped, column_at, later=()):
    shapes, scratch = [], []
    for (weight, _, _), span, flip in zip(states, spans, flipped):
        shapes += [like(weight.shape, full)] * 4
        lanes = -(-sum(size for _, _, size in span[0]) // 128) * 128
        scratch.append(pltpu.VMEM((128, lanes) if flip else (8, 128), full))
    shapes.append(like((groups[0][0].shape[0], SPARE), full))
    flat = [array for state in states for array in state]
    results = call(
        functools.partial(step_kernel, [len(group) for group in groups], flipped, spans, column_at),
        "step",
        [piece for group in groups for piece in group] + flat,
        shapes,
        later=later,
        scratch=scratch,
    )
    return [results[4 * at : 4 * at + 4] for at in range(len(states))] + [results[-1]]


def shards(
    tokens,
    cotangent,
    w_qkv,
    w_attn_out,
    w_in,
    w_mlp_out,
    gains,
    first_qkv,
    first_attn_out,
    first_in,
    first_mlp_out,
    first_gains,
    second_qkv,
    second_attn_out,
    second_in,
    second_mlp_out,
    second_gains,
):
    count = lax.axis_size("dp")
    fast = staged(count)
    core = lax.axis_index("tensor") % 2
    head_width = w_qkv.shape[2]
    unit_width = w_in.shape[2]
    depth = tokens.shape[1]
    qkv_layouts = [sum((head_layout(part * head_width, head_width) for part in range(3)), [])]
    gains_at = 3 * head_width
    gate_at, up_at, down_at = (head_width + part * unit_width for part in range(3))
    rest_layouts = [
        head_layout(0, head_width),
        unit_layout(gate_at, unit_width) + unit_layout(up_at, unit_width),
        unit_layout(down_at, unit_width),
    ]

    shard_one = pack(w_qkv, gains)
    shard_two = pack_rest(w_attn_out, w_in, w_mlp_out, [shard_one])
    cosine, sine = rope_tables(core * (L // 2))

    def halves(shard, along):
        half = shard.shape[0] // 2
        pieces = [shard] + along
        return jnp.stack([p[:half] for p in pieces]), jnp.stack([p[half:] for p in pieces])

    if fast:
        along_one = [z_shift(shard_one, count, jump) for jump in (1, 2, 3)]
        x_other = core_swap(tokens)
        za, zb = halves(after(shard_one, shard_two, x_other, cosine, sine), along_one)
        shard_two = after(shard_two, *along_one)
        along_two = [z_shift(shard_two, count, jump) for jump in (1, 2, 3)]
        xa, yb = x_swap(za, count), y_swap(zb)
        both_a, both_b = jnp.stack([za, xa]), jnp.stack([zb, yb])
        ya, xb = y_swap(both_a), x_swap(both_b, count)
        first_pieces = [za, xa, ya, zb, yb, xb]
        za, zb = halves(shard_two, [after(piece, both_a, both_b) for piece in along_two])
        w_qkv_all, gains_all = assemble(
            first_pieces, qkv_layouts, depth, (), gains_at, later=[za, zb]
        )
    else:
        x_other = core_swap(tokens)
        w_qkv_all, gains_all = gathered_plainly(shard_one, qkv_layouts, (), gains_at)
    gain_one, gain_two = gains_all[0:1], gains_all[1:2]
    if fast:
        xa, yb = x_swap(za, count), y_swap(zb)
    normed_one, query, key, value = project(tokens, x_other, gain_one, w_qkv_all, cosine, sine)
    if fast:
        xa, yb = after(xa, query), after(yb, query)
        ya, xb = y_swap(jnp.stack([za, xa])), x_swap(jnp.stack([zb, yb]), count)
    dy_other = core_swap(after(cotangent, query))
    mixed, lse = attend(query, key, value)
    mixed_other = core_swap(mixed)
    if fast:
        ya, xb = after(ya, mixed), after(xb, mixed)
        rest = assemble([za, xa, ya, zb, yb, xb], rest_layouts, depth, (0, 1, 2))
    else:
        rest = gathered_plainly(shard_two, rest_layouts, (0, 1, 2))
    wo_flat, w_both, w_down_flat, wo, w_both_flat, w_down = rest
    wo_other = core_swap(wo)
    normed_two, scale_two, hidden, dboth, out_own, out_other, dnormed = feed_forward(
        mixed,
        mixed_other,
        tokens,
        x_other,
        cotangent,
        dy_other,
        gain_two,
        wo,
        wo_other,
        w_both,
        w_both_flat,
        w_down,
        w_down_flat,
    )
    units = w_down.shape[0]
    dnormed_other = core_swap(dnormed)
    grad_1 = weight_grad(
        [normed_two, dboth, cotangent, dy_other, hidden],
        [
            ((0,), (1,), [(0, unit_width, unit_width), (units, units + unit_width, unit_width)]),
            ((2, 3), (4,), [(0, unit_width, unit_width)]),
        ],
        count,
        w_both,
        [(0, 2 * units)],
    )
    if fast:
        from_y, from_x = y_swap(grad_1[1]), x_swap(grad_1[3], count)
    output = (out_own + core_swap(out_other).astype(full)).astype(low)
    dresid, dresid_low, dmixed = resid_back(
        normed_two,
        scale_two,
        dnormed,
        dnormed_other,
        cotangent,
        dy_other,
        gain_two,
        wo_flat,
        later=grad_1[:1],
    )
    bundle = (query, key, value, mixed, dmixed, lse, cosine, sine)
    pair_0 = attend_back(0, *bundle, later=[output])
    if fast:
        sums_1 = add_first([(grad_1[0], from_y, grad_1[2], from_x)], later=pair_0[:1])
        next_a, next_b = x_swap(sums_1[1], count), y_swap(sums_1[3])
    pair_2 = attend_back(2, *bundle, later=[sums_1[1], sums_1[3]] if fast else pair_0[:1])
    if fast:
        merged = add_second(sums_1[0], next_a, sums_1[2], next_b, later=pair_2[:1])
        pieces_1 = across_z(merged, count)
    grad_2 = weight_grad(
        [normed_one, *(group[part] for part in range(3) for group in (pair_0, pair_2)), dresid_low, mixed],
        [
            ((0,), tuple(range(1, 7)), [(2 * part * PAIR, (2 * part + 1) * PAIR, PAIR) for part in range(3)]),
            ((7,), (8,), [(0, 2 * PAIR, PAIR), (PAIR, PAIR + HD, HD)]),
        ],
        count,
        w_qkv_all,
        [(part * 3 * PAIR + at * PAIR, PAIR) for part in range(3) for at in (0, 2)],
        later=merged[:1] if fast else (),
    )
    if fast:
        from_y2, from_x2 = y_swap(grad_2[1]), x_swap(grad_2[3], count)
    pair_1 = attend_back(1, *bundle, later=grad_2[:1])
    grad_3 = weight_grad(
        [normed_one, *pair_1],
        [((0,), (1, 2, 3), [(part * PAIR, part * PAIR + HD, HD) for part in range(3)])],
        count,
        w_qkv_all,
        [(part * 3 * PAIR + PAIR, PAIR) for part in range(3)],
        later=[from_y2, from_x2] if fast else (),
    )
    trios = [group[part] for part in range(3) for group in (pair_0, pair_1, pair_2)]
    grad_one, grad_one_low = project_back(
        trios, w_qkv_all, later=[grad_3[0], *pieces_1] if fast else grad_3[:1]
    )
    if fast:
        from_y3, from_x3 = y_swap(grad_3[1]), x_swap(grad_3[3], count)
        from_y3, from_x3 = after(from_y3, grad_one), after(from_x3, grad_one)
        sums_2 = add_first(
            [(grad_2[0], from_y2, grad_2[2], from_x2), (grad_3[0], from_y3, grad_3[2], from_x3)]
        )
        next_a, next_b = x_swap(sums_2[1], count), y_swap(sums_2[3])
        grad_one_low = after(grad_one_low, sums_2[1], sums_2[3])
    else:
        pieces_1 = reduced_plainly(*grad_1)
    grad_other = core_swap(grad_one_low)
    grad_inputs = input_back(tokens, grad_one, grad_other, dresid, gain_one)
    new_in, new_down, column_two = step(
        [pieces_1],
        [
            [[(0, 0, unit_width)], [(0, unit_width, unit_width)]],
            [[(0, 2 * unit_width, unit_width)]],
        ],
        [(w_in, first_in, second_in), (w_mlp_out, first_mlp_out, second_mlp_out)],
        (False, True),
        [(0, 3 * unit_width)],
        later=[grad_inputs],
    )
    if fast:
        next_a, next_b = after(next_a, grad_inputs), after(next_b, grad_inputs)
        pieces_2 = across_z(add_second(sums_2[0], next_a, sums_2[2], next_b), count)
    else:
        joined = [jnp.concatenate(pair, axis=1) for pair in zip(grad_2[:2], grad_3[:2])]
        pieces_2 = reduced_plainly(*joined)
    split = grad_2[0].shape[-1]
    new_qkv, new_attn, column_one = step(
        [pieces_2],
        [
            [[(0, part * PAIR, PAIR), (0, split + part * HD, HD)] for part in range(3)],
            [[(0, 3 * PAIR, head_width)]],
        ],
        [(w_qkv, first_qkv, second_qkv), (w_attn_out, first_attn_out, second_attn_out)],
        (False, True),
        [(0, split - SPARE), (0, split + 3 * HD)],
    )
    sums = jnp.concatenate([column_one[:, :1], column_two[:, :1]], axis=1)
    shard_gain = (sums + core_swap(sums)).T / gains
    new_gain = adamw(gains, shard_gain, first_gains, second_gains, gain_rate, 0.0)
    return (
        output,
        grad_inputs,
        new_qkv[0],
        new_attn[0],
        new_in[0],
        new_down[0],
        shard_gain,
        new_qkv[1],
        new_attn[1],
        new_in[1],
        new_down[1],
        new_gain[0],
        new_qkv[2],
        new_attn[2],
        new_in[2],
        new_down[2],
        new_gain[1],
        new_qkv[3],
        new_attn[3],
        new_in[3],
        new_down[3],
        new_gain[2],
    )


def solution(mesh):
    return jax.shard_map(
        shards,
        mesh=mesh,
        in_specs=(
            P(("dp", "tensor"), None),
            P(("dp", "tensor"), None),
            P(None, "dp", "tensor"),
            P("tensor", "dp"),
            P(None, "dp", "tensor"),
            P("tensor", "dp"),
            P(None, "dp"),
            P(None, "dp", "tensor"),
            P("tensor", "dp"),
            P(None, "dp", "tensor"),
            P("tensor", "dp"),
            P(None, "dp"),
            P(None, "dp", "tensor"),
            P("tensor", "dp"),
            P(None, "dp", "tensor"),
            P("tensor", "dp"),
            P(None, "dp"),
        ),
        out_specs=(
            P(("dp", "tensor"), None),
            P(("dp", "tensor"), None),
            P(None, "dp", "tensor"),
            P("tensor", "dp"),
            P(None, "dp", "tensor"),
            P("tensor", "dp"),
            P(None, "dp"),
            P(None, "dp", "tensor"),
            P("tensor", "dp"),
            P(None, "dp", "tensor"),
            P("tensor", "dp"),
            P(None, "dp"),
            P(None, "dp", "tensor"),
            P("tensor", "dp"),
            P(None, "dp", "tensor"),
            P("tensor", "dp"),
            P(None, "dp"),
            P(None, "dp", "tensor"),
            P("tensor", "dp"),
            P(None, "dp", "tensor"),
            P("tensor", "dp"),
            P(None, "dp"),
        ),
        check_vma=False,
    )
```

```python
import functools

import jax
import jax.numpy as jnp
import numpy as np
from jax import lax
from jax.experimental import pallas as pl
from jax.experimental.pallas import tpu as pltpu
from jax.sharding import PartitionSpec as P

HD = 64
L = 1024
STEP = 10


eps_norm = 1e-05
rope_base = 160000.0
beta_one = 0.9
beta_two = 0.98
adam_eps = 1e-06
weight_rate = 0.02
gain_rate = 0.2
weight_decay = 0.01

low = jnp.bfloat16
full = jnp.float32
ROWS = 512
CHUNK = 256
PAIR = 2 * HD
VMEM_BYTES = 28 << 20
SPARE = 64
PACE = 800_000_000


def pace(microseconds):
    return pl.CostEstimate(flops=int(microseconds * PACE), bytes_accessed=0, transcendentals=0)


def dot(left, right, left_dim, right_dim):
    return lax.dot_general(
        left, right, (((left_dim,), (right_dim,)), ((), ())), preferred_element_type=full
    )


def params():
    return pltpu.CompilerParams(vmem_limit_bytes=VMEM_BYTES)


def whole(shape):
    return pl.BlockSpec(shape, lambda *_: (0,) * len(shape))


def rows_of(width, index=lambda i: i):
    return pl.BlockSpec((ROWS, width), lambda i: (index(i), 0))


def own_half(i):
    return jnp.minimum(i, L // ROWS // 2 - 1)


def other_half(i):
    return jnp.maximum(i - L // ROWS // 2, 0)


def swapped(i):
    return (i + L // ROWS // 2) % (L // ROWS)


def is_own(i):
    return i < L // ROWS // 2


def core_swap(array):
    return lax.ppermute(array, "tensor", [(t, t ^ 1) for t in range(4)])


def y_swap(array):
    return lax.ppermute(array, "tensor", [(t, t ^ 2) for t in range(4)])


def x_swap(array, count):
    return lax.ppermute(array, "dp", [(d, d ^ 1) for d in range(count)])


def z_shift(array, count, step):
    around = count // 2
    return lax.ppermute(
        array, "dp", [(d, (d // 2 + step) % around * 2 + d % 2) for d in range(count)]
    )


def staged(count):
    return count == 8


def after(array, *others):
    return lax.optimization_barrier((array, *others))[0]


ANY = pl.BlockSpec(memory_space=pl.ANY)
LOCAL = pl.BlockSpec(memory_space=pltpu.VMEM)
SCALAR = pl.BlockSpec(memory_space=pltpu.SMEM)


TIMES = {"weight_grad": 6, "assemble": 3, "step": 2, "pack": 1, "pack_rest": 1, "add_first": 2, "add_second": 1}


def call(kernel, name, ins, shapes, later=(), place=None, scratch=()):
    head = [] if place is None else [place]
    lead, skip = len(head), len(later)

    def body(*refs):
        kernel(*refs[: lead + len(ins)], *refs[lead + len(ins) + skip :])

    return pl.pallas_call(
        body,
        in_specs=[SCALAR] * lead + [LOCAL] * len(ins) + [ANY] * skip,
        out_specs=[LOCAL] * len(shapes),
        out_shape=shapes,
        scratch_shapes=list(scratch),
        compiler_params=params(),
        cost_estimate=pace(TIMES[name]),
        name=name,
    )(*head, *ins, *later)


def like(shape, kind=low):
    return jax.ShapeDtypeStruct(shape, kind)


def pack_kernel(w_qkv, gains, shard, padded):
    rows = w_qkv.shape[1]
    padded[...] = jnp.zeros_like(padded)
    padded[0 : gains.shape[0], 0:rows] = gains[...]
    columns = padded[...].T[0:rows, 0:2]
    high = columns.astype(low)
    rest = columns - high.astype(full)
    middle = rest.astype(low)
    last = (rest - middle.astype(full)).astype(low)
    filler = jnp.zeros((rows, SPARE - 6), full)
    pieces = [w_qkv[part] for part in range(3)]
    shard[...] = jnp.concatenate(
        pieces + [high.astype(full), middle.astype(full), last.astype(full), filler], axis=1
    ).astype(low)


def pack(w_qkv, gains):
    rows, width = w_qkv.shape[1:]
    return call(
        pack_kernel,
        "pack",
        [w_qkv, gains],
        [like((rows, 3 * width + SPARE))],
        scratch=[pltpu.VMEM((128, 128), full)],
    )[0]


def pack_rest_kernel(w_attn_out, w_in, w_mlp_out, shard, wide):
    rows = w_in.shape[1]
    flipped = []
    for weight in (w_attn_out, w_mlp_out):
        wide[...] = jnp.zeros_like(wide)
        wide[0 : weight.shape[0], 0:rows] = weight[...]
        flipped.append(wide[...].T[0:rows, 0 : weight.shape[0]])
    pieces = [flipped[0], w_in[0], w_in[1], flipped[1]]
    shard[...] = jnp.concatenate(pieces, axis=1).astype(low)


def pack_rest(w_attn_out, w_in, w_mlp_out, later):
    rows, units = w_in.shape[1:]
    heads = w_attn_out.shape[0]
    return call(
        pack_rest_kernel,
        "pack_rest",
        [w_attn_out, w_in, w_mlp_out],
        [like((rows, heads + 3 * units))],
        later=later,
        scratch=[pltpu.VMEM((-(-units // 128) * 128, 128), full)],
    )[0]


def unpack_gains(columns):
    wide = jnp.concatenate([columns.astype(full), jnp.zeros(columns.shape, full)], axis=1).T
    return wide[0:2] + wide[2:4] + wide[4:6]


def columns_of(layout, own, other):
    pieces = []
    for item in layout:
        if item is None:
            pieces.append(jnp.zeros((own.shape[0], SPARE), own.dtype))
        else:
            side, start, width = item
            pieces.append((own, other)[side][:, start : start + width])
    return jnp.concatenate(pieces, axis=1)


def layout_width(layout):
    return sum(SPARE if item is None else item[2] for item in layout)


def head_layout(start, width):
    first = width // 3 * 2
    return [(0, start, width), (1, start + first, width - first), (1, start, first)]


def unit_layout(start, width):
    return [(0, start, width), (1, start, width), None]


def assemble_kernel(layouts, flips, gains_at, place_ref, za, xa, ya, zb, yb, xb, *outs):
    place = place_ref[0]
    half = za.shape[1]
    for jx in range(2):
        for jz in range(4):
            source = (place // 2 + 4 - jz) % 4 * 2 + (place % 2 + jx) % 2
            own_a = (za, xa)[jx][jz]
            other_a = ya[jx, jz]
            own_b = zb[jz] if jx == 0 else xb[0, jz]
            other_b = yb[jz] if jx == 0 else xb[1, jz]
            for part, (own, other) in enumerate(((own_a, other_a), (own_b, other_b))):
                start = pl.multiple_of(source * 2 * half + part * half, half)
                for layout, out in zip(layouts, outs):
                    out[pl.ds(start, half), :] = columns_of(layout, own, other)
                if gains_at is not None:
                    outs[-1][pl.ds(start, half), :] = own[:, gains_at : gains_at + SPARE]
    for at, flip in enumerate(flips):
        outs[len(layouts) + at][...] = outs[flip][...].T
    if gains_at is not None:
        outs[-2][...] = unpack_gains(outs[-1][...])


def assemble(pieces, layouts, depth, flips=(), gains_at=None, later=()):
    place = lax.axis_index("dp").astype(jnp.int32)[None]
    shapes = [like((depth, layout_width(layout))) for layout in layouts]
    shapes += [like((layout_width(layouts[flip]), depth)) for flip in flips]
    scratch = []
    if gains_at is not None:
        shapes.append(like((2, depth), full))
        scratch.append(pltpu.VMEM((depth, SPARE), low))
    return call(
        functools.partial(assemble_kernel, layouts, flips, gains_at),
        "assemble",
        pieces,
        shapes,
        later=later,
        place=place,
        scratch=scratch,
    )


def gathered_plainly(shard, layouts, flips=(), gains_at=None):
    own = lax.all_gather(shard, "dp", axis=0, tiled=True)
    other = y_swap(own)
    results = [columns_of(layout, own, other) for layout in layouts]
    results += [results[flip].T for flip in flips]
    if gains_at is not None:
        results.append(unpack_gains(own[:, gains_at : gains_at + SPARE]))
    return results


def stacked(ins, at, axis):
    parts = [ins[index][...] for index in at]
    return parts[0] if len(parts) == 1 else jnp.concatenate(parts, axis=axis)


def weight_grad_kernel(products, fast, weights, ins, place_ref, refs):
    outs, scratch = (refs[:4], refs[4:]) if fast else (refs[:2], refs[2:])
    place = place_ref[0]
    for index, (held, (left, right, _)) in enumerate(zip(scratch, products)):
        grad = dot(stacked(ins, left, 0), stacked(ins, right, 1), 0, 0)
        held[...] = grad
        if weights and index == 0:
            weight = [ins[-1][:, start : start + width] for start, width in weights]
            weight = weight[0] if len(weight) == 1 else jnp.concatenate(weight, axis=1)
            sums = jnp.sum(weight.astype(full) * grad, axis=1, keepdims=True)
            scratch[-1][...] = jnp.broadcast_to(sums, (sums.shape[0], 128))

    def split(rows):
        sides = [[], []]
        for held, (_, _, spans) in zip(scratch, products):
            values = held[rows, :]
            for *starts, width in spans:
                for side, start in zip(sides, starts):
                    side.append(values[:, start : start + width])
        if weights:
            for side in sides:
                side.append(scratch[-1][rows, :][:, :SPARE])
        return [jnp.concatenate(side, axis=1).astype(low) for side in sides]

    if not fast:
        outs[0][...], outs[1][...] = split(slice(None))
        return
    size = outs[0].shape[2]
    for jx in range(2):
        for jz in range(4):
            target = (place // 2 + jz) % 4 * 2 + (place % 2 + jx) % 2
            for part in range(2):
                start = pl.multiple_of((target * 2 + part) * size, size)
                own, other = split(pl.ds(start, size))
                if part == 0:
                    outs[0][jx, jz] = own
                    outs[1][jx, jz] = other
                else:
                    outs[2 + jx][0, jz] = own
                    outs[2 + jx][1, jz] = other


def weight_grad(arrays, products, count, weight=None, lanes=(), later=()):
    depth = arrays[products[0][0][0]].shape[1]
    widths = [sum(arrays[at].shape[1] for at in right) for _, right, _ in products]
    total = sum(span[2] for _, _, spans in products for span in spans)
    total += SPARE if weight is not None else 0
    fast = staged(count)
    if fast:
        shapes = [like((2, 4, depth // count // 2, total))] * 4
    else:
        shapes = [like((depth, total))] * 2
    place = lax.axis_index("dp").astype(jnp.int32)[None]
    ins = list(arrays) + ([] if weight is None else [weight])
    weights = [] if weight is None else list(lanes)
    held = [pltpu.VMEM((depth, width), full) for width in widths]
    if weights:
        held.append(pltpu.VMEM((depth, 128), full))

    def kernel(place_ref, *refs):
        weight_grad_kernel(
            products, fast, weights, refs[: len(ins)], place_ref, refs[len(ins) :]
        )

    return call(
        kernel,
        "weight_grad",
        ins,
        shapes,
        later=later,
        place=place,
        scratch=held,
    )


def reduced_plainly(own, other):
    summed = own.astype(full) + y_swap(other).astype(full)
    return [lax.psum_scatter(summed, "dp", scatter_dimension=0, tiled=True)]


def add_kernel(groups, *refs):
    ins, outs = refs[: 4 * groups], refs[4 * groups :]
    for half in range(2):
        for side in range(2):
            sums = []
            for group in range(groups):
                here, there = ins[4 * group + 2 * half : 4 * group + 2 * half + 2]
                sums.append((here[side].astype(full) + there[side].astype(full)).astype(low))
            out = outs[2 * half + side]
            out[...] = sums[0] if groups == 1 else jnp.concatenate(sums, axis=-1)


def add_first(groups, later=()):
    rows = groups[0][0].shape[2]
    width = sum(group[0].shape[3] for group in groups)
    return call(
        functools.partial(add_kernel, len(groups)),
        "add_first",
        [array for group in groups for array in group],
        [like((4, rows, width))] * 4,
        later=later,
    )


def merge_kernel(here_a, there_a, here_b, there_b, *outs):
    for jump, out in enumerate(outs):
        part_a = here_a[jump].astype(full) + there_a[jump].astype(full)
        part_b = here_b[jump].astype(full) + there_b[jump].astype(full)
        out[...] = jnp.concatenate([part_a.astype(low), part_b.astype(low)], axis=0)


def add_second(here_a, there_a, here_b, there_b, later=()):
    _, rows, width = here_a.shape
    return call(
        merge_kernel,
        "add_second",
        [here_a, there_a, here_b, there_b],
        [like((2 * rows, width))] * 4,
        later=later,
    )


def across_z(parts, count):
    return [parts[0]] + [z_shift(parts[step], count, step) for step in (1, 2, 3)]


def normalized(values):
    centred = values - jnp.mean(values, axis=-1, keepdims=True)
    spread = jnp.mean(centred * centred, axis=-1, keepdims=True)
    scale = lax.rsqrt(spread + eps_norm)
    return centred * scale, scale


def norm_back(unit, scale, gains, grads):
    inner = grads * gains
    mean_inner = jnp.mean(inner, axis=-1, keepdims=True)
    mean_unit = jnp.mean(inner * unit, axis=-1, keepdims=True)
    return scale * (inner - mean_inner - unit * mean_unit)


def rope_tables(offset):
    half_width = HD // 2
    frequency = rope_base ** (-(jnp.arange(half_width, dtype=full) * 2.0 / HD))
    position = ((jnp.arange(L) + offset) % L).astype(full)
    angles = position[:, None] * frequency[None, :]
    cosine, sine = jnp.cos(angles), jnp.sin(angles)
    return (
        jnp.concatenate([cosine] * 4, axis=1),
        jnp.concatenate([-sine, sine, -sine, sine], axis=1),
    )


def turn(values, cosine, sine):
    lane = lax.broadcasted_iota(jnp.int32, values.shape, 1)
    ahead = pltpu.roll(values, PAIR - HD // 2, 1)
    behind = pltpu.roll(values, HD // 2, 1)
    turned = jnp.where(lane % HD < HD // 2, ahead, behind)
    return values * cosine + turned * sine


def qkv_kernel(x_own, x_other, gain, weight, cosine, sine, normed, q_out, k_out, v_out, raw):
    own = is_own(pl.program_id(0))
    unit, _ = normalized(jnp.where(own, x_own[...], x_other[...]).astype(full))
    rows = (unit * gain[...]).astype(low)
    normed[...] = rows
    raw[...] = dot(rows, weight[...], 1, 0)
    width = q_out.shape[1]
    near, far = cosine[...], sine[...]
    for start in range(0, width, PAIR):
        lanes = slice(start, start + PAIR)
        query = turn(raw[:, lanes], near, far).astype(low)
        q_out[:, lanes] = query * jnp.asarray(HD ** (-0.5), low)
        key = raw[:, width + start : width + start + PAIR]
        k_out[:, lanes] = turn(key, near, far).astype(low)
    v_out[...] = raw[:, 2 * width :].astype(low)


def project(x_own, x_other, gain, weight, cosine, sine):
    depth, total = weight.shape
    width = total // 3
    return pl.pallas_call(
        qkv_kernel,
        grid=(L // ROWS,),
        in_specs=[
            rows_of(depth, own_half),
            rows_of(depth, other_half),
            whole((1, depth)),
            whole((depth, total)),
            rows_of(PAIR),
            rows_of(PAIR),
        ],
        out_specs=[rows_of(depth), rows_of(width), rows_of(width), rows_of(width)],
        out_shape=[like((L, depth))] + [like((L, width))] * 3,
        scratch_shapes=[pltpu.VMEM((ROWS, total), full)],
        compiler_params=params(),
        cost_estimate=pace(6),
        name="project",
    )(x_own, x_other, gain, weight, cosine, sine)


def head_masks(height):
    lane = lax.broadcasted_iota(jnp.int32, (height, PAIR), 1)
    return [(lane // HD == head).astype(full).astype(low) for head in range(2)]


def flat_heads(rows):
    flat = rows.astype(full).T
    head_of = lax.broadcasted_iota(jnp.int32, flat.shape, 0) // HD
    return [jnp.where(head_of == head, flat, 0.0).astype(low) for head in range(2)]


def attend_kernel(q_ref, k_ref, v_ref, mixed, lse_ref):
    flat_keys, values = flat_heads(k_ref[...]), v_ref[...]
    lane = lax.broadcasted_iota(jnp.int32, (CHUNK, PAIR), 1)
    for start in range(0, L, CHUNK):
        rows = slice(start, start + CHUNK)
        query = q_ref[rows, :]
        results = []
        for head in range(2):
            scores = dot(query, flat_keys[head], 1, 0)
            row_max = jnp.max(scores, axis=1, keepdims=True)
            raised = jnp.exp(scores - row_max)
            total = jnp.sum(raised, axis=1, keepdims=True)
            results.append(dot(raised.astype(low), values, 1, 0) / total)
            lse = jnp.broadcast_to(row_max + jnp.log(total), (CHUNK, PAIR))
            lse_ref[0, head : head + 1, rows] = lse.T[0:1]
        mixed[rows, :] = jnp.where(lane < HD, results[0], results[1]).astype(low)


def attend(query, key, value):
    width = query.shape[1]
    pairs = width // PAIR
    block = pl.BlockSpec((L, PAIR), lambda i: (0, i))
    totals = pl.BlockSpec((1, 2, L), lambda i: (i, 0, 0))
    return pl.pallas_call(
        attend_kernel,
        grid=(pairs,),
        in_specs=[block] * 3,
        out_specs=[block, totals],
        out_shape=[
            jax.ShapeDtypeStruct((L, width), low),
            jax.ShapeDtypeStruct((pairs, 2, L), full),
        ],
        compiler_params=params(),
        cost_estimate=pace(13),
        name="attend",
    )(query, key, value)


def attend_back_kernel(
    q_ref, k_ref, v_ref, o_ref, grad_ref, lse_ref, cosine, sine, dq_out, dk_out, dv_out, dk, dv
):
    masks = head_masks(L)
    chunk_masks = head_masks(CHUNK)
    keys, values = k_ref[...], v_ref[...]
    head_keys = [keys * mask for mask in masks]
    head_values = [values * mask for mask in masks]
    flipped_keys = flat_heads(keys)
    flat_query = q_ref[...].astype(full).T.astype(low)
    flat_grad = grad_ref[...].astype(full).T.astype(low)
    product = (grad_ref[...].astype(full) * o_ref[...].astype(full)).T
    inner = [jnp.sum(product[head * HD : (head + 1) * HD], axis=0, keepdims=True) for head in range(2)]
    for start in range(0, L, CHUNK):
        rows = slice(start, start + CHUNK)
        query, grad = q_ref[rows, :], grad_ref[rows, :]
        dq = None
        for head in range(2):
            scores = dot(head_keys[head], flat_query[:, rows], 1, 0)
            probs = jnp.exp(scores - lse_ref[0, head : head + 1, rows])
            grad_probs = dot(head_values[head], flat_grad[:, rows], 1, 0)
            grad_scores = (probs * (grad_probs - inner[head][:, rows])).astype(low)
            add_v = dot(probs.astype(low), grad * chunk_masks[head], 1, 0)
            add_k = dot(grad_scores, query * chunk_masks[head], 1, 0)
            add_q = dot(flipped_keys[head], grad_scores, 1, 0)
            dq = add_q if dq is None else dq + add_q
            if start == 0 and head == 0:
                dv[...] = add_v
                dk[...] = add_k
            else:
                dv[...] += add_v
                dk[...] += add_k
        dq_out[rows, :] = turn(dq.T * HD ** (-0.5), cosine[rows, :], -sine[rows, :]).astype(low)
    dk_out[...] = turn(dk[...], cosine[...], -sine[...]).astype(low)
    dv_out[...] = dv[...].astype(low)


def attend_back(pair, query, key, value, mixed, grad, lse, cosine, sine, later=()):
    block = pl.BlockSpec((L, PAIR), lambda i: (0, pair))
    result = pl.BlockSpec((L, PAIR), lambda i: (0, 0))
    totals = pl.BlockSpec((1, 2, L), lambda i: (pair, 0, 0))
    skip = len(later)

    def body(*refs):
        attend_back_kernel(*refs[:8], *refs[8 + skip :])

    return pl.pallas_call(
        body,
        grid=(1,),
        in_specs=[block] * 5 + [totals] + [whole((L, PAIR))] * 2 + [ANY] * skip,
        out_specs=[result] * 3,
        out_shape=[like((L, PAIR))] * 3,
        scratch_shapes=[pltpu.VMEM((L, PAIR), full)] * 2,
        compiler_params=params(),
        cost_estimate=pace(7),
        name="attend_back",
    )(query, key, value, mixed, grad, lse, cosine, sine, *later)


def feed_forward_kernel(
    mixed_own,
    mixed_other,
    x_own,
    x_other,
    dy_own,
    dy_other,
    gain,
    wo_own,
    wo_other,
    w_both,
    w_both_flat,
    w_down,
    w_down_flat,
    normed,
    scale_out,
    hidden_out,
    dboth_out,
    out_own,
    out_other,
    dnormed,
):
    own = is_own(pl.program_id(0))
    units = w_down.shape[0]
    tokens = jnp.where(own, x_own[...], x_other[...]).astype(full)
    resid = (
        tokens + dot(mixed_own[...], wo_own[...], 1, 0) + dot(mixed_other[...], wo_other[...], 1, 0)
    )
    unit, scale = normalized(resid)
    rows = (unit * gain[...]).astype(low)
    normed[...] = rows
    scale_out[...] = jnp.broadcast_to(scale, scale_out.shape)
    both = dot(rows, w_both[...], 1, 0)
    gate, up = both[:, :units], both[:, units:]
    cumulative = 0.5 + 0.5 * lax.erf(gate * np.float32(0.5**0.5))
    density = jnp.exp(gate * gate * -0.5) * np.float32((2.0 * np.pi) ** -0.5)
    activated = gate * cumulative
    hidden = (activated * up).astype(low)
    hidden_out[...] = hidden
    part = dot(hidden, w_down[...], 1, 0)
    dhidden = dot(jnp.where(own, dy_own[...], dy_other[...]), w_down_flat[...], 1, 0)
    dgate = (dhidden * up * (cumulative + gate * density)).astype(low)
    dup = (dhidden * activated).astype(low)
    dboth = jnp.concatenate([dgate, dup], axis=1)
    dboth_out[...] = dboth
    dnormed[...] = dot(dboth, w_both_flat[...], 1, 0).astype(low)

    @pl.when(own)
    def _():
        out_own[...] = resid + part

    @pl.when(jnp.logical_not(own))
    def _():
        out_other[...] = part.astype(low)


def feed_forward(*arrays):
    width, depth = arrays[7].shape
    units = arrays[11].shape[0]
    half = L // 2
    return pl.pallas_call(
        feed_forward_kernel,
        grid=(L // ROWS,),
        in_specs=[
            rows_of(width),
            rows_of(width, swapped),
            rows_of(depth, own_half),
            rows_of(depth, other_half),
            rows_of(depth, own_half),
            rows_of(depth, other_half),
            whole((1, depth)),
            whole((width, depth)),
            whole((width, depth)),
            whole((depth, 2 * units)),
            whole((2 * units, depth)),
            whole((units, depth)),
            whole((depth, units)),
        ],
        out_specs=[
            rows_of(depth),
            rows_of(128),
            rows_of(units),
            rows_of(2 * units),
            rows_of(depth, own_half),
            rows_of(depth, other_half),
            rows_of(depth),
        ],
        out_shape=[
            like((L, depth)),
            like((L, 128), full),
            like((L, units)),
            like((L, 2 * units)),
            like((half, depth), full),
            like((half, depth)),
            like((L, depth)),
        ],
        compiler_params=params(),
        cost_estimate=pace(18),
        name="feed_forward",
    )(*arrays)


def resid_back_kernel(
    normed, scale_ref, grad_own, grad_other, dy_own, dy_other, gain, wo, dresid, dresid_low, dmixed
):
    own = is_own(pl.program_id(0))
    inverse = 1.0 / gain[...]
    pull = jnp.where(own, dy_own[...], dy_other[...]).astype(full)
    grads = grad_own[...].astype(full) + grad_other[...].astype(full)
    unit = normed[...].astype(full) * inverse
    total = pull + norm_back(unit, scale_ref[:, 0:1], gain[...], grads)
    rounded = total.astype(low)
    dresid_low[...] = rounded
    dmixed[...] = dot(rounded, wo[...], 1, 0).astype(low)

    @pl.when(own)
    def _():
        dresid[...] = total


def resid_back(normed, scale, grad_own, grad_other, dy_own, dy_other, gain, wo, later=()):
    depth, width = wo.shape
    skip = len(later)

    def body(*refs):
        resid_back_kernel(*refs[:8], *refs[8 + skip :])

    return pl.pallas_call(
        body,
        grid=(L // ROWS,),
        in_specs=[
            rows_of(depth),
            rows_of(128),
            rows_of(depth),
            rows_of(depth, swapped),
            rows_of(depth, own_half),
            rows_of(depth, other_half),
            whole((1, depth)),
            whole((depth, width)),
        ]
        + [ANY] * skip,
        out_specs=[rows_of(depth, own_half), rows_of(depth), rows_of(width)],
        out_shape=[like((L // 2, depth), full), like((L, depth)), like((L, width))],
        compiler_params=params(),
        cost_estimate=pace(7),
        name="resid_back",
    )(normed, scale, grad_own, grad_other, dy_own, dy_other, gain, wo, *later)


def project_back_kernel(*refs):
    grads, weight, (grad_own, grad_other, flat) = refs[:9], refs[9], refs[10:13]

    @pl.when(pl.program_id(0) == 0)
    def _():
        flat[...] = weight[...].T

    rows = jnp.concatenate([ref[...] for ref in grads], axis=1)
    grad = dot(rows, flat[...], 1, 0)
    own = is_own(pl.program_id(0))

    @pl.when(own)
    def _():
        grad_own[...] = grad

    @pl.when(jnp.logical_not(own))
    def _():
        grad_other[...] = grad.astype(low)


def project_back(grads, weight, later=()):
    depth, total = weight.shape
    skip = len(later)

    def body(*refs):
        project_back_kernel(*refs[:10], *refs[10 + skip :])

    return pl.pallas_call(
        body,
        grid=(L // ROWS,),
        in_specs=[rows_of(PAIR)] * 9 + [whole((depth, total))] + [ANY] * skip,
        out_specs=[rows_of(depth, own_half), rows_of(depth, other_half)],
        out_shape=[like((L // 2, depth), full), like((L // 2, depth))],
        scratch_shapes=[pltpu.VMEM((total, depth), low)],
        compiler_params=params(),
        cost_estimate=pace(6),
        name="project_back",
    )(*grads, weight, *later)


def input_back_kernel(tokens, grad_own, grad_other, dresid, gain, result):
    grads = grad_own[...] + grad_other[...].astype(full)
    unit, scale = normalized(tokens[...].astype(full))
    result[...] = dresid[...] + norm_back(unit, scale, gain[...], grads)


def input_back(tokens, grad_own, grad_other, dresid, gain):
    height, depth = tokens.shape
    return pl.pallas_call(
        input_back_kernel,
        grid=(height // ROWS,),
        in_specs=[rows_of(depth)] * 4 + [whole((1, depth))],
        out_specs=rows_of(depth),
        out_shape=like((height, depth), full),
        compiler_params=params(),
        cost_estimate=pace(3),
        name="input_back",
    )(tokens, grad_own, grad_other, dresid, gain)


def adamw(weight, grad, first, second, rate, decay):
    first_new = beta_one * first + (1.0 - beta_one) * grad
    second_new = beta_two * second + (1.0 - beta_two) * grad * grad
    step_size = (
        first_new
        / (1.0 - beta_one**STEP)
        / (jnp.sqrt(second_new / (1.0 - beta_two**STEP)) + adam_eps)
    )
    return (weight - rate * (step_size + decay * weight), first_new, second_new)


def step_kernel(counts, flipped, spans, column_at, *refs):
    totals, used = [], 0
    for count in counts:
        total = refs[used][...].astype(full)
        for piece in refs[used + 1 : used + count]:
            total = total + piece[...].astype(full)
        totals.append(total)
        used += count
    rest, count = refs[used:], len(spans)
    states, outs = rest[: 3 * count], rest[3 * count : 7 * count]
    scratch = rest[7 * count + 1 :]
    rows = totals[0].shape[0]
    column = None
    for group, start in column_at:
        term = totals[group][:, start : start + SPARE]
        column = term if column is None else column + term
    rest[7 * count][...] = column
    for at, span in enumerate(spans):
        weight, first, second = states[3 * at : 3 * at + 3]
        grad_out, weight_out, first_out, second_out = outs[4 * at : 4 * at + 4]
        for part, slices in enumerate(span):
            pieces = [totals[group][:, start : start + size] for group, start, size in slices]
            grad = pieces[0] if len(pieces) == 1 else jnp.concatenate(pieces, axis=1)
            width = grad.shape[1]
            if flipped[at]:
                padded = scratch[at]
                padded[...] = jnp.zeros_like(padded)
                padded[0:rows, 0:width] = grad
                grad = padded[...].T[0:width, 0:rows]
                where = Ellipsis
            else:
                where = part
            new = adamw(
                weight[where], grad, first[where], second[where], weight_rate, weight_decay
            )
            grad_out[where] = grad
            weight_out[where], first_out[where], second_out[where] = new


def step(groups, spans, states, flipped, column_at, later=()):
    shapes, scratch = [], []
    for (weight, _, _), span, flip in zip(states, spans, flipped):
        shapes += [like(weight.shape, full)] * 4
        lanes = -(-sum(size for _, _, size in span[0]) // 128) * 128
        scratch.append(pltpu.VMEM((128, lanes) if flip else (8, 128), full))
    shapes.append(like((groups[0][0].shape[0], SPARE), full))
    flat = [array for state in states for array in state]
    results = call(
        functools.partial(step_kernel, [len(group) for group in groups], flipped, spans, column_at),
        "step",
        [piece for group in groups for piece in group] + flat,
        shapes,
        later=later,
        scratch=scratch,
    )
    return [results[4 * at : 4 * at + 4] for at in range(len(states))] + [results[-1]]


def shards(
    tokens,
    cotangent,
    w_qkv,
    w_attn_out,
    w_in,
    w_mlp_out,
    gains,
    first_qkv,
    first_attn_out,
    first_in,
    first_mlp_out,
    first_gains,
    second_qkv,
    second_attn_out,
    second_in,
    second_mlp_out,
    second_gains,
):
    count = lax.axis_size("dp")
    fast = staged(count)
    core = lax.axis_index("tensor") % 2
    head_width = w_qkv.shape[2]
    unit_width = w_in.shape[2]
    depth = tokens.shape[1]
    qkv_layouts = [sum((head_layout(part * head_width, head_width) for part in range(3)), [])]
    gains_at = 3 * head_width
    gate_at, up_at, down_at = (head_width + part * unit_width for part in range(3))
    rest_layouts = [
        head_layout(0, head_width),
        unit_layout(gate_at, unit_width) + unit_layout(up_at, unit_width),
        unit_layout(down_at, unit_width),
    ]

    shard_one = pack(w_qkv, gains)
    shard_two = pack_rest(w_attn_out, w_in, w_mlp_out, [shard_one])
    cosine, sine = rope_tables(core * (L // 2))

    def halves(shard, along):
        half = shard.shape[0] // 2
        pieces = [shard] + along
        return jnp.stack([p[:half] for p in pieces]), jnp.stack([p[half:] for p in pieces])

    if fast:
        along_one = [z_shift(shard_one, count, jump) for jump in (1, 2, 3)]
        x_other = core_swap(tokens)
        za, zb = halves(after(shard_one, shard_two, x_other, cosine, sine), along_one)
        shard_two = after(shard_two, *along_one)
        along_two = [z_shift(shard_two, count, jump) for jump in (1, 2, 3)]
        xa, yb = x_swap(za, count), y_swap(zb)
        both_a, both_b = jnp.stack([za, xa]), jnp.stack([zb, yb])
        ya, xb = y_swap(both_a), x_swap(both_b, count)
        first_pieces = [za, xa, ya, zb, yb, xb]
        za, zb = halves(shard_two, [after(piece, both_a, both_b) for piece in along_two])
        w_qkv_all, gains_all = assemble(
            first_pieces, qkv_layouts, depth, (), gains_at, later=[za, zb]
        )
    else:
        x_other = core_swap(tokens)
        w_qkv_all, gains_all = gathered_plainly(shard_one, qkv_layouts, (), gains_at)
    gain_one, gain_two = gains_all[0:1], gains_all[1:2]
    if fast:
        xa, yb = x_swap(za, count), y_swap(zb)
    normed_one, query, key, value = project(tokens, x_other, gain_one, w_qkv_all, cosine, sine)
    if fast:
        xa, yb = after(xa, query), after(yb, query)
        ya, xb = y_swap(jnp.stack([za, xa])), x_swap(jnp.stack([zb, yb]), count)
    dy_other = core_swap(after(cotangent, query))
    mixed, lse = attend(query, key, value)
    mixed_other = core_swap(mixed)
    if fast:
        ya, xb = after(ya, mixed), after(xb, mixed)
        rest = assemble([za, xa, ya, zb, yb, xb], rest_layouts, depth, (0, 1, 2))
    else:
        rest = gathered_plainly(shard_two, rest_layouts, (0, 1, 2))
    wo_flat, w_both, w_down_flat, wo, w_both_flat, w_down = rest
    wo_other = core_swap(wo)
    normed_two, scale_two, hidden, dboth, out_own, out_other, dnormed = feed_forward(
        mixed,
        mixed_other,
        tokens,
        x_other,
        cotangent,
        dy_other,
        gain_two,
        wo,
        wo_other,
        w_both,
        w_both_flat,
        w_down,
        w_down_flat,
    )
    units = w_down.shape[0]
    dnormed_other = core_swap(dnormed)
    grad_1 = weight_grad(
        [normed_two, dboth, cotangent, dy_other, hidden],
        [
            ((0,), (1,), [(0, unit_width, unit_width), (units, units + unit_width, unit_width)]),
            ((2, 3), (4,), [(0, unit_width, unit_width)]),
        ],
        count,
        w_both,
        [(0, 2 * units)],
    )
    if fast:
        from_y, from_x = y_swap(grad_1[1]), x_swap(grad_1[3], count)
    output = (out_own + core_swap(out_other).astype(full)).astype(low)
    dresid, dresid_low, dmixed = resid_back(
        normed_two,
        scale_two,
        dnormed,
        dnormed_other,
        cotangent,
        dy_other,
        gain_two,
        wo_flat,
        later=grad_1[:1],
    )
    bundle = (query, key, value, mixed, dmixed, lse, cosine, sine)
    pair_0 = attend_back(0, *bundle, later=[output])
    if fast:
        sums_1 = add_first([(grad_1[0], from_y, grad_1[2], from_x)], later=pair_0[:1])
        next_a, next_b = x_swap(sums_1[1], count), y_swap(sums_1[3])
    pair_2 = attend_back(2, *bundle, later=[sums_1[1], sums_1[3]] if fast else pair_0[:1])
    if fast:
        merged = add_second(sums_1[0], next_a, sums_1[2], next_b, later=pair_2[:1])
        pieces_1 = across_z(merged, count)
    grad_2 = weight_grad(
        [normed_one, *(group[part] for part in range(3) for group in (pair_0, pair_2)), dresid_low, mixed],
        [
            ((0,), tuple(range(1, 7)), [(2 * part * PAIR, (2 * part + 1) * PAIR, PAIR) for part in range(3)]),
            ((7,), (8,), [(0, 2 * PAIR, PAIR), (PAIR, PAIR + HD, HD)]),
        ],
        count,
        w_qkv_all,
        [(part * 3 * PAIR + at * PAIR, PAIR) for part in range(3) for at in (0, 2)],
        later=merged[:1] if fast else (),
    )
    if fast:
        from_y2, from_x2 = y_swap(grad_2[1]), x_swap(grad_2[3], count)
    pair_1 = attend_back(1, *bundle, later=grad_2[:1])
    if fast:
        sums_2 = add_first([(grad_2[0], from_y2, grad_2[2], from_x2)], later=pair_1[:1])
        next_a, next_b = x_swap(sums_2[1], count), y_swap(sums_2[3])
    grad_3 = weight_grad(
        [normed_one, *pair_1],
        [((0,), (1, 2, 3), [(part * PAIR, part * PAIR + HD, HD) for part in range(3)])],
        count,
        w_qkv_all,
        [(part * 3 * PAIR + PAIR, PAIR) for part in range(3)],
        later=[sums_2[1], sums_2[3], *pieces_1] if fast else (),
    )
    trios = [group[part] for part in range(3) for group in (pair_0, pair_1, pair_2)]
    grad_one, grad_one_low = project_back(trios, w_qkv_all, later=grad_3[:1])
    if fast:
        from_y3, from_x3 = y_swap(grad_3[1]), x_swap(grad_3[3], count)
        merged = add_second(sums_2[0], next_a, sums_2[2], next_b, later=[grad_one])
        pieces_2 = across_z(merged, count)
        sums_3 = add_first([(grad_3[0], from_y3, grad_3[2], from_x3)], later=merged[:1])
        grad_one_low = after(grad_one_low, sums_3[1], sums_3[3])
    else:
        pieces_1 = reduced_plainly(*grad_1)
    grad_other = core_swap(grad_one_low)
    grad_inputs = input_back(tokens, grad_one, grad_other, dresid, gain_one)
    new_in, new_down, column_two = step(
        [pieces_1],
        [
            [[(0, 0, unit_width)], [(0, unit_width, unit_width)]],
            [[(0, 2 * unit_width, unit_width)]],
        ],
        [(w_in, first_in, second_in), (w_mlp_out, first_mlp_out, second_mlp_out)],
        (False, True),
        [(0, 3 * unit_width)],
        later=sums_3[:1] if fast else (),
    )
    if fast:
        next_a = x_swap(after(sums_3[1], grad_other), count)
        next_b = y_swap(after(sums_3[3], grad_other))
        merged = add_second(sums_3[0], next_a, sums_3[2], next_b, later=[grad_inputs, column_two, *pieces_2])
        pieces_3 = across_z(merged, count)
    else:
        pieces_2, pieces_3 = reduced_plainly(*grad_2), reduced_plainly(*grad_3)
    new_qkv, new_attn, column_one = step(
        [pieces_2, pieces_3],
        [
            [[(0, part * PAIR, PAIR), (1, part * HD, HD)] for part in range(3)],
            [[(0, 3 * PAIR, head_width)]],
        ],
        [(w_qkv, first_qkv, second_qkv), (w_attn_out, first_attn_out, second_attn_out)],
        (False, True),
        [(0, grad_2[0].shape[-1] - SPARE), (1, 3 * HD)],
    )
    sums = jnp.concatenate([column_one[:, :1], column_two[:, :1]], axis=1)
    shard_gain = (sums + core_swap(sums)).T / gains
    new_gain = adamw(gains, shard_gain, first_gains, second_gains, gain_rate, 0.0)
    return (
        output,
        grad_inputs,
        new_qkv[0],
        new_attn[0],
        new_in[0],
        new_down[0],
        shard_gain,
        new_qkv[1],
        new_attn[1],
        new_in[1],
        new_down[1],
        new_gain[0],
        new_qkv[2],
        new_attn[2],
        new_in[2],
        new_down[2],
        new_gain[1],
        new_qkv[3],
        new_attn[3],
        new_in[3],
        new_down[3],
        new_gain[2],
    )


def solution(mesh):
    return jax.shard_map(
        shards,
        mesh=mesh,
        in_specs=(
            P(("dp", "tensor"), None),
            P(("dp", "tensor"), None),
            P(None, "dp", "tensor"),
            P("tensor", "dp"),
            P(None, "dp", "tensor"),
            P("tensor", "dp"),
            P(None, "dp"),
            P(None, "dp", "tensor"),
            P("tensor", "dp"),
            P(None, "dp", "tensor"),
            P("tensor", "dp"),
            P(None, "dp"),
            P(None, "dp", "tensor"),
            P("tensor", "dp"),
            P(None, "dp", "tensor"),
            P("tensor", "dp"),
            P(None, "dp"),
        ),
        out_specs=(
            P(("dp", "tensor"), None),
            P(("dp", "tensor"), None),
            P(None, "dp", "tensor"),
            P("tensor", "dp"),
            P(None, "dp", "tensor"),
            P("tensor", "dp"),
            P(None, "dp"),
            P(None, "dp", "tensor"),
            P("tensor", "dp"),
            P(None, "dp", "tensor"),
            P("tensor", "dp"),
            P(None, "dp"),
            P(None, "dp", "tensor"),
            P("tensor", "dp"),
            P(None, "dp", "tensor"),
            P("tensor", "dp"),
            P(None, "dp"),
            P(None, "dp", "tensor"),
            P("tensor", "dp"),
            P(None, "dp", "tensor"),
            P("tensor", "dp"),
            P(None, "dp"),
        ),
        check_vma=False,
    )
```

```python
import functools

import jax
import jax.numpy as jnp
import numpy as np
from jax import lax
from jax.experimental import pallas as pl
from jax.experimental.pallas import tpu as pltpu
from jax.sharding import PartitionSpec as P

HD = 64
L = 1024
STEP = 10


eps_norm = 1e-05
rope_base = 160000.0
beta_one = 0.9
beta_two = 0.98
adam_eps = 1e-06
weight_rate = 0.02
gain_rate = 0.2
weight_decay = 0.01

low = jnp.bfloat16
full = jnp.float32
ROWS = 512
CHUNK = 256
PAIR = 2 * HD
VMEM_BYTES = 28 << 20
SPARE = 64
PACE = 800_000_000


def pace(microseconds):
    return pl.CostEstimate(flops=int(microseconds * PACE), bytes_accessed=0, transcendentals=0)


def dot(left, right, left_dim, right_dim):
    return lax.dot_general(
        left, right, (((left_dim,), (right_dim,)), ((), ())), preferred_element_type=full
    )


def params():
    return pltpu.CompilerParams(vmem_limit_bytes=VMEM_BYTES)


def whole(shape):
    return pl.BlockSpec(shape, lambda *_: (0,) * len(shape))


def rows_of(width, index=lambda i: i):
    return pl.BlockSpec((ROWS, width), lambda i: (index(i), 0))


def own_half(i):
    return jnp.minimum(i, L // ROWS // 2 - 1)


def other_half(i):
    return jnp.maximum(i - L // ROWS // 2, 0)


def swapped(i):
    return (i + L // ROWS // 2) % (L // ROWS)


def is_own(i):
    return i < L // ROWS // 2


def core_swap(array):
    return lax.ppermute(array, "tensor", [(t, t ^ 1) for t in range(4)])


def y_swap(array):
    return lax.ppermute(array, "tensor", [(t, t ^ 2) for t in range(4)])


def x_swap(array, count):
    return lax.ppermute(array, "dp", [(d, d ^ 1) for d in range(count)])


def z_shift(array, count, step):
    around = count // 2
    return lax.ppermute(
        array, "dp", [(d, (d // 2 + step) % around * 2 + d % 2) for d in range(count)]
    )


def staged(count):
    return count == 8


def after(array, *others):
    return lax.optimization_barrier((array, *others))[0]


ANY = pl.BlockSpec(memory_space=pl.ANY)
LOCAL = pl.BlockSpec(memory_space=pltpu.VMEM)
SCALAR = pl.BlockSpec(memory_space=pltpu.SMEM)


TIMES = {"weight_grad": 6, "assemble": 3, "step": 2, "pack": 1, "pack_rest": 1, "add_first": 2, "add_second": 1}


def call(kernel, name, ins, shapes, later=(), place=None, scratch=()):
    head = [] if place is None else [place]
    lead, skip = len(head), len(later)

    def body(*refs):
        kernel(*refs[: lead + len(ins)], *refs[lead + len(ins) + skip :])

    return pl.pallas_call(
        body,
        in_specs=[SCALAR] * lead + [LOCAL] * len(ins) + [ANY] * skip,
        out_specs=[LOCAL] * len(shapes),
        out_shape=shapes,
        scratch_shapes=list(scratch),
        compiler_params=params(),
        cost_estimate=pace(TIMES[name]),
        name=name,
    )(*head, *ins, *later)


def like(shape, kind=low):
    return jax.ShapeDtypeStruct(shape, kind)


def pack_kernel(w_qkv, gains, shard, padded):
    rows = w_qkv.shape[1]
    padded[...] = jnp.zeros_like(padded)
    padded[0 : gains.shape[0], 0:rows] = gains[...]
    columns = padded[...].T[0:rows, 0:2]
    high = columns.astype(low)
    rest = columns - high.astype(full)
    middle = rest.astype(low)
    last = (rest - middle.astype(full)).astype(low)
    filler = jnp.zeros((rows, SPARE - 6), full)
    pieces = [w_qkv[part] for part in range(3)]
    shard[...] = jnp.concatenate(
        pieces + [high.astype(full), middle.astype(full), last.astype(full), filler], axis=1
    ).astype(low)


def pack(w_qkv, gains):
    rows, width = w_qkv.shape[1:]
    return call(
        pack_kernel,
        "pack",
        [w_qkv, gains],
        [like((rows, 3 * width + SPARE))],
        scratch=[pltpu.VMEM((128, 128), full)],
    )[0]


def pack_rest_kernel(w_attn_out, w_in, w_mlp_out, shard, wide):
    rows = w_in.shape[1]
    flipped = []
    for weight in (w_attn_out, w_mlp_out):
        wide[...] = jnp.zeros_like(wide)
        wide[0 : weight.shape[0], 0:rows] = weight[...]
        flipped.append(wide[...].T[0:rows, 0 : weight.shape[0]])
    pieces = [flipped[0], w_in[0], w_in[1], flipped[1]]
    shard[...] = jnp.concatenate(pieces, axis=1).astype(low)


def pack_rest(w_attn_out, w_in, w_mlp_out, later):
    rows, units = w_in.shape[1:]
    heads = w_attn_out.shape[0]
    return call(
        pack_rest_kernel,
        "pack_rest",
        [w_attn_out, w_in, w_mlp_out],
        [like((rows, heads + 3 * units))],
        later=later,
        scratch=[pltpu.VMEM((-(-units // 128) * 128, 128), full)],
    )[0]


def unpack_gains(columns):
    wide = jnp.concatenate([columns.astype(full), jnp.zeros(columns.shape, full)], axis=1).T
    return wide[0:2] + wide[2:4] + wide[4:6]


def columns_of(layout, own, other):
    pieces = []
    for item in layout:
        if item is None:
            pieces.append(jnp.zeros((own.shape[0], SPARE), own.dtype))
        else:
            side, start, width = item
            pieces.append((own, other)[side][:, start : start + width])
    return jnp.concatenate(pieces, axis=1)


def layout_width(layout):
    return sum(SPARE if item is None else item[2] for item in layout)


def head_layout(start, width):
    first = width // 3 * 2
    return [(0, start, width), (1, start + first, width - first), (1, start, first)]


def unit_layout(start, width):
    return [(0, start, width), (1, start, width), None]


def assemble_kernel(layouts, flips, gains_at, place_ref, za, xa, ya, zb, yb, xb, *outs):
    place = place_ref[0]
    half = za.shape[1]
    for jx in range(2):
        for jz in range(4):
            source = (place // 2 + 4 - jz) % 4 * 2 + (place % 2 + jx) % 2
            own_a = (za, xa)[jx][jz]
            other_a = ya[jx, jz]
            own_b = zb[jz] if jx == 0 else xb[0, jz]
            other_b = yb[jz] if jx == 0 else xb[1, jz]
            for part, (own, other) in enumerate(((own_a, other_a), (own_b, other_b))):
                start = pl.multiple_of(source * 2 * half + part * half, half)
                for layout, out in zip(layouts, outs):
                    out[pl.ds(start, half), :] = columns_of(layout, own, other)
                if gains_at is not None:
                    outs[-1][pl.ds(start, half), :] = own[:, gains_at : gains_at + SPARE]
    for at, flip in enumerate(flips):
        outs[len(layouts) + at][...] = outs[flip][...].T
    if gains_at is not None:
        outs[-2][...] = unpack_gains(outs[-1][...])


def assemble(pieces, layouts, depth, flips=(), gains_at=None, later=()):
    place = lax.axis_index("dp").astype(jnp.int32)[None]
    shapes = [like((depth, layout_width(layout))) for layout in layouts]
    shapes += [like((layout_width(layouts[flip]), depth)) for flip in flips]
    scratch = []
    if gains_at is not None:
        shapes.append(like((2, depth), full))
        scratch.append(pltpu.VMEM((depth, SPARE), low))
    return call(
        functools.partial(assemble_kernel, layouts, flips, gains_at),
        "assemble",
        pieces,
        shapes,
        later=later,
        place=place,
        scratch=scratch,
    )


def gathered_plainly(shard, layouts, flips=(), gains_at=None):
    own = lax.all_gather(shard, "dp", axis=0, tiled=True)
    other = y_swap(own)
    results = [columns_of(layout, own, other) for layout in layouts]
    results += [results[flip].T for flip in flips]
    if gains_at is not None:
        results.append(unpack_gains(own[:, gains_at : gains_at + SPARE]))
    return results


def stacked(ins, at, axis):
    parts = [ins[index][...] for index in at]
    return parts[0] if len(parts) == 1 else jnp.concatenate(parts, axis=axis)


def weight_grad_kernel(products, fast, weights, ins, place_ref, refs):
    outs, scratch = (refs[:4], refs[4:]) if fast else (refs[:2], refs[2:])
    place = place_ref[0]
    for index, (held, (left, right, _)) in enumerate(zip(scratch, products)):
        grad = dot(stacked(ins, left, 0), stacked(ins, right, 1), 0, 0)
        held[...] = grad
        if weights and index == 0:
            weight = [ins[-1][:, start : start + width] for start, width in weights]
            weight = weight[0] if len(weight) == 1 else jnp.concatenate(weight, axis=1)
            sums = jnp.sum(weight.astype(full) * grad, axis=1, keepdims=True)
            scratch[-1][...] = jnp.broadcast_to(sums, (sums.shape[0], 128))

    def split(rows):
        sides = [[], []]
        for held, (_, _, spans) in zip(scratch, products):
            values = held[rows, :]
            for *starts, width in spans:
                for side, start in zip(sides, starts):
                    side.append(values[:, start : start + width])
        if weights:
            for side in sides:
                side.append(scratch[-1][rows, :][:, :SPARE])
        return [jnp.concatenate(side, axis=1).astype(low) for side in sides]

    if not fast:
        outs[0][...], outs[1][...] = split(slice(None))
        return
    size = outs[0].shape[2]
    for jx in range(2):
        for jz in range(4):
            target = (place // 2 + jz) % 4 * 2 + (place % 2 + jx) % 2
            for part in range(2):
                start = pl.multiple_of((target * 2 + part) * size, size)
                own, other = split(pl.ds(start, size))
                if part == 0:
                    outs[0][jx, jz] = own
                    outs[1][jx, jz] = other
                else:
                    outs[2 + jx][0, jz] = own
                    outs[2 + jx][1, jz] = other


def weight_grad(arrays, products, count, weight=None, lanes=(), later=()):
    depth = arrays[products[0][0][0]].shape[1]
    widths = [sum(arrays[at].shape[1] for at in right) for _, right, _ in products]
    total = sum(span[2] for _, _, spans in products for span in spans)
    total += SPARE if weight is not None else 0
    fast = staged(count)
    if fast:
        shapes = [like((2, 4, depth // count // 2, total))] * 4
    else:
        shapes = [like((depth, total))] * 2
    place = lax.axis_index("dp").astype(jnp.int32)[None]
    ins = list(arrays) + ([] if weight is None else [weight])
    weights = [] if weight is None else list(lanes)
    held = [pltpu.VMEM((depth, width), full) for width in widths]
    if weights:
        held.append(pltpu.VMEM((depth, 128), full))

    def kernel(place_ref, *refs):
        weight_grad_kernel(
            products, fast, weights, refs[: len(ins)], place_ref, refs[len(ins) :]
        )

    return call(
        kernel,
        "weight_grad",
        ins,
        shapes,
        later=later,
        place=place,
        scratch=held,
    )


def reduced_plainly(own, other):
    summed = own.astype(full) + y_swap(other).astype(full)
    return [lax.psum_scatter(summed, "dp", scatter_dimension=0, tiled=True)]


def add_kernel(groups, *refs):
    ins, outs = refs[: 4 * groups], refs[4 * groups :]
    for half in range(2):
        for side in range(2):
            sums = []
            for group in range(groups):
                here, there = ins[4 * group + 2 * half : 4 * group + 2 * half + 2]
                sums.append((here[side].astype(full) + there[side].astype(full)).astype(low))
            out = outs[2 * half + side]
            out[...] = sums[0] if groups == 1 else jnp.concatenate(sums, axis=-1)


def add_first(groups, later=()):
    rows = groups[0][0].shape[2]
    width = sum(group[0].shape[3] for group in groups)
    return call(
        functools.partial(add_kernel, len(groups)),
        "add_first",
        [array for group in groups for array in group],
        [like((4, rows, width))] * 4,
        later=later,
    )


def merge_kernel(here_a, there_a, here_b, there_b, *outs):
    for jump, out in enumerate(outs):
        part_a = here_a[jump].astype(full) + there_a[jump].astype(full)
        part_b = here_b[jump].astype(full) + there_b[jump].astype(full)
        out[...] = jnp.concatenate([part_a.astype(low), part_b.astype(low)], axis=0)


def add_second(here_a, there_a, here_b, there_b, later=()):
    _, rows, width = here_a.shape
    return call(
        merge_kernel,
        "add_second",
        [here_a, there_a, here_b, there_b],
        [like((2 * rows, width))] * 4,
        later=later,
    )


def across_z(parts, count):
    return [parts[0]] + [z_shift(parts[step], count, step) for step in (1, 2, 3)]


def normalized(values):
    centred = values - jnp.mean(values, axis=-1, keepdims=True)
    spread = jnp.mean(centred * centred, axis=-1, keepdims=True)
    scale = lax.rsqrt(spread + eps_norm)
    return centred * scale, scale


def norm_back(unit, scale, gains, grads):
    inner = grads * gains
    mean_inner = jnp.mean(inner, axis=-1, keepdims=True)
    mean_unit = jnp.mean(inner * unit, axis=-1, keepdims=True)
    return scale * (inner - mean_inner - unit * mean_unit)


def rope_tables(offset):
    half_width = HD // 2
    frequency = rope_base ** (-(jnp.arange(half_width, dtype=full) * 2.0 / HD))
    position = ((jnp.arange(L) + offset) % L).astype(full)
    angles = position[:, None] * frequency[None, :]
    cosine, sine = jnp.cos(angles), jnp.sin(angles)
    return (
        jnp.concatenate([cosine] * 4, axis=1),
        jnp.concatenate([-sine, sine, -sine, sine], axis=1),
    )


def turn(values, cosine, sine):
    lane = lax.broadcasted_iota(jnp.int32, values.shape, 1)
    ahead = pltpu.roll(values, PAIR - HD // 2, 1)
    behind = pltpu.roll(values, HD // 2, 1)
    turned = jnp.where(lane % HD < HD // 2, ahead, behind)
    return values * cosine + turned * sine


def qkv_kernel(x_own, x_other, gain, weight, cosine, sine, normed, q_out, k_out, v_out, raw):
    own = is_own(pl.program_id(0))
    unit, _ = normalized(jnp.where(own, x_own[...], x_other[...]).astype(full))
    rows = (unit * gain[...]).astype(low)
    normed[...] = rows
    raw[...] = dot(rows, weight[...], 1, 0)
    width = q_out.shape[1]
    near, far = cosine[...], sine[...]
    for start in range(0, width, PAIR):
        lanes = slice(start, start + PAIR)
        query = turn(raw[:, lanes], near, far).astype(low)
        q_out[:, lanes] = query * jnp.asarray(HD ** (-0.5), low)
        key = raw[:, width + start : width + start + PAIR]
        k_out[:, lanes] = turn(key, near, far).astype(low)
    v_out[...] = raw[:, 2 * width :].astype(low)


def project(x_own, x_other, gain, weight, cosine, sine):
    depth, total = weight.shape
    width = total // 3
    return pl.pallas_call(
        qkv_kernel,
        grid=(L // ROWS,),
        in_specs=[
            rows_of(depth, own_half),
            rows_of(depth, other_half),
            whole((1, depth)),
            whole((depth, total)),
            rows_of(PAIR),
            rows_of(PAIR),
        ],
        out_specs=[rows_of(depth), rows_of(width), rows_of(width), rows_of(width)],
        out_shape=[like((L, depth))] + [like((L, width))] * 3,
        scratch_shapes=[pltpu.VMEM((ROWS, total), full)],
        compiler_params=params(),
        cost_estimate=pace(6),
        name="project",
    )(x_own, x_other, gain, weight, cosine, sine)


def head_masks(height):
    lane = lax.broadcasted_iota(jnp.int32, (height, PAIR), 1)
    return [(lane // HD == head).astype(full).astype(low) for head in range(2)]


def flat_heads(rows):
    flat = rows.astype(full).T
    head_of = lax.broadcasted_iota(jnp.int32, flat.shape, 0) // HD
    return [jnp.where(head_of == head, flat, 0.0).astype(low) for head in range(2)]


def attend_kernel(q_ref, k_ref, v_ref, mixed, lse_ref):
    flat_keys, values = flat_heads(k_ref[...]), v_ref[...]
    lane = lax.broadcasted_iota(jnp.int32, (CHUNK, PAIR), 1)
    for start in range(0, L, CHUNK):
        rows = slice(start, start + CHUNK)
        query = q_ref[rows, :]
        results = []
        for head in range(2):
            scores = dot(query, flat_keys[head], 1, 0)
            row_max = jnp.max(scores, axis=1, keepdims=True)
            raised = jnp.exp(scores - row_max)
            total = jnp.sum(raised, axis=1, keepdims=True)
            results.append(dot(raised.astype(low), values, 1, 0) / total)
            lse = jnp.broadcast_to(row_max + jnp.log(total), (CHUNK, PAIR))
            lse_ref[0, head : head + 1, rows] = lse.T[0:1]
        mixed[rows, :] = jnp.where(lane < HD, results[0], results[1]).astype(low)


def attend(query, key, value):
    width = query.shape[1]
    pairs = width // PAIR
    block = pl.BlockSpec((L, PAIR), lambda i: (0, i))
    totals = pl.BlockSpec((1, 2, L), lambda i: (i, 0, 0))
    return pl.pallas_call(
        attend_kernel,
        grid=(pairs,),
        in_specs=[block] * 3,
        out_specs=[block, totals],
        out_shape=[
            jax.ShapeDtypeStruct((L, width), low),
            jax.ShapeDtypeStruct((pairs, 2, L), full),
        ],
        compiler_params=params(),
        cost_estimate=pace(13),
        name="attend",
    )(query, key, value)


def attend_back_kernel(
    q_ref, k_ref, v_ref, o_ref, grad_ref, lse_ref, cosine, sine, dq_out, dk_out, dv_out, dk, dv
):
    masks = head_masks(L)
    chunk_masks = head_masks(CHUNK)
    keys, values = k_ref[...], v_ref[...]
    head_keys = [keys * mask for mask in masks]
    head_values = [values * mask for mask in masks]
    flipped_keys = flat_heads(keys)
    flat_query = q_ref[...].astype(full).T.astype(low)
    flat_grad = grad_ref[...].astype(full).T.astype(low)
    product = (grad_ref[...].astype(full) * o_ref[...].astype(full)).T
    inner = [jnp.sum(product[head * HD : (head + 1) * HD], axis=0, keepdims=True) for head in range(2)]
    for start in range(0, L, CHUNK):
        rows = slice(start, start + CHUNK)
        query, grad = q_ref[rows, :], grad_ref[rows, :]
        dq = None
        for head in range(2):
            scores = dot(head_keys[head], flat_query[:, rows], 1, 0)
            probs = jnp.exp(scores - lse_ref[0, head : head + 1, rows])
            grad_probs = dot(head_values[head], flat_grad[:, rows], 1, 0)
            grad_scores = (probs * (grad_probs - inner[head][:, rows])).astype(low)
            add_v = dot(probs.astype(low), grad * chunk_masks[head], 1, 0)
            add_k = dot(grad_scores, query * chunk_masks[head], 1, 0)
            add_q = dot(flipped_keys[head], grad_scores, 1, 0)
            dq = add_q if dq is None else dq + add_q
            if start == 0 and head == 0:
                dv[...] = add_v
                dk[...] = add_k
            else:
                dv[...] += add_v
                dk[...] += add_k
        dq_out[rows, :] = turn(dq.T * HD ** (-0.5), cosine[rows, :], -sine[rows, :]).astype(low)
    dk_out[...] = turn(dk[...], cosine[...], -sine[...]).astype(low)
    dv_out[...] = dv[...].astype(low)


def attend_back(pair, query, key, value, mixed, grad, lse, cosine, sine, later=()):
    block = pl.BlockSpec((L, PAIR), lambda i: (0, pair))
    result = pl.BlockSpec((L, PAIR), lambda i: (0, 0))
    totals = pl.BlockSpec((1, 2, L), lambda i: (pair, 0, 0))
    skip = len(later)

    def body(*refs):
        attend_back_kernel(*refs[:8], *refs[8 + skip :])

    return pl.pallas_call(
        body,
        grid=(1,),
        in_specs=[block] * 5 + [totals] + [whole((L, PAIR))] * 2 + [ANY] * skip,
        out_specs=[result] * 3,
        out_shape=[like((L, PAIR))] * 3,
        scratch_shapes=[pltpu.VMEM((L, PAIR), full)] * 2,
        compiler_params=params(),
        cost_estimate=pace(7),
        name="attend_back",
    )(query, key, value, mixed, grad, lse, cosine, sine, *later)


def feed_forward_kernel(
    mixed_own,
    mixed_other,
    x_own,
    x_other,
    dy_own,
    dy_other,
    gain,
    wo_own,
    wo_other,
    w_both,
    w_both_flat,
    w_down,
    w_down_flat,
    normed,
    scale_out,
    hidden_out,
    dboth_out,
    out_own,
    out_other,
    dnormed,
):
    own = is_own(pl.program_id(0))
    units = w_down.shape[0]
    tokens = jnp.where(own, x_own[...], x_other[...]).astype(full)
    resid = (
        tokens + dot(mixed_own[...], wo_own[...], 1, 0) + dot(mixed_other[...], wo_other[...], 1, 0)
    )
    unit, scale = normalized(resid)
    rows = (unit * gain[...]).astype(low)
    normed[...] = rows
    scale_out[...] = jnp.broadcast_to(scale, scale_out.shape)
    both = dot(rows, w_both[...], 1, 0)
    gate, up = both[:, :units], both[:, units:]
    cumulative = 0.5 + 0.5 * lax.erf(gate * np.float32(0.5**0.5))
    density = jnp.exp(gate * gate * -0.5) * np.float32((2.0 * np.pi) ** -0.5)
    activated = gate * cumulative
    hidden = (activated * up).astype(low)
    hidden_out[...] = hidden
    part = dot(hidden, w_down[...], 1, 0)
    dhidden = dot(jnp.where(own, dy_own[...], dy_other[...]), w_down_flat[...], 1, 0)
    dgate = (dhidden * up * (cumulative + gate * density)).astype(low)
    dup = (dhidden * activated).astype(low)
    dboth = jnp.concatenate([dgate, dup], axis=1)
    dboth_out[...] = dboth
    dnormed[...] = dot(dboth, w_both_flat[...], 1, 0).astype(low)

    @pl.when(own)
    def _():
        out_own[...] = resid + part

    @pl.when(jnp.logical_not(own))
    def _():
        out_other[...] = part.astype(low)


def feed_forward(*arrays):
    width, depth = arrays[7].shape
    units = arrays[11].shape[0]
    half = L // 2
    return pl.pallas_call(
        feed_forward_kernel,
        grid=(L // ROWS,),
        in_specs=[
            rows_of(width),
            rows_of(width, swapped),
            rows_of(depth, own_half),
            rows_of(depth, other_half),
            rows_of(depth, own_half),
            rows_of(depth, other_half),
            whole((1, depth)),
            whole((width, depth)),
            whole((width, depth)),
            whole((depth, 2 * units)),
            whole((2 * units, depth)),
            whole((units, depth)),
            whole((depth, units)),
        ],
        out_specs=[
            rows_of(depth),
            rows_of(128),
            rows_of(units),
            rows_of(2 * units),
            rows_of(depth, own_half),
            rows_of(depth, other_half),
            rows_of(depth),
        ],
        out_shape=[
            like((L, depth)),
            like((L, 128), full),
            like((L, units)),
            like((L, 2 * units)),
            like((half, depth), full),
            like((half, depth)),
            like((L, depth)),
        ],
        compiler_params=params(),
        cost_estimate=pace(18),
        name="feed_forward",
    )(*arrays)


def resid_back_kernel(
    normed, scale_ref, grad_own, grad_other, dy_own, dy_other, gain, wo, dresid, dresid_low, dmixed
):
    own = is_own(pl.program_id(0))
    inverse = 1.0 / gain[...]
    pull = jnp.where(own, dy_own[...], dy_other[...]).astype(full)
    grads = grad_own[...].astype(full) + grad_other[...].astype(full)
    unit = normed[...].astype(full) * inverse
    total = pull + norm_back(unit, scale_ref[:, 0:1], gain[...], grads)
    rounded = total.astype(low)
    dresid_low[...] = rounded
    dmixed[...] = dot(rounded, wo[...], 1, 0).astype(low)

    @pl.when(own)
    def _():
        dresid[...] = total


def resid_back(normed, scale, grad_own, grad_other, dy_own, dy_other, gain, wo, later=()):
    depth, width = wo.shape
    skip = len(later)

    def body(*refs):
        resid_back_kernel(*refs[:8], *refs[8 + skip :])

    return pl.pallas_call(
        body,
        grid=(L // ROWS,),
        in_specs=[
            rows_of(depth),
            rows_of(128),
            rows_of(depth),
            rows_of(depth, swapped),
            rows_of(depth, own_half),
            rows_of(depth, other_half),
            whole((1, depth)),
            whole((depth, width)),
        ]
        + [ANY] * skip,
        out_specs=[rows_of(depth, own_half), rows_of(depth), rows_of(width)],
        out_shape=[like((L // 2, depth), full), like((L, depth)), like((L, width))],
        compiler_params=params(),
        cost_estimate=pace(7),
        name="resid_back",
    )(normed, scale, grad_own, grad_other, dy_own, dy_other, gain, wo, *later)


def project_back_kernel(*refs):
    grads, weight, (grad_own, grad_other, flat) = refs[:9], refs[9], refs[10:13]

    @pl.when(pl.program_id(0) == 0)
    def _():
        flat[...] = weight[...].T

    rows = jnp.concatenate([ref[...] for ref in grads], axis=1)
    grad = dot(rows, flat[...], 1, 0)
    own = is_own(pl.program_id(0))

    @pl.when(own)
    def _():
        grad_own[...] = grad

    @pl.when(jnp.logical_not(own))
    def _():
        grad_other[...] = grad.astype(low)


def project_back(grads, weight, later=()):
    depth, total = weight.shape
    skip = len(later)

    def body(*refs):
        project_back_kernel(*refs[:10], *refs[10 + skip :])

    return pl.pallas_call(
        body,
        grid=(L // ROWS,),
        in_specs=[rows_of(PAIR)] * 9 + [whole((depth, total))] + [ANY] * skip,
        out_specs=[rows_of(depth, own_half), rows_of(depth, other_half)],
        out_shape=[like((L // 2, depth), full), like((L // 2, depth))],
        scratch_shapes=[pltpu.VMEM((total, depth), low)],
        compiler_params=params(),
        cost_estimate=pace(6),
        name="project_back",
    )(*grads, weight, *later)


def input_back_kernel(tokens, grad_own, grad_other, dresid, gain, result):
    grads = grad_own[...] + grad_other[...].astype(full)
    unit, scale = normalized(tokens[...].astype(full))
    result[...] = dresid[...] + norm_back(unit, scale, gain[...], grads)


def input_back(tokens, grad_own, grad_other, dresid, gain):
    height, depth = tokens.shape
    return pl.pallas_call(
        input_back_kernel,
        grid=(height // ROWS,),
        in_specs=[rows_of(depth)] * 4 + [whole((1, depth))],
        out_specs=rows_of(depth),
        out_shape=like((height, depth), full),
        compiler_params=params(),
        cost_estimate=pace(3),
        name="input_back",
    )(tokens, grad_own, grad_other, dresid, gain)


def adamw(weight, grad, first, second, rate, decay):
    first_new = beta_one * first + (1.0 - beta_one) * grad
    second_new = beta_two * second + (1.0 - beta_two) * grad * grad
    step_size = (
        first_new
        / (1.0 - beta_one**STEP)
        / (jnp.sqrt(second_new / (1.0 - beta_two**STEP)) + adam_eps)
    )
    return (weight - rate * (step_size + decay * weight), first_new, second_new)


def step_kernel(counts, flipped, spans, column_at, *refs):
    totals, used = [], 0
    for count in counts:
        total = refs[used][...].astype(full)
        for piece in refs[used + 1 : used + count]:
            total = total + piece[...].astype(full)
        totals.append(total)
        used += count
    rest, count = refs[used:], len(spans)
    states, outs = rest[: 3 * count], rest[3 * count : 7 * count]
    scratch = rest[7 * count + 1 :]
    rows = totals[0].shape[0]
    column = None
    for group, start in column_at:
        term = totals[group][:, start : start + SPARE]
        column = term if column is None else column + term
    rest[7 * count][...] = column
    for at, span in enumerate(spans):
        weight, first, second = states[3 * at : 3 * at + 3]
        grad_out, weight_out, first_out, second_out = outs[4 * at : 4 * at + 4]
        for part, slices in enumerate(span):
            pieces = [totals[group][:, start : start + size] for group, start, size in slices]
            grad = pieces[0] if len(pieces) == 1 else jnp.concatenate(pieces, axis=1)
            width = grad.shape[1]
            if flipped[at]:
                padded = scratch[at]
                padded[...] = jnp.zeros_like(padded)
                padded[0:rows, 0:width] = grad
                grad = padded[...].T[0:width, 0:rows]
                where = Ellipsis
            else:
                where = part
            new = adamw(
                weight[where], grad, first[where], second[where], weight_rate, weight_decay
            )
            grad_out[where] = grad
            weight_out[where], first_out[where], second_out[where] = new


def step(groups, spans, states, flipped, column_at, later=()):
    shapes, scratch = [], []
    for (weight, _, _), span, flip in zip(states, spans, flipped):
        shapes += [like(weight.shape, full)] * 4
        lanes = -(-sum(size for _, _, size in span[0]) // 128) * 128
        scratch.append(pltpu.VMEM((128, lanes) if flip else (8, 128), full))
    shapes.append(like((groups[0][0].shape[0], SPARE), full))
    flat = [array for state in states for array in state]
    results = call(
        functools.partial(step_kernel, [len(group) for group in groups], flipped, spans, column_at),
        "step",
        [piece for group in groups for piece in group] + flat,
        shapes,
        later=later,
        scratch=scratch,
    )
    return [results[4 * at : 4 * at + 4] for at in range(len(states))] + [results[-1]]


def shards(
    tokens,
    cotangent,
    w_qkv,
    w_attn_out,
    w_in,
    w_mlp_out,
    gains,
    first_qkv,
    first_attn_out,
    first_in,
    first_mlp_out,
    first_gains,
    second_qkv,
    second_attn_out,
    second_in,
    second_mlp_out,
    second_gains,
):
    count = lax.axis_size("dp")
    fast = staged(count)
    core = lax.axis_index("tensor") % 2
    head_width = w_qkv.shape[2]
    unit_width = w_in.shape[2]
    depth = tokens.shape[1]
    qkv_layouts = [sum((head_layout(part * head_width, head_width) for part in range(3)), [])]
    gains_at = 3 * head_width
    gate_at, up_at, down_at = (head_width + part * unit_width for part in range(3))
    rest_layouts = [
        head_layout(0, head_width),
        unit_layout(gate_at, unit_width) + unit_layout(up_at, unit_width),
        unit_layout(down_at, unit_width),
    ]

    shard_one = pack(w_qkv, gains)
    shard_two = pack_rest(w_attn_out, w_in, w_mlp_out, [shard_one])
    cosine, sine = rope_tables(core * (L // 2))

    def halves(shard, along):
        half = shard.shape[0] // 2
        pieces = [shard] + along
        return jnp.stack([p[:half] for p in pieces]), jnp.stack([p[half:] for p in pieces])

    if fast:
        along_one = [z_shift(shard_one, count, jump) for jump in (1, 2, 3)]
        x_other = core_swap(tokens)
        za, zb = halves(after(shard_one, shard_two, x_other, cosine, sine), along_one)
        shard_two = after(shard_two, *along_one)
        along_two = [z_shift(shard_two, count, jump) for jump in (1, 2, 3)]
        xa, yb = x_swap(za, count), y_swap(zb)
        both_a, both_b = jnp.stack([za, xa]), jnp.stack([zb, yb])
        ya, xb = y_swap(both_a), x_swap(both_b, count)
        first_pieces = [za, xa, ya, zb, yb, xb]
        za, zb = halves(shard_two, [after(piece, both_a, both_b) for piece in along_two])
        w_qkv_all, gains_all = assemble(
            first_pieces, qkv_layouts, depth, (), gains_at, later=[za, zb]
        )
    else:
        x_other = core_swap(tokens)
        w_qkv_all, gains_all = gathered_plainly(shard_one, qkv_layouts, (), gains_at)
    gain_one, gain_two = gains_all[0:1], gains_all[1:2]
    if fast:
        xa, yb = x_swap(za, count), y_swap(zb)
    normed_one, query, key, value = project(tokens, x_other, gain_one, w_qkv_all, cosine, sine)
    if fast:
        xa, yb = after(xa, query), after(yb, query)
        ya, xb = y_swap(jnp.stack([za, xa])), x_swap(jnp.stack([zb, yb]), count)
    dy_other = core_swap(after(cotangent, query))
    mixed, lse = attend(query, key, value)
    mixed_other = core_swap(mixed)
    if fast:
        ya, xb = after(ya, mixed), after(xb, mixed)
        rest = assemble([za, xa, ya, zb, yb, xb], rest_layouts, depth, (0, 1, 2))
    else:
        rest = gathered_plainly(shard_two, rest_layouts, (0, 1, 2))
    wo_flat, w_both, w_down_flat, wo, w_both_flat, w_down = rest
    wo_other = core_swap(wo)
    normed_two, scale_two, hidden, dboth, out_own, out_other, dnormed = feed_forward(
        mixed,
        mixed_other,
        tokens,
        x_other,
        cotangent,
        dy_other,
        gain_two,
        wo,
        wo_other,
        w_both,
        w_both_flat,
        w_down,
        w_down_flat,
    )
    units = w_down.shape[0]
    dnormed_other = core_swap(dnormed)
    grad_1 = weight_grad(
        [normed_two, dboth, cotangent, dy_other, hidden],
        [
            ((0,), (1,), [(0, unit_width, unit_width), (units, units + unit_width, unit_width)]),
            ((2, 3), (4,), [(0, unit_width, unit_width)]),
        ],
        count,
        w_both,
        [(0, 2 * units)],
    )
    if fast:
        from_y, from_x = y_swap(grad_1[1]), x_swap(grad_1[3], count)
    output = (out_own + core_swap(out_other).astype(full)).astype(low)
    dresid, dresid_low, dmixed = resid_back(
        normed_two,
        scale_two,
        dnormed,
        dnormed_other,
        cotangent,
        dy_other,
        gain_two,
        wo_flat,
        later=grad_1[:1],
    )
    bundle = (query, key, value, mixed, dmixed, lse, cosine, sine)
    pair_0 = attend_back(0, *bundle, later=[output])
    pair_1 = attend_back(1, *bundle, later=pair_0[:1])
    pair_2 = attend_back(2, *bundle, later=pair_1[:1])
    if fast:
        sums_1 = add_first([(grad_1[0], from_y, grad_1[2], from_x)], later=pair_2[:1])
        next_a, next_b = x_swap(sums_1[1], count), y_swap(sums_1[3])
    trios = [group[part] for part in range(3) for group in (pair_0, pair_1, pair_2)]
    spans = [(0, 2 * PAIR, PAIR), (PAIR, PAIR + HD, HD)]
    grad_2 = weight_grad(
        [normed_one, *trios, dresid_low, mixed],
        [
            (
                (0,),
                tuple(range(1, 10)),
                [(part + own, part + other, size) for part in (0, 3 * PAIR, 6 * PAIR) for own, other, size in spans],
            ),
            ((10,), (11,), spans),
        ],
        count,
        w_qkv_all,
        [(0, 9 * PAIR)],
        later=[sums_1[1], sums_1[3]] if fast else (),
    )
    if fast:
        from_y2, from_x2 = y_swap(grad_2[1]), x_swap(grad_2[3], count)
        merged = add_second(sums_1[0], next_a, sums_1[2], next_b, later=grad_2[:1])
        pieces_1 = across_z(merged, count)
    grad_one, grad_one_low = project_back(trios, w_qkv_all, later=merged[:1] if fast else ())
    if fast:
        from_y2, from_x2 = after(from_y2, grad_one), after(from_x2, grad_one)
        sums_2 = add_first([(grad_2[0], from_y2, grad_2[2], from_x2)], later=pieces_1)
        next_a, next_b = x_swap(sums_2[1], count), y_swap(sums_2[3])
        grad_one_low = after(grad_one_low, sums_2[1], sums_2[3])
    else:
        pieces_1 = reduced_plainly(*grad_1)
    grad_other = core_swap(grad_one_low)
    grad_inputs = input_back(tokens, grad_one, grad_other, dresid, gain_one)
    new_in, new_down, column_two = step(
        [pieces_1],
        [
            [[(0, 0, unit_width)], [(0, unit_width, unit_width)]],
            [[(0, 2 * unit_width, unit_width)]],
        ],
        [(w_in, first_in, second_in), (w_mlp_out, first_mlp_out, second_mlp_out)],
        (False, True),
        [(0, 3 * unit_width)],
        later=sums_2[:1] if fast else (),
    )
    if fast:
        merged = add_second(sums_2[0], next_a, sums_2[2], next_b, later=[column_two, grad_inputs])
        pieces_2 = across_z(merged, count)
    else:
        pieces_2 = reduced_plainly(*grad_2)
    new_qkv, new_attn, column_one = step(
        [pieces_2],
        [
            [[(0, part * head_width, head_width)] for part in range(3)],
            [[(0, 3 * head_width, head_width)]],
        ],
        [(w_qkv, first_qkv, second_qkv), (w_attn_out, first_attn_out, second_attn_out)],
        (False, True),
        [(0, 4 * head_width)],
    )
    sums = jnp.concatenate([column_one[:, :1], column_two[:, :1]], axis=1)
    shard_gain = (sums + core_swap(sums)).T / gains
    new_gain = adamw(gains, shard_gain, first_gains, second_gains, gain_rate, 0.0)
    return (
        output,
        grad_inputs,
        new_qkv[0],
        new_attn[0],
        new_in[0],
        new_down[0],
        shard_gain,
        new_qkv[1],
        new_attn[1],
        new_in[1],
        new_down[1],
        new_gain[0],
        new_qkv[2],
        new_attn[2],
        new_in[2],
        new_down[2],
        new_gain[1],
        new_qkv[3],
        new_attn[3],
        new_in[3],
        new_down[3],
        new_gain[2],
    )


def solution(mesh):
    return jax.shard_map(
        shards,
        mesh=mesh,
        in_specs=(
            P(("dp", "tensor"), None),
            P(("dp", "tensor"), None),
            P(None, "dp", "tensor"),
            P("tensor", "dp"),
            P(None, "dp", "tensor"),
            P("tensor", "dp"),
            P(None, "dp"),
            P(None, "dp", "tensor"),
            P("tensor", "dp"),
            P(None, "dp", "tensor"),
            P("tensor", "dp"),
            P(None, "dp"),
            P(None, "dp", "tensor"),
            P("tensor", "dp"),
            P(None, "dp", "tensor"),
            P("tensor", "dp"),
            P(None, "dp"),
        ),
        out_specs=(
            P(("dp", "tensor"), None),
            P(("dp", "tensor"), None),
            P(None, "dp", "tensor"),
            P("tensor", "dp"),
            P(None, "dp", "tensor"),
            P("tensor", "dp"),
            P(None, "dp"),
            P(None, "dp", "tensor"),
            P("tensor", "dp"),
            P(None, "dp", "tensor"),
            P("tensor", "dp"),
            P(None, "dp"),
            P(None, "dp", "tensor"),
            P("tensor", "dp"),
            P(None, "dp", "tensor"),
            P("tensor", "dp"),
            P(None, "dp"),
            P(None, "dp", "tensor"),
            P("tensor", "dp"),
            P(None, "dp", "tensor"),
            P("tensor", "dp"),
            P(None, "dp"),
        ),
        check_vma=False,
    )
```
